32 devices in a mesh: dp: 8 (over y, x, core), ctx: 4 (over z).
Axes of the slice: x: 2, y: 2, z: 4, core: 2. Of those that a mesh axis runs over, the one named last changes fastest.
Arguments:
- hidden_in: bfloat16 [8, 1536, 1024], P('dp', 'ctx'), may hold values from -6 to 6
- cotangent: bfloat16 [8, 1536, 1024], P('dp', 'ctx'), may hold values from -6 to 6
- context_len: int32 [8], P('dp'), may hold values from 576 to 1152, as said below
- block_device: int32 [8], P('dp'), may hold values from 0 to 3
- timestep: int32 [8], P('dp'), may hold values from 0 to 511, as said below
- query_weight: bfloat16 [1024, 1024], P('ctx'), may hold values from -0.1875 to 0.1875
- key_weight: bfloat16 [1024, 1024], P('ctx'), may hold values from -0.1875 to 0.1875
- value_weight: bfloat16 [1024, 1024], P('ctx'), may hold values from -0.1875 to 0.1875
- output_weight: bfloat16 [1024, 1024], P('ctx'), may hold values from -1.5 to 1.5
- inner_weight: bfloat16 [1024, 4096], P('ctx'), may hold values from -0.1875 to 0.1875
- outer_weight: bfloat16 [4096, 1024], P('ctx'), may hold values from -0.09375 to 0.09375
- query_bias: bfloat16 [1024], replicated, may hold values from -1.5 to 1.5
- value_bias: bfloat16 [1024], replicated, may hold values from -1.5 to 1.5
- output_bias: bfloat16 [1024], replicated, may hold values from -1.5 to 1.5
- inner_bias: bfloat16 [4096], replicated, may hold values from -1.5 to 1.5
- outer_bias: bfloat16 [1024], replicated, may hold values from -1.5 to 1.5
- attn_gain: bfloat16 [1024], replicated, may hold values from 0.5 to 1.5
- attn_shift: bfloat16 [1024], replicated, may hold values from -1.5 to 1.5
- ffn_gain: bfloat16 [1024], replicated, may hold values from 0.5 to 1.5
- ffn_shift: bfloat16 [1024], replicated, may hold values from -1.5 to 1.5
- time_table: bfloat16 [512, 1024], replicated, may hold values from -3 to 3
Outputs:
- hidden_out: bfloat16 [8, 1536, 1024], P('dp', 'ctx')
- grad_hidden: float32 [8, 1536, 1024], P('dp', 'ctx')
- query_weight_grad: float32 [1024, 1024], P('ctx')
- key_weight_grad: float32 [1024, 1024], P('ctx')
- value_weight_grad: float32 [1024, 1024], P('ctx')
- output_weight_grad: float32 [1024, 1024], P('ctx')
- inner_weight_grad: float32 [1024, 4096], P('ctx')
- outer_weight_grad: float32 [4096, 1024], P('ctx')
- query_bias_grad: float32 [1024], P('ctx')
- value_bias_grad: float32 [1024], P('ctx')
- output_bias_grad: float32 [1024], P('ctx')
- inner_bias_grad: float32 [4096], P('ctx')
- outer_bias_grad: float32 [1024], P('ctx')
- attn_gain_grad: float32 [1024], P('ctx')
- attn_shift_grad: float32 [1024], P('ctx')
- ffn_gain_grad: float32 [1024], P('ctx')
- ffn_shift_grad: float32 [1024], P('ctx')
- time_table_grad: float32 [512, 1024], P('ctx')
The draws below stay inside these ranges and needn't reach their ends.
Inputs may be any that keep to these rules, and one draw needn't show every extreme that they name: `context_len`: at least half of 1152; some row has exactly 1152. `timestep`: mostly in the upper half, a few near zero.
All inputs are finite; a program needn't handle non-finite values.
Results may differ from the reference program's by a relative error of at most 0.014.
Values may be sent and summed in bfloat16 or wider, within the bound.
No kernel may reach another device: no remote copies, remote signals or barrier semaphores. Data moves between devices by JAX's collectives and lax.ppermute only.
A program may use at most 192 MiB of HBM per device.

```python
import math
import jax
import jax.numpy as jnp
from jax import lax

D = 1024
HEADS = 16
HD = 64
FF = 4096
SLOT = 384
BLOCK = 25
TSTEPS = 512
ROWS = 8
SPAN = 1536
CTX_MAX = 1152
N_CTX = 4


def draw_context_len(key, part):
    key = jax.random.fold_in(key, 5)
    first, second = jax.random.split(key)
    longest = CTX_MAX
    shortest = CTX_MAX // 2
    lengths = jax.random.randint(first, (ROWS,), shortest, longest + 1, dtype=jnp.int32)
    marker = jax.random.randint(second, (), 0, ROWS, dtype=jnp.int32)
    lengths = lengths.at[marker].set(longest)
    return lengths.at[(marker + 1) % ROWS].set(shortest)


def draw_timestep(key, part):
    key = jax.random.fold_in(key, 9)
    parts = jax.random.split(key, 4)
    noisy = jax.random.randint(parts[0], (ROWS,), TSTEPS // 2, TSTEPS, dtype=jnp.int32)
    clean = jax.random.randint(parts[1], (ROWS,), 0, max(TSTEPS // 16, 1), dtype=jnp.int32)
    chosen = jax.random.randint(parts[2], (ROWS,), 0, 8, dtype=jnp.int32) == 0
    levels = jnp.where(chosen, clean, noisy)
    marker = jax.random.randint(parts[3], (), 0, ROWS, dtype=jnp.int32)
    levels = levels.at[marker].set(TSTEPS - 1)
    return levels.at[(marker + 1) % ROWS].set(0)


def with_ends(entries, own_key, least, largest):
    longest = entries.shape.index(max(entries.shape))
    spots = []
    for shift in (0, 1):
        where = [jax.random.randint(jax.random.fold_in(own_key, axis), (), 0, length) for axis, length in enumerate(entries.shape)]
        where[longest] = (where[longest] + shift) % entries.shape[longest]
        spots.append(tuple(where))
    return entries.at[spots[0]].set(least).at[spots[1]].set(largest)


def level_of(rng, shape, pieces, low, top_value):
    factor_of, own = 1.0, jax.random.fold_in(rng, 6)
    for axis_at, blocks in pieces:
        heights = jnp.exp(jax.random.uniform(jax.random.fold_in(own, axis_at), (blocks,), jnp.float32, low / len(pieces), top_value / len(pieces)))
        factor_of = factor_of * jnp.repeat(heights, shape[axis_at] // blocks).reshape([-1 if axis == axis_at else 1 for axis in range(len(shape))])
    return factor_of


def centred(stream_key, dims, scale, bound, shards=(), held_as=jnp.bfloat16):
    loudness = level_of(stream_key, dims, shards, -0.22, 0.18) if shards else 1.0
    values = jax.random.normal(stream_key, dims, jnp.float32) * scale * loudness
    return jnp.minimum(jnp.maximum(values, -bound), bound).astype(held_as)


def setup_inputs(seed: int = 0) -> dict:
    key_of = jax.random.split(jax.random.key(seed), 22)
    hidden_in = centred(key_of[0], (ROWS, SPAN, D), 1.0, 6.0, ((0, 8), (1, 4)))
    cotangent = centred(key_of[1], (ROWS, SPAN, D), 1.0, 6.0, ((0, 8), (1, 4)))
    context_len = draw_context_len(jax.random.fold_in(key_of[21], 71), 0)
    block_device = with_ends(jax.random.randint(key_of[3], (ROWS,), 0, N_CTX), jax.random.fold_in(key_of[3], 1), 0, N_CTX - 1).astype(jnp.int32)
    timestep = draw_timestep(jax.random.fold_in(key_of[21], 71), 0)
    query_weight = centred(key_of[5], (D, D), D ** -0.5, 0.1875, ((0, 4),))
    key_weight = centred(key_of[6], (D, D), D ** -0.5, 0.1875, ((0, 4),))
    value_weight = centred(key_of[7], (D, D), D ** -0.5, 0.1875, ((0, 4),))
    output_weight = centred(key_of[8], (D, D), (max(D // 64, 1)) ** -0.5, 1.5, ((0, 4),))
    inner_weight = centred(key_of[9], (D, FF), D ** -0.5, 0.1875, ((0, 4),))
    outer_weight = centred(key_of[10], (FF, D), FF ** -0.5, 0.09375, ((0, 4),))
    query_bias = centred(key_of[11], (D,), 0.3, 1.5)
    value_bias = centred(key_of[12], (D,), 0.3, 1.5)
    output_bias = centred(key_of[13], (D,), 0.3, 1.5)
    inner_bias = centred(key_of[14], (FF,), 0.3, 1.5)
    outer_bias = centred(key_of[15], (D,), 0.3, 1.5)
    attn_gain = jnp.clip(1.0 + 0.1 * jax.random.normal(key_of[16], (D,), jnp.float32), 0.5, 1.5).astype(jnp.bfloat16)
    attn_shift = centred(key_of[17], (D,), 0.3, 1.5)
    ffn_gain = jnp.clip(1.0 + 0.1 * jax.random.normal(key_of[18], (D,), jnp.float32), 0.5, 1.5).astype(jnp.bfloat16)
    ffn_shift = centred(key_of[19], (D,), 0.3, 1.5)
    time_table = centred(key_of[20], (TSTEPS, D), 0.5, 3.0)
    return {"hidden_in": hidden_in, "cotangent": cotangent, "context_len": context_len, "block_device": block_device, "timestep": timestep, "query_weight": query_weight, "key_weight": key_weight, "value_weight": value_weight, "output_weight": output_weight, "inner_weight": inner_weight, "outer_weight": outer_weight, "query_bias": query_bias, "value_bias": value_bias, "output_bias": output_bias, "inner_bias": inner_bias, "outer_bias": outer_bias, "attn_gain": attn_gain, "attn_shift": attn_shift, "ffn_gain": ffn_gain, "ffn_shift": ffn_shift, "time_table": time_table}


@jax.custom_vjp
def low(v):
    return lax.optimization_barrier(v.astype(jnp.bfloat16)).astype(jnp.float32)

@jax.custom_vjp
def low_back(v):
    return v

def low_keep(v):
    return (low(v), None)

def low_pass(kept, grad):
    return (grad,)

def back_keep(v):
    return (v, None)

def back_low(kept, grad):
    return (low(grad),)
low.defvjp(low_keep, low_pass)
low_back.defvjp(back_keep, back_low)
EPSILON = 1e-05

def matmul(left, right):
    return jnp.dot(left, right, precision=lax.Precision.HIGHEST, preferred_element_type=jnp.float32)

def layer_norm(values, gain, shift):
    center = values - lax.optimization_barrier(jnp.mean(values, -1, keepdims=True))
    spread = lax.optimization_barrier(jnp.mean(center * center, -1, keepdims=True))
    return center * lax.rsqrt(spread + EPSILON) * gain + shift

def part_counts(context_len, block_device, count_ctx):
    device = jnp.arange(count_ctx, dtype=jnp.int32)[None, :]
    base = (context_len // (count_ctx - 1)).astype(jnp.int32)[:, None]
    extra = (context_len % (count_ctx - 1)).astype(jnp.int32)[:, None]
    order = device - (device > block_device[:, None]).astype(jnp.int32)
    count = base + (order < extra).astype(jnp.int32)
    return jnp.where(device == block_device[:, None], BLOCK, count).astype(jnp.int32)

def attend(trio, keymask):
    query, keys, values = trio
    scale = 1.0 / math.sqrt(HD)
    scores = low_back(jnp.where(keymask[None, :], matmul(query, keys.T) * scale, -1e+30))
    probs = jax.nn.softmax(scores, axis=-1)
    return matmul(low(probs), values)

def forward(weights, hidden, table, valid, block, step):
    query_weight, key_weight, value_weight, output_weight, inner_weight, outer_weight, query_bias, value_bias, output_bias, inner_bias, outer_bias, attn_gain, attn_shift, ffn_gain, ffn_shift = weights
    span = hidden.shape[0]
    start = hidden + block[:, None] * table[step][None, :]
    start_low = low(start)
    query = low_back(low(matmul(start_low, query_weight) + query_bias))
    keys = low_back(low(matmul(start_low, key_weight)))
    values = low_back(low(matmul(start_low, value_weight) + value_bias))
    keymask = valid > 0.5
    split_query = query.reshape(span, HEADS, HD).transpose(1, 0, 2)
    split_keys = keys.reshape(span, HEADS, HD).transpose(1, 0, 2)
    split_values = values.reshape(span, HEADS, HD).transpose(1, 0, 2)
    mixed = lax.map(jax.checkpoint(lambda trio: attend(trio, keymask)), (split_query, split_keys, split_values))
    attn = low_back(low(mixed.transpose(1, 0, 2).reshape(span, HEADS * HD)))
    first = low_back(matmul(attn, output_weight)) + output_bias + start
    normed = layer_norm(first, attn_gain, attn_shift)
    inner = low_back(matmul(low(normed), inner_weight) + inner_bias)
    active = low(jax.nn.gelu(inner))
    second = low_back(matmul(active, outer_weight)) + outer_bias + normed
    return layer_norm(second, ffn_gain, ffn_shift) * valid[:, None]

def reference(hidden_in, cotangent, context_len, block_device, timestep, query_weight, key_weight, value_weight, output_weight, inner_weight, outer_weight, query_bias, value_bias, output_bias, inner_bias, outer_bias, attn_gain, attn_shift, ffn_gain, ffn_shift, time_table):
    weights = tuple((item.astype(jnp.float32) for item in (query_weight, key_weight, value_weight, output_weight, inner_weight, outer_weight, query_bias, value_bias, output_bias, inner_bias, outer_bias, attn_gain, attn_shift, ffn_gain, ffn_shift)))
    table = time_table.astype(jnp.float32)
    hidden = hidden_in.astype(jnp.float32)
    incoming = cotangent.astype(jnp.float32)
    counts = part_counts(context_len, block_device, N_CTX)
    slot = jnp.arange(SLOT, dtype=jnp.int32)
    device = jnp.arange(N_CTX, dtype=jnp.int32)
    valid = (slot[None, None, :] < counts[:, :, None]).astype(jnp.float32).reshape(ROWS, SPAN)
    block = (device[None, :, None] == block_device[:, None, None]) & (slot[None, None, :] < BLOCK)
    block = block.astype(jnp.float32).reshape(ROWS, SPAN)
    zeros = (jax.tree.map(jnp.zeros_like, weights), jnp.zeros_like(table))

    def one_row(carry, row):
        hidden_row, cot_row, valid_row, block_row, step = row

        def apply(weights_now, hidden_now, table_now):
            return forward(weights_now, hidden_now, table_now, valid_row, block_row, step)
        result, pull = jax.vjp(apply, weights, hidden_row, table)
        weight_grads, hidden_grad, table_grad = pull(cot_row)
        carry = (jax.tree.map(jnp.add, carry[0], weight_grads), carry[1] + table_grad)
        return (carry, (result.astype(jnp.bfloat16), hidden_grad))
    (grads, table_grad), (outputs, hidden_grads) = lax.scan(one_row, zeros, (hidden, incoming, valid, block, timestep.astype(jnp.int32)))
    return (outputs, hidden_grads, grads[0], grads[1], grads[2], grads[3], grads[4], grads[5], grads[6], grads[7], grads[8], grads[9], grads[10], grads[11], grads[12], grads[13], grads[14], table_grad)
```

```python
import functools
import math

import jax
import jax.numpy as jnp
from jax import lax
from jax.experimental import pallas as pl
from jax.experimental.pallas import tpu as pltpu
from jax.sharding import PartitionSpec as P

HEADS = 16
HD = 64
BLOCK = 25
EPSILON = 1e-05
GROUP = 8
TAIL = 128
PAIR = 2 * HD
LOG2E = 1.4426950408889634
LOW = jnp.bfloat16
WIDE = jnp.float32
VMEM = pl.BlockSpec(memory_space=pltpu.VMEM)
SMEM = pl.BlockSpec(memory_space=pltpu.SMEM)
ANY = pl.BlockSpec(memory_space=pl.ANY)


def params(mib=48):
    return pltpu.CompilerParams(vmem_limit_bytes=mib << 20)


def layer_norm(values, gain, shift):
    center = values - jnp.mean(values, -1, keepdims=True)
    spread = jnp.mean(center * center, -1, keepdims=True)
    return center * lax.rsqrt(spread + EPSILON) * gain + shift


def dot(left, right, dims, out=WIDE):
    return lax.dot_general(left, right, (dims, ((), ())), preferred_element_type=out)


def left_dot(left, right, out=WIDE):
    return dot(left, right, ((0,), (0,)), out)


def right_dot(left, right):
    return dot(left, right, ((1,), (1,)))


def swap(value, mask):
    size = lax.axis_size("dp")
    return lax.ppermute(value, "dp", [(i, i ^ mask) for i in range(size)])


def turn(value, k):
    size = lax.axis_size("ctx")
    return lax.ppermute(value, "ctx", [(i, (i + k) % size) for i in range(size)])


def take(value, index, axis=0):
    return lax.dynamic_index_in_dim(value, index, axis, keepdims=False)


def add(left, right):
    return (left.astype(WIDE) + right.astype(WIDE)).astype(LOW)


def plane_gather(one, two):
    one, two = {0: one}, {0: two}
    one[2], two[4] = swap(one[0], 2), swap(two[0], 4)
    one[4], two[2] = swap(one[0], 4), swap(two[0], 2)
    one[6], two[6] = swap(one[2], 4), swap(two[4], 2)
    for mask in (0, 2, 4, 6):
        one[mask + 1], two[mask + 1] = swap(one[mask], 1), swap(two[mask], 1)
    return [one[m] for m in range(GROUP)], [two[m] for m in range(GROUP)]


def plane_reduce(grad, d):
    core, x, y = d & 1, (d >> 1) & 1, (d >> 2) & 1
    grad = add(take(grad, core, 3), swap(take(grad, 1 - core, 3), 1))
    one, two = grad[:, :, :, 0], grad[:, :, :, 1]
    got_one, got_two = swap(take(one, 1 - x, 2), 2), swap(take(two, 1 - y, 1), 4)
    one, two = add(take(one, x, 2), got_one), add(take(two, y, 1), got_two)
    got_one, got_two = swap(take(one, 1 - y, 1), 4), swap(take(two, 1 - x, 1), 2)
    return add(take(one, y, 1), got_one), add(take(two, x, 1), got_two)


def place_weight(shard, masks, halves, ids_ref, own_ref, *refs):
    pieces, out_ref, sems = refs[:-2], refs[-2], refs[-1]
    n = out_ref.shape[0] // shard
    part = shard // GROUP
    rows = part // halves
    copies = [
        pltpu.make_async_copy(
            own_ref, out_ref.at[pl.ds(pl.multiple_of(ids_ref[0] * shard, 16), shard)], sems.at[0]
        )
    ]
    for m in range(masks):
        start = (ids_ref[1] ^ m) * part
        for h in range(halves):
            piece = pieces[m * halves + h]
            for k in range(1, n):
                home = lax.rem(ids_ref[0] + n - k, n) * shard
                where = pl.multiple_of(home + start + h * rows, rows)
                copies.append(
                    pltpu.make_async_copy(
                        piece.at[k - 1], out_ref.at[pl.ds(where, rows)], sems.at[len(copies)]
                    )
                )
    for copy in copies:
        copy.start()
    for copy in copies:
        copy.wait()


def whole_weight(ids, own, pieces, halves, n):
    rows, cols = own.shape
    body = functools.partial(place_weight, rows, GROUP, halves)
    return pl.pallas_call(
        body,
        out_shape=jax.ShapeDtypeStruct((n * rows, cols), own.dtype),
        in_specs=[SMEM] + [ANY] * (1 + len(pieces)),
        out_specs=VMEM,
        scratch_shapes=[pltpu.SemaphoreType.DMA((1 + len(pieces) * (n - 1),))],
        compiler_params=params(),
        cost_estimate=pl.CostEstimate(
            flops=0, bytes_accessed=n * rows * cols * 4, transcendentals=0
        ),
    )(ids, own, *pieces)


def gather_weight(ids, own, d, n):
    part = own.shape[0] // GROUP
    piece = lax.dynamic_slice_in_dim(own, d * part, part, 0)
    got = jnp.stack([turn(piece, k) for k in range(1, n)])
    one, two = plane_gather(got[:, : part // 2], got[:, part // 2 :])
    pieces = [item for pair in zip(one, two) for item in pair]
    return whole_weight(ids, own, pieces, 2, n)


def gather_columns(ids, own, d, place, n):
    part = own.shape[0] // GROUP
    cols = own.shape[1] // n
    blocks = own.reshape(own.shape[0], 3, n, cols // 3)
    piece = lax.dynamic_slice_in_dim(blocks, d * part, part, 0)
    pick = lambda v, g: take(v, g % n, 2).reshape(v.shape[0], cols)
    got = jnp.stack([turn(pick(piece, place + k), k) for k in range(1, n)])
    pieces = [got] + [swap(got, m) for m in range(1, GROUP)]
    return whole_weight(ids, pick(blocks, place), pieces, 1, n)


def place_grad(ids_ref, *refs):
    pieces, out_ref = refs[:-1], refs[-1]
    rows = pieces[0].shape[0]
    for i, piece in enumerate(pieces):
        where = ((ids_ref[1] ^ (i // 2)) * 2 + i % 2) * rows
        out_ref[pl.ds(pl.multiple_of(where, rows), rows), :] = piece[...].astype(WIDE)


def share_grad(ids, grad, d, place, n):
    rows, cols = grad.shape
    part = rows // (n * GROUP * 2)
    one, two = plane_reduce(grad.reshape(n, 2, 2, 2, 2, part, cols), d)
    both = jnp.stack([one, two], 1)
    return finish_grad(ids, both, place, n)


def finish_grad(ids, both, place, n):
    got = [turn(take(both, (place + k) % n), k) for k in range(1, n)]
    total = take(both, place).astype(WIDE)
    for item in got:
        total = total + item.astype(WIDE)
    return spread_grad(ids, total)


def spread_grad(ids, total):
    total = total.astype(LOW)
    mask = GROUP
    while mask < lax.axis_size("dp"):
        total = add(total, swap(total, mask))
        mask *= 2
    one, two = plane_gather(total[0], total[1])
    pieces = [item for pair in zip(one, two) for item in pair]
    part, cols = total.shape[1:]
    return pl.pallas_call(
        place_grad,
        out_shape=jax.ShapeDtypeStruct((2 * GROUP * part, cols), WIDE),
        in_specs=[SMEM] + [VMEM] * len(pieces),
        out_specs=VMEM,
        compiler_params=params(),
    )(ids, *pieces)


def attend(full, bias_ref, q_ref, k_ref, v_ref, out_ref, lse_ref):
    tile = pl.program_id(0)
    slots = out_ref.shape[0]
    first = lax.broadcasted_iota(jnp.int32, (1, PAIR), 1) < HD

    def work(rows):
        query = q_ref[:rows, :]
        keys, values = k_ref[...], v_ref[...]
        outs = []
        for h in range(2):
            mine = first if h == 0 else jnp.logical_not(first)
            scores = right_dot(jnp.where(mine, query, 0), keys)
            scores = scores * (LOG2E / math.sqrt(HD)) + bias_ref[...]
            high = jnp.max(scores, -1, keepdims=True)
            expo = jnp.exp2(scores - high)
            total = jnp.sum(expo, -1, keepdims=True)
            probs = (expo * (1.0 / total)).astype(LOW)
            outs.append(dot(probs, values, ((1,), (0,))))
            lse = jnp.broadcast_to(high + jnp.log2(total), (rows, 128))
            lse_ref[h : h + 1, :rows] = lse.T[:1, :]
        out_ref[:rows, :] = jnp.where(first, outs[0], outs[1]).astype(LOW)

    @pl.when(tile < full)
    def _():
        work(slots)

    @pl.when(tile == full)
    def _():
        work(TAIL)
        out_ref[TAIL:, :] = jnp.zeros((slots - TAIL, PAIR), LOW)
        lse_ref[:, TAIL:] = jnp.zeros((8, slots - TAIL), WIDE)


def attention(qkv, bias, pair, pairs, n, slots):
    span = qkv.shape[0]
    whole = lambda col: pl.BlockSpec((span, PAIR), lambda t: (0, col))
    return pl.pallas_call(
        functools.partial(attend, n - 1),
        grid=(n,),
        out_shape=(
            jax.ShapeDtypeStruct((n * slots, PAIR), LOW),
            jax.ShapeDtypeStruct((8, n * slots), WIDE),
        ),
        in_specs=[
            pl.BlockSpec((1, span), lambda t: (0, 0)),
            pl.BlockSpec((slots, PAIR), lambda t: (t, pair)),
            whole(pairs + pair),
            whole(2 * pairs + pair),
        ],
        out_specs=(
            pl.BlockSpec((slots, PAIR), lambda t: (t, 0)),
            pl.BlockSpec((8, slots), lambda t: (0, t)),
        ),
        compiler_params=params(),
        cost_estimate=pl.CostEstimate(
            flops=8 * span * span * PAIR, bytes_accessed=span * PAIR * 10, transcendentals=0
        ),
    )(bias, qkv, qkv, qkv)


def attend_back(full, bias_ref, q_ref, k_ref, v_ref, do_ref, lse_ref, out_ref, dk_ref, dv_ref):
    tile = pl.program_id(0)
    slots = q_ref.shape[0]
    span = k_ref.shape[0]
    first = lax.broadcasted_iota(jnp.int32, (1, PAIR), 1) < HD
    scale = 1.0 / math.sqrt(HD)

    @pl.when(tile == 0)
    def _():
        dk_ref[...] = jnp.zeros_like(dk_ref)
        dv_ref[...] = jnp.zeros_like(dv_ref)
        out_ref[span:, :] = jnp.zeros((out_ref.shape[0] - span, 3 * PAIR), LOW)

    def work(rows):
        keys, values = k_ref[...], v_ref[...]
        outs = []
        for h in range(2):
            mine = first if h == 0 else jnp.logical_not(first)
            query = jnp.where(mine, q_ref[:rows, :], 0)
            grad = jnp.where(mine, do_ref[:rows, :], 0)
            scores = right_dot(keys, query) * (LOG2E * scale)
            bias = jnp.concatenate([bias_ref[...]] * (rows // 128), 1)
            probs = jnp.exp2(scores + bias - lse_ref[h : h + 1, :rows])
            grad_probs = right_dot(values, grad)
            center = jnp.sum(grad_probs * probs, 0, keepdims=True)
            grad_scores = (probs * (grad_probs - center)).astype(LOW)
            dk_ref[...] += dot(grad_scores, query, ((1,), (0,)))
            dv_ref[...] += dot(probs.astype(LOW), grad, ((1,), (0,)))
            outs.append(left_dot(grad_scores, keys))
        start = pl.multiple_of(tile * slots, slots)
        out_ref[pl.ds(start, rows), :PAIR] = (jnp.where(first, outs[0], outs[1]) * scale).astype(LOW)

    @pl.when(tile < full)
    def _():
        work(slots)

    @pl.when(tile == full)
    def _():
        work(TAIL)
        out_ref[:span, PAIR : 2 * PAIR] = (dk_ref[...] * scale).astype(LOW)
        out_ref[:span, 2 * PAIR :] = dv_ref[...].astype(LOW)


def attention_back(qkv, bias, grad, lse, pair, pairs, n, slots):
    span = qkv.shape[0]
    whole = lambda col: pl.BlockSpec((span, PAIR), lambda t: (0, col))
    return pl.pallas_call(
        functools.partial(attend_back, n - 1),
        grid=(n,),
        out_shape=jax.ShapeDtypeStruct((n * slots, 3 * PAIR), LOW),
        in_specs=[
            pl.BlockSpec((span, 128), lambda t: (0, 0)),
            pl.BlockSpec((slots, PAIR), lambda t: (t, pair)),
            whole(pairs + pair),
            whole(2 * pairs + pair),
            pl.BlockSpec((slots, PAIR), lambda t: (t, pair)),
            pl.BlockSpec((8, slots), lambda t: (0, t)),
        ],
        out_specs=pl.BlockSpec((n * slots, 3 * PAIR), lambda t: (0, 0)),
        scratch_shapes=[pltpu.VMEM((span, PAIR), WIDE), pltpu.VMEM((span, PAIR), WIDE)],
        compiler_params=params(),
        cost_estimate=pl.CostEstimate(
            flops=20 * span * span * PAIR, bytes_accessed=span * PAIR * 20, transcendentals=0
        ),
    )(bias, qkv, qkv, qkv, grad, lse)


def per_device(
    hidden_in,
    cotangent,
    context_len,
    block_device,
    timestep,
    query_weight,
    key_weight,
    value_weight,
    output_weight,
    inner_weight,
    outer_weight,
    query_bias,
    value_bias,
    output_bias,
    inner_bias,
    outer_bias,
    attn_gain,
    attn_shift,
    ffn_gain,
    ffn_shift,
    time_table,
):
    n = lax.axis_size("ctx")
    place = lax.axis_index("ctx")
    dp_index = lax.axis_index("dp")
    d = dp_index % GROUP
    ids = jnp.stack([place, d]).astype(jnp.int32)
    rows, slots, width = hidden_in.shape
    own_cols = width // n
    pairs = own_cols // PAIR
    span = (n - 1) * slots + TAIL
    holder = block_device[0]
    context = context_len[0]

    order = [j + (j >= holder).astype(jnp.int32) for j in range(n - 1)] + [holder]
    steps = [(place - g + n) % n for g in order]
    position = lambda g: jnp.where(g == holder, n - 1, g - (g > holder).astype(jnp.int32))
    counts = [context // (n - 1) + (j < context % (n - 1)).astype(jnp.int32) for j in range(n - 1)]
    counts = jnp.stack(counts + [jnp.int32(BLOCK)])
    slot = jnp.arange(slots, dtype=jnp.int32)
    live = (slot[None, :] < counts[:, None]).reshape(n * slots)[:span]
    bias = jnp.where(live, 0.0, -1e30).astype(WIDE)
    bias_row, bias_col = bias[None, :], jnp.broadcast_to(bias[:, None], (span, 128))
    owned = take(counts, position(place))
    valid = (slot < owned).astype(WIDE)[:, None]
    block = ((holder == place) & (slot < BLOCK)).astype(WIDE)[:, None]
    embed = lax.dynamic_slice_in_dim(time_table, timestep[0], 1, 0).astype(WIDE)
    start = hidden_in[0].astype(WIDE) + block * embed
    start_low = start.astype(LOW)

    qkv_weight = jnp.concatenate([query_weight, key_weight, value_weight], 1)
    qkv_own = gather_columns(ids, qkv_weight, d, place, n)
    parts = jnp.stack([start_low] + [turn(start_low, k) for k in range(1, n)])
    compact = jnp.concatenate([take(parts, k) for k in steps])
    output_full = gather_weight(ids, output_weight, d, n)
    inner_full = gather_weight(ids, inner_weight, d, n)
    outer_full = gather_weight(ids, outer_weight, d, n)
    qkv_full = gather_weight(ids, qkv_weight, d, n)

    own_bias = lambda v: lax.dynamic_slice_in_dim(v, place * own_cols, own_cols, 0).astype(WIDE)
    qkv_bias = jnp.concatenate(
        [own_bias(query_bias), jnp.zeros((own_cols,), WIDE), own_bias(value_bias)]
    )
    qkv = (jnp.dot(compact[:span], qkv_own, preferred_element_type=WIDE) + qkv_bias).astype(LOW)

    to_group = lambda v, g: lax.dynamic_slice_in_dim(v, position(g % n) * slots, slots, 0)

    def by_group(parts):
        turned = jnp.stack([parts[-k % n] for k in range(n)] * 2)
        return lax.dynamic_slice_in_dim(turned, (n - place) % n, n, 0)

    mixed, lses = [], []
    for pair in range(pairs):
        out, lse = attention(qkv, bias_row, pair, pairs, n, slots)
        lses.append(lse)
        mixed.append(
            by_group([to_group(out, place)] + [turn(to_group(out, place + k), k) for k in range(1, n)])
        )
    attn = jnp.stack(mixed).transpose(2, 1, 0, 3).reshape(slots, width)

    first = (
        jnp.dot(attn, output_full, preferred_element_type=WIDE) + output_bias.astype(WIDE) + start
    )
    normed, norm_pull = jax.vjp(layer_norm, first, attn_gain.astype(WIDE), attn_shift.astype(WIDE))
    normed_low = normed.astype(LOW)
    inner = jnp.dot(normed_low, inner_full, preferred_element_type=WIDE) + inner_bias.astype(WIDE)
    active, gelu_pull = jax.vjp(jax.nn.gelu, inner)
    active_low = active.astype(LOW)
    second = (
        jnp.dot(active_low, outer_full, preferred_element_type=WIDE)
        + outer_bias.astype(WIDE)
        + normed
    )
    result, final_pull = jax.vjp(layer_norm, second, ffn_gain.astype(WIDE), ffn_shift.astype(WIDE))
    hidden_out = (result * valid).astype(LOW)[None]
    incoming = cotangent[0].astype(WIDE) * valid
    grad_second, ffn_gain_grad, ffn_shift_grad = final_pull(incoming)
    outer_bias_grad = jnp.sum(grad_second, 0)
    second_low = grad_second.astype(LOW)
    outer_weight_grad = share_grad(ids, left_dot(active_low, second_low, LOW), d, place, n)
    (grad_inner,) = gelu_pull(right_dot(second_low, outer_full))
    inner_low = grad_inner.astype(LOW)
    inner_bias_grad = jnp.sum(inner_low.astype(WIDE), 0)
    inner_weight_grad = share_grad(ids, left_dot(normed_low, inner_low, LOW), d, place, n)
    grad_normed = right_dot(inner_low, inner_full) + grad_second
    grad_first, attn_gain_grad, attn_shift_grad = norm_pull(grad_normed)
    output_bias_grad = jnp.sum(grad_first, 0)
    first_low = grad_first.astype(LOW)
    output_weight_grad = share_grad(ids, left_dot(attn, first_low, LOW), d, place, n)
    grad_attn = right_dot(first_low, output_full).astype(LOW)

    columns = lambda v, g: lax.dynamic_slice_in_dim(v, (g % n) * own_cols, own_cols, 1)
    parts = jnp.stack(
        [columns(grad_attn, place)]
        + [turn(columns(grad_attn, place + k), k) for k in range(1, n)]
    )
    grad_mixed = jnp.concatenate([take(parts, k) for k in steps])
    backs, received = [], []
    for pair in range(pairs):
        back = attention_back(qkv, bias_col, grad_mixed, lses[pair], pair, pairs, n, slots)
        backs.append(back)
        received.append(
            by_group([to_group(back, place)] + [turn(to_group(back, place + k), k) for k in range(1, n)])
        )
    grad_qkv = jnp.stack(received).reshape(pairs, n, slots, 3, PAIR)
    grad_qkv = grad_qkv.transpose(2, 3, 1, 0, 4).reshape(slots, 3 * width)
    grad_start = right_dot(grad_qkv, qkv_full) + grad_first
    grad_hidden = grad_start[None]

    back = jnp.stack(backs).reshape(pairs, n * slots, 3, PAIR)
    back = back.transpose(1, 2, 0, 3).reshape(n * slots, 3 * own_cols)
    bias_sums = jnp.sum(back.astype(WIDE), 0)
    own_grad = left_dot(compact, back, LOW)
    part = width // (n * GROUP * 2)
    one, two = plane_reduce(own_grad.reshape(n, 2, 2, 2, 2, part, 3 * own_cols), d)
    both = jnp.stack([one, two], 1)
    got = [take(both, place)] + [turn(take(both, (place + k) % n), k) for k in range(1, n)]
    got = by_group(got).reshape(n, 2, part, 3, own_cols)
    got = got.transpose(1, 2, 3, 0, 4).reshape(2, part, 3 * width)
    qkv_grad = spread_grad(ids, got)
    weight_grads = [qkv_grad[:, i * width : (i + 1) * width] for i in range(3)]

    small = [
        output_bias_grad,
        inner_bias_grad,
        outer_bias_grad,
        attn_gain_grad,
        attn_shift_grad,
        ffn_gain_grad,
        ffn_shift_grad,
    ]
    packed = jnp.concatenate([v.reshape(n, -1) for v in small], 1)
    total = take(packed, place)
    for k in range(1, n):
        total = total + turn(take(packed, (place + k) % n), k)
    total = jnp.concatenate([total, bias_sums])
    mask = 1
    while mask < lax.axis_size("dp"):
        total = total + swap(total, mask)
        mask *= 2
    sums, at = [], 0
    for v in small:
        sums.append(total[at : at + v.shape[0] // n])
        at += v.shape[0] // n
    query_sum, value_sum = total[at : at + own_cols], total[at + 2 * own_cols : at + 3 * own_cols]

    block_sums = lax.psum(jnp.sum(grad_start * block, 0), "ctx")
    all_sums = lax.all_gather(block_sums, "dp")
    all_steps = lax.all_gather(timestep, "dp", tiled=True)
    levels = jnp.arange(time_table.shape[0] // n, dtype=jnp.int32) + place * (
        time_table.shape[0] // n
    )
    onehot = (all_steps[:, None] == levels[None, :]).astype(WIDE)
    time_table_grad = lax.dot_general(
        onehot,
        all_sums,
        (((0,), (0,)), ((), ())),
        precision=lax.Precision.HIGHEST,
        preferred_element_type=WIDE,
    )
    return (
        hidden_out,
        grad_hidden,
        *weight_grads,
        output_weight_grad,
        inner_weight_grad,
        outer_weight_grad,
        query_sum,
        value_sum,
        *sums,
        time_table_grad,
    )


def solution(mesh):
    row, shard, same = P("dp", "ctx", None), P("ctx", None), P()
    return jax.shard_map(
        per_device,
        mesh=mesh,
        in_specs=(row, row, P("dp"), P("dp"), P("dp")) + (shard,) * 6 + (same,) * 10,
        out_specs=(row, row) + (shard,) * 6 + (P("ctx"),) * 9 + (shard,),
        check_vma=False,
    )
```

```python
import functools
import math

import jax
import jax.numpy as jnp
from jax import lax
from jax.experimental import pallas as pl
from jax.experimental.pallas import tpu as pltpu
from jax.sharding import PartitionSpec as P

HEADS = 16
HD = 64
BLOCK = 25
EPSILON = 1e-05
GROUP = 8
TAIL = 128
PAIR = 2 * HD
STEP = 512
LOG2E = 1.4426950408889634
LOW = jnp.bfloat16
WIDE = jnp.float32
VMEM = pl.BlockSpec(memory_space=pltpu.VMEM)
SMEM = pl.BlockSpec(memory_space=pltpu.SMEM)
ANY = pl.BlockSpec(memory_space=pl.ANY)
PLACE, INDEX, CORE, X, Y, OWNED, HERE, LISTS = range(8)


def params(mib=56):
    return pltpu.CompilerParams(vmem_limit_bytes=mib << 20)


def cost(flops, nbytes):
    return pl.CostEstimate(flops=int(flops), bytes_accessed=int(nbytes), transcendentals=0)


def shape(*dims, dtype=LOW):
    return jax.ShapeDtypeStruct(dims, dtype)


def dot(left, right, dims=((1,), (0,))):
    return lax.dot_general(left, right, (dims, ((), ())), preferred_element_type=WIDE)


def left_dot(left, right):
    return dot(left, right, ((0,), (0,)))


def right_dot(left, right):
    return dot(left, right, ((1,), (1,)))


def part_of(start, size):
    return pl.ds(pl.multiple_of(start, size), size)


def swap(value, mask):
    size = lax.axis_size("dp")
    return lax.ppermute(value, "dp", [(i, i ^ mask) for i in range(size)])


def turn(value, k):
    size = lax.axis_size("ctx")
    return lax.ppermute(value, "ctx", [(i, (i + k) % size) for i in range(size)])


def after(value, *others):
    return lax.optimization_barrier((value, *others))[0]


def plane_gather(one, two):
    one, two = {0: one}, {0: two}
    one[2], two[4] = swap(one[0], 2), swap(two[0], 4)
    one[4], two[2] = swap(one[0], 4), swap(two[0], 2)
    one[6], two[6] = swap(one[2], 4), swap(two[4], 2)
    for mask in (0, 2, 4, 6):
        one[mask + 1], two[mask + 1] = swap(one[mask], 1), swap(two[mask], 1)
    return [item[m] for m in range(GROUP) for item in (one, two)]


def loads(ids, own, pieces, sems, held, rows, row, col):
    n, _, cols = held.shape
    copies = []
    at = 0
    for ref, width in own:
        copies.append(
            pltpu.make_async_copy(ref, held.at[0, :, pl.ds(at, width)], sems.at[len(copies)])
        )
        at += width
    for i, piece in enumerate(pieces):
        where = ((ids[INDEX] ^ (i // 2)) * 2 + i % 2) * rows
        copies.append(
            pltpu.make_async_copy(
                piece.at[:, pl.ds(row, rows), pl.ds(col, cols)],
                held.at[pl.ds(1, n - 1), part_of(where, rows), :],
                sems.at[len(copies)],
            )
        )
    return copies


def begin(copies):
    for copy in copies:
        copy.start()


def finish(copies):
    for copy in copies:
        copy.wait()


def shard_of(ids, k, n):
    return lax.rem(ids[PLACE] + n - k, n)


def project(n, ids, *refs):
    parts, (wq, wk, wv), refs = refs[:n], refs[n : n + 3], refs[n + 3 :]
    pieces, (bias, compact, out, held, sems) = refs[: 2 * GROUP], refs[2 * GROUP :]
    slots, width = parts[0].shape
    cols = width // n
    rows = pieces[0].shape[1]
    copies = []
    for j, own in enumerate((wq, wk, wv)):
        copies.append(
            pltpu.make_async_copy(
                own.at[:, part_of(ids[PLACE] * cols, cols)],
                held.at[0, :, pl.ds(j * cols, cols)],
                sems.at[len(copies)],
            )
        )
        for i, piece in enumerate(pieces):
            where = ((ids[INDEX] ^ (i // 2)) * 2 + i % 2) * rows
            copies.append(
                pltpu.make_async_copy(
                    piece.at[:, :, part_of(j * width + ids[PLACE] * cols, cols)],
                    held.at[pl.ds(1, n - 1), part_of(where, rows), pl.ds(j * cols, cols)],
                    sems.at[len(copies)],
                )
            )
    begin(copies)
    for k in range(n):
        compact[part_of(ids[LISTS + k] * slots, slots), :] = parts[k][...]
    finish(copies)

    def block(i, _):
        row = part_of(i * 256, 256)
        total = bias[...]
        for k in range(n):
            column = part_of(shard_of(ids, k, n) * cols, cols)
            total = total + dot(compact[row, column], held[k])
        out[row, :] = total.astype(LOW)
        return 0

    lax.fori_loop(0, out.shape[0] // 256, block, 0)


def attend(n, ids, bias_ref, q_ref, k_ref, v_ref, *refs):
    outs, lse_ref = refs[:n], refs[n]
    tile = pl.program_id(0)
    slots = q_ref.shape[0]
    first = lax.broadcasted_iota(jnp.int32, (1, PAIR), 1) < HD

    def work(rows):
        query = q_ref[:rows, :]
        keys, values = k_ref[...], v_ref[...]
        mixed = []
        for h in range(2):
            mine = first if h == 0 else jnp.logical_not(first)
            scores = right_dot(jnp.where(mine, query, 0), keys)
            scores = scores * (LOG2E / math.sqrt(HD)) + bias_ref[...]
            high = jnp.max(scores, -1, keepdims=True)
            expo = jnp.exp2(scores - high)
            total = jnp.sum(expo, -1, keepdims=True)
            probs = (expo * (1.0 / total)).astype(LOW)
            mixed.append(dot(probs, values))
            lse = jnp.broadcast_to(high + jnp.log2(total), (rows, 128))
            lse_ref[h : h + 1, :rows] = lse.T[:1, :]
        result = jnp.where(first, mixed[0], mixed[1]).astype(LOW)
        for k, out_ref in enumerate(outs):

            @pl.when(ids[LISTS + n + tile] == k)
            def _():
                out_ref[:rows, :] = result
                if rows < slots:
                    out_ref[rows:, :] = jnp.zeros((slots - rows, PAIR), LOW)

    @pl.when(tile < n - 1)
    def _():
        work(slots)

    @pl.when(tile == n - 1)
    def _():
        work(TAIL)
        lse_ref[:, TAIL:] = jnp.zeros((8, slots - TAIL), WIDE)


def attention(ids, qkv, bias, pair, pairs, n, slots):
    span = qkv.shape[0]
    whole = lambda col: pl.BlockSpec((span, PAIR), lambda t, ids: (0, col))
    return pl.pallas_call(
        functools.partial(attend, n),
        grid_spec=pltpu.PrefetchScalarGridSpec(
            num_scalar_prefetch=1,
            grid=(n,),
            in_specs=[
                pl.BlockSpec((1, span), lambda t, ids: (0, 0)),
                pl.BlockSpec((slots, PAIR), lambda t, ids: (t, pair)),
                whole(pairs + pair),
                whole(2 * pairs + pair),
            ],
            out_specs=[pl.BlockSpec((slots, PAIR), lambda t, ids: (0, 0))] * n
            + [pl.BlockSpec((8, slots), lambda t, ids: (0, t))],
        ),
        out_shape=[shape(slots, PAIR)] * n + [shape(8, n * slots, dtype=WIDE)],
        compiler_params=params(),
        cost_estimate=cost(8 * span * span * PAIR, span * PAIR * 10),
    )(ids, bias, qkv, qkv, qkv)


def attend_back(n, ids, bias_ref, q_ref, k_ref, v_ref, *refs):
    grads, (lse_ref,), outs = refs[:n], refs[n : n + 1], refs[n + 1 : 2 * n + 1]
    do_ref, dk_ref, dv_ref = refs[2 * n + 1 :]
    tile = pl.program_id(0)
    slots = q_ref.shape[0]
    span = k_ref.shape[0]
    first = lax.broadcasted_iota(jnp.int32, (1, PAIR), 1) < HD
    scale = 1.0 / math.sqrt(HD)

    @pl.when(tile == 0)
    def _():
        dk_ref[...] = jnp.zeros_like(dk_ref)
        dv_ref[...] = jnp.zeros_like(dv_ref)
        for k in range(n):
            do_ref[part_of(ids[LISTS + k] * slots, slots), :] = grads[k][...]

    def work(rows):
        keys, values = k_ref[...], v_ref[...]
        here = pl.ds(pl.multiple_of(tile * slots, slots), rows)
        parts = []
        for h in range(2):
            mine = first if h == 0 else jnp.logical_not(first)
            query = jnp.where(mine, q_ref[:rows, :], 0)
            grad = jnp.where(mine, do_ref[here, :], 0)
            scores = right_dot(keys, query) * (LOG2E * scale)
            bias = jnp.concatenate([bias_ref[...]] * (rows // 128), 1)
            probs = jnp.exp2(scores + bias - lse_ref[h : h + 1, :rows])
            grad_probs = right_dot(values, grad)
            center = jnp.sum(grad_probs * probs, 0, keepdims=True)
            grad_scores = (probs * (grad_probs - center)).astype(LOW)
            dk_ref[:span, :] += dot(grad_scores, query)
            dv_ref[:span, :] += dot(probs.astype(LOW), grad)
            parts.append(left_dot(grad_scores, keys))
        result = (jnp.where(first, parts[0], parts[1]) * scale).astype(LOW)
        for k, out_ref in enumerate(outs):

            @pl.when(ids[LISTS + n + tile] == k)
            def _():
                out_ref[:rows, :PAIR] = result
                if rows < slots:
                    out_ref[rows:, :PAIR] = jnp.zeros((slots - rows, PAIR), LOW)

    @pl.when(tile < n - 1)
    def _():
        work(slots)

    @pl.when(tile == n - 1)
    def _():
        work(TAIL)
        for k, out_ref in enumerate(outs):
            here = part_of(ids[LISTS + 2 * n + k] * slots, slots)
            out_ref[:, PAIR : 2 * PAIR] = (dk_ref[here, :] * scale).astype(LOW)
            out_ref[:, 2 * PAIR :] = dv_ref[here, :].astype(LOW)


def attention_back(ids, qkv, bias, grads, lse, pair, pairs, n, slots):
    span = qkv.shape[0]
    whole = lambda col: pl.BlockSpec((span, PAIR), lambda t, ids: (0, col))
    return pl.pallas_call(
        functools.partial(attend_back, n),
        grid_spec=pltpu.PrefetchScalarGridSpec(
            num_scalar_prefetch=1,
            grid=(n,),
            in_specs=[
                pl.BlockSpec((span, 128), lambda t, ids: (0, 0)),
                pl.BlockSpec((slots, PAIR), lambda t, ids: (t, pair)),
                whole(pairs + pair),
                whole(2 * pairs + pair),
            ]
            + [pl.BlockSpec((slots, PAIR), lambda t, ids: (0, pair))] * n
            + [pl.BlockSpec((8, slots), lambda t, ids: (0, t))],
            out_specs=[pl.BlockSpec((slots, 3 * PAIR), lambda t, ids: (0, 0))] * n,
            scratch_shapes=[
                pltpu.VMEM((n * slots, PAIR), LOW),
                pltpu.VMEM((n * slots, PAIR), WIDE),
                pltpu.VMEM((n * slots, PAIR), WIDE),
            ],
        ),
        out_shape=[shape(slots, 3 * PAIR)] * n,
        compiler_params=params(),
        cost_estimate=cost(20 * span * span * PAIR, span * PAIR * 20),
    )(ids, bias, qkv, qkv, qkv, *grads, lse)


def normal(values):
    center = values - jnp.mean(values, -1, keepdims=True)
    scale = lax.rsqrt(jnp.mean(center * center, -1, keepdims=True) + EPSILON)
    return center * scale, scale


def normal_back(grad, unit, scale):
    inner = jnp.mean(grad * unit, -1, keepdims=True)
    return (grad - jnp.mean(grad, -1, keepdims=True) - unit * inner) * scale


def wide(ref):
    return ref[...].astype(WIDE)


def forward(n, pairs, ids, *refs):
    parts, refs = refs[: n * pairs], refs[n * pairs :]
    start, cotangent, wo_own, wi_own, wu_own = refs[:5]
    bo, bi, bu, gain1, shift1, gain2, shift2 = refs[5:12]
    refs = refs[12:]
    side, tall, refs = refs[: 2 * GROUP], refs[2 * GROUP : 4 * GROUP], refs[4 * GROUP :]
    attn, first, normed_low, active, slope, out, grad_second, second_low, sums = refs[:9]
    wo, wi, wu, normed, second, sem_o, sem_i, sem_u = refs[9:]
    slots, width = start.shape
    cols = width // n
    hidden = active.shape[1]
    deep = hidden // n
    row_o, row_u = cols // (2 * GROUP), deep // (2 * GROUP)
    get_o = loads(ids, [(wo_own, width)], tall, sem_o, wo, row_o, 0, 0)
    get_i = loads(ids, [(wi_own, hidden)], side, sem_i, wi, row_o, 0, 3 * width)
    get_u = loads(ids, [(wu_own, width)], tall, sem_u, wu, row_u, row_o, 0)
    begin(get_o)
    begin(get_i)
    begin(get_u)
    for k in range(n):
        mine = jnp.concatenate([parts[p * n + k][...] for p in range(pairs)], 1)
        attn[:, part_of(shard_of(ids, k, n) * cols, cols)] = mine
    finish(get_o)

    def mix(j, _):
        column = part_of(j * STEP, STEP)
        total = start[:, column] + wide(bo.at[:, column])
        for k in range(n):
            left = attn[:, part_of(shard_of(ids, k, n) * cols, cols)]
            total = total + dot(left, wo[k, :, column])
        first[:, column] = total
        return 0

    lax.fori_loop(0, width // STEP, mix, 0)

    def norm(i, _):
        row = part_of(i * 128, 128)
        unit, _ = normal(first[row, :])
        value = unit * wide(gain1) + wide(shift1)
        normed[row, :] = value
        normed_low[row, :] = value.astype(LOW)
        return 0

    lax.fori_loop(0, slots // 128, norm, 0)
    finish(get_i)

    def expand(j, _):
        column = part_of(j * STEP, STEP)
        x = jnp.broadcast_to(wide(bi.at[:, column]), (slots, STEP))
        for k in range(n):
            left = normed_low[:, part_of(shard_of(ids, k, n) * cols, cols)]
            x = x + dot(left, wi[k, :, column])
        factor = math.sqrt(2 / math.pi)
        square = x * x
        t = jnp.tanh(factor * x * (1.0 + 0.044715 * square))
        half = 0.5 * (1.0 + t)
        active[:, column] = (x * half).astype(LOW)
        slope[:, column] = half + (0.5 * factor) * x * (1.0 - t * t) * (1.0 + 0.134145 * square)
        return 0

    lax.fori_loop(0, hidden // STEP, expand, 0)
    finish(get_u)

    def contract(j, _):
        column = part_of(j * STEP, STEP)
        total = normed[:, column] + wide(bu.at[:, column])
        for k in range(n):
            left = active[:, part_of(shard_of(ids, k, n) * deep, deep)]
            total = total + dot(left, wu[k, :, column])
        second[:, column] = total
        return 0

    lax.fori_loop(0, width // STEP, contract, 0)
    sums[...] = jnp.zeros_like(sums)

    def last(i, _):
        row = part_of(i * 128, 128)
        live = lax.broadcasted_iota(jnp.int32, (128, 1), 0) + i * 128 < ids[OWNED]
        live = live.astype(WIDE)
        unit, scale = normal(second[row, :])
        out[row, :] = ((unit * wide(gain2) + wide(shift2)) * live).astype(LOW)
        grad = cotangent[row, :].astype(WIDE) * live
        result = normal_back(grad * wide(gain2), unit, scale)
        grad_second[row, :] = result
        second_low[row, :] = result.astype(LOW)
        for j, item in enumerate((grad * unit, grad, result)):
            sums[j : j + 1, :] += jnp.sum(item, 0, keepdims=True)
        return 0

    lax.fori_loop(0, slots // 128, last, 0)


def backward(n, ids, *refs):
    second_low, grad_second, slope, first, gain1, sums = refs[:6]
    wo_own, wi_own, wu_own = refs[6:9]
    refs = refs[9:]
    side, tall, refs = refs[: 2 * GROUP], refs[2 * GROUP : 4 * GROUP], refs[4 * GROUP :]
    inner_low, grad_first, first_low = refs[:3]
    outs, small = refs[3 : 3 + n], refs[3 + n]
    wo, wi, wu, grad_normed, bias_sum, more, sem_o, sem_i, sem_u = refs[4 + n :]
    slots, width = first.shape
    cols = width // n
    hidden = slope.shape[1]
    deep = hidden // n
    row_o, row_u = cols // (2 * GROUP), deep // (2 * GROUP)
    get_o = loads(ids, [(wo_own, width)], tall, sem_o, wo, row_o, 0, 0)
    get_i = loads(ids, [(wi_own, hidden)], side, sem_i, wi, row_o, 0, 3 * width)
    get_u = loads(ids, [(wu_own, width)], tall, sem_u, wu, row_u, row_o, 0)
    begin(get_u)
    begin(get_i)
    begin(get_o)
    finish(get_u)

    def expand(j, _):
        for k in range(n):
            column = part_of(shard_of(ids, k, n) * deep + j * STEP, STEP)
            grad = right_dot(second_low[...], wu[k, part_of(j * STEP, STEP), :])
            value = (grad * slope[:, column]).astype(LOW)
            inner_low[:, column] = value
            bias_sum[:, column] = jnp.sum(value.astype(WIDE), 0, keepdims=True)
        return 0

    lax.fori_loop(0, deep // STEP, expand, 0)
    finish(get_i)
    for k in range(n):
        column = part_of(shard_of(ids, k, n) * cols, cols)
        grad_normed[:, column] = right_dot(inner_low[...], wi[k]) + grad_second[:, column]
    more[...] = jnp.zeros_like(more)

    def norm(i, _):
        row = part_of(i * 128, 128)
        unit, scale = normal(first[row, :])
        grad = grad_normed[row, :]
        result = normal_back(grad * wide(gain1), unit, scale)
        grad_first[row, :] = result
        first_low[row, :] = result.astype(LOW)
        for j, item in enumerate((result, grad * unit, grad)):
            more[j : j + 1, :] += jnp.sum(item, 0, keepdims=True)
        return 0

    lax.fori_loop(0, slots // 128, norm, 0)
    finish(get_o)
    for k in range(n):
        outs[k][...] = right_dot(first_low[...], wo[k]).astype(LOW)
    small[...] = jnp.zeros_like(small)
    for z in range(n):
        far = lax.rem(z + n - ids[PLACE], n)
        here = pl.ds(z * cols, cols)
        rows = [more[0:1, here]]
        rows += [bias_sum[:, pl.ds(z * deep + j * cols, cols)] for j in range(deep // cols)]
        rows += [sums[2:3, here], more[1:2, here], more[2:3, here], sums[0:1, here], sums[1:2, here]]
        for j, item in enumerate(rows):
            small[far, j : j + 1, :] = item


def finish_hidden(n, pairs, ids, *refs):
    parts, refs = refs[: n * pairs], refs[n * pairs :]
    grad_first, wq, wk, wv = refs[:4]
    side, (out, total, held, acts, sems) = refs[4 : 4 + 2 * GROUP], refs[4 + 2 * GROUP :]
    slots, width = out.shape
    cols = width // n
    copies = loads(
        ids, [(wq, width), (wk, width), (wv, width)], side, sems, held, cols // (2 * GROUP), 0, 0
    )
    begin(copies)
    for k in range(n):
        for p in range(pairs):
            for j in range(3):
                column = j * width + shard_of(ids, k, n) * cols + p * PAIR
                acts[:, part_of(column, PAIR)] = parts[p * n + k][:, j * PAIR : (j + 1) * PAIR]
    finish(copies)
    for k in range(n):
        column = part_of(shard_of(ids, k, n) * cols, cols)
        out[:, column] = right_dot(acts[...], held[k]) + grad_first[:, column]
    block = lax.broadcasted_iota(jnp.int32, (32, 1), 0) < ids[HERE]
    total[...] = jnp.sum(jnp.where(block, out[:32, :], 0.0), 0, keepdims=True)


def outer_product(spec, keep, ids, *refs):
    lefts, rights = [], []
    for count, _ in spec:
        lefts.append(refs[:count])
        rights.append(refs[count : 2 * count])
        refs = refs[2 * count :]
    at = 0
    for (count, cols), left, right in zip(spec, lefts, rights):
        step = min(cols, 1024)
        for col in range(0, cols, step):
            total = left_dot(left[0][...], right[0][:, col : col + step])
            for i in range(1, count):
                total = total + left_dot(left[i][...], right[i][:, col : col + step])
            here = slice(at + col, at + col + step)
            if not keep:
                refs[0][0, :, here] = total.astype(LOW)
                continue
            got, outs = refs[0], refs[1:]
            total = (total + got[0, :, here].astype(WIDE)).astype(LOW)
            split_halves(ids, total, [out.at[0, :, here] for out in outs], (X, Y))
        at += cols


def split_halves(ids, total, outs, bits):
    rows = total.shape[0] // 4
    parts = [total[i * rows : (i + 1) * rows] for i in range(4)]
    for half, bit in enumerate(bits):
        high = ids[bit] == 1
        low_part, high_part = parts[2 * half], parts[2 * half + 1]
        outs[2 * half][...] = jnp.where(high, low_part, high_part)
        outs[2 * half + 1][...] = jnp.where(high, high_part, low_part)


def gradient(ids, spec, n, got=None):
    rows = spec[0][0][0][0].shape[1] // (2 * n)
    keep = got is not None
    in_specs, args, total, flops = [], [], 0, 0
    for pairs, cols in spec:
        for left, _ in pairs:
            block = lambda z, ids: (0, 2 * z + (ids[CORE] if keep else 1 - ids[CORE]))
            in_specs.append(pl.BlockSpec((left.shape[0], rows), block))
            args.append(left)
        for _, right in pairs:
            in_specs.append(pl.BlockSpec(right.shape, lambda z, ids: (0, 0)))
            args.append(right)
            flops += 2 * n * rows * right.shape[0] * cols
        total += cols
    if keep:
        in_specs.append(pl.BlockSpec((1, rows, total), lambda z, ids: (z, 0, 0)))
        args.append(got)
    out_rows, count = (rows // 4, 4) if keep else (rows, 1)
    return pl.pallas_call(
        functools.partial(outer_product, [(len(pairs), cols) for pairs, cols in spec], keep),
        grid_spec=pltpu.PrefetchScalarGridSpec(
            num_scalar_prefetch=1,
            grid=(n,),
            in_specs=in_specs,
            out_specs=[pl.BlockSpec((1, out_rows, total), lambda z, ids: (z, 0, 0))] * count,
        ),
        out_shape=[shape(n, out_rows, total)] * count,
        compiler_params=params(),
        cost_estimate=cost(flops, flops / 500),
    )(ids, *args)


def fold_two(ids, keep_one, got_one, keep_two, got_two, *outs):
    rows = keep_one.shape[1] // 2
    for z in range(keep_one.shape[0]):
        one = (keep_one[z].astype(WIDE) + got_one[z].astype(WIDE)).astype(LOW)
        two = (keep_two[z].astype(WIDE) + got_two[z].astype(WIDE)).astype(LOW)
        for total, bit, (send, keep) in ((one, Y, outs[:2]), (two, X, outs[2:])):
            high = ids[bit] == 1
            send[z] = jnp.where(high, total[:rows], total[rows:])
            keep[z] = jnp.where(high, total[rows:], total[:rows])


def fold_three(ids, keep_one, got_one, keep_two, got_two, *outs):
    n = len(outs)
    for k, out in enumerate(outs):
        z = lax.rem(ids[PLACE] + k, n)
        out[0] = (keep_one[z].astype(WIDE) + got_one[z].astype(WIDE)).astype(LOW)
        out[1] = (keep_two[z].astype(WIDE) + got_two[z].astype(WIDE)).astype(LOW)


def fold_four(*refs):
    refs, outs = refs[:-2], refs[-2:]
    for h, out in enumerate(outs):
        total = refs[0][h].astype(WIDE)
        for ref in refs[1:]:
            total = total + ref[h].astype(WIDE)
        out[...] = total.astype(LOW)


def fold_heads(ids, *refs):
    refs, outs = refs[:-2], refs[-2:]
    n, cols = len(refs), refs[0].shape[2]
    for h, out in enumerate(outs):
        for k, ref in enumerate(refs):
            out[:, part_of(shard_of(ids, k, n) * cols, cols)] = ref[h]


def small_call(body, ids, args, outs):
    nbytes = sum(v.size * 2 for v in args)
    return pl.pallas_call(
        body,
        in_specs=([SMEM] if ids is not None else []) + [VMEM] * len(args),
        out_specs=[VMEM] * len(outs),
        out_shape=outs,
        compiler_params=params(),
        cost_estimate=cost(0, 2 * nbytes),
    )(*([ids] if ids is not None else []), *args)


def reduce_first(ids, spec, n):
    (send,) = gradient(ids, spec, n)
    return swap(send, 1)


def reduce_second(ids, spec, n, got):
    send_one, keep_one, send_two, keep_two = gradient(ids, spec, n, got)
    return keep_one, swap(send_one, 2), keep_two, swap(send_two, 4)


def reduce_third(ids, n, held):
    rows, cols = held[0].shape[1:]
    outs = [shape(n, rows // 2, cols)] * 4
    send_one, keep_one, send_two, keep_two = small_call(fold_two, ids, held, outs)
    return keep_one, swap(send_one, 4), keep_two, swap(send_two, 2)


def reduce_fourth(ids, n, held):
    rows, cols = held[0].shape[1:]
    outs = small_call(fold_three, ids, held, [shape(2, rows, cols)] * n)
    return [outs[0]] + [turn(outs[k], k) for k in range(1, n)]


def reduce_fifth(ids, held, heads=False):
    rows, cols = held[0].shape[1:]
    if heads:
        one, two = small_call(fold_heads, ids, held, [shape(rows, len(held) * cols)] * 2)
    else:
        one, two = small_call(fold_four, None, held, [shape(rows, cols)] * 2)
    mask = GROUP
    while mask < lax.axis_size("dp"):
        one, two = [(v.astype(WIDE) + swap(v, mask).astype(WIDE)).astype(LOW) for v in (one, two)]
        mask *= 2
    return plane_gather(one, two)


def place_grad(plan, ids, *refs):
    pieces, outs = refs[: 2 * GROUP], refs[2 * GROUP :]
    rows = pieces[0].shape[0]
    for i, piece in enumerate(pieces):
        home = ids[INDEX] ^ (i // 2)
        core, x, y = home & 1, (home >> 1) & 1, (home >> 2) & 1
        block = core * 8 + (x * 2 + y if i % 2 == 0 else 4 + y * 2 + x)
        row = part_of(block * rows, rows)
        for out, moves in zip(outs, plan):
            for source, target, size in moves:
                out[row, target : target + size] = piece[:, source : source + size].astype(WIDE)


def reduce_last(ids, pieces, plan, widths):
    rows = pieces[0].shape[0] * 2 * GROUP
    return small_call(
        functools.partial(place_grad, plan),
        ids,
        pieces,
        [shape(rows, width, dtype=WIDE) for width in widths],
    )


def per_device(
    hidden_in,
    cotangent,
    context_len,
    block_device,
    timestep,
    query_weight,
    key_weight,
    value_weight,
    output_weight,
    inner_weight,
    outer_weight,
    query_bias,
    value_bias,
    output_bias,
    inner_bias,
    outer_bias,
    attn_gain,
    attn_shift,
    ffn_gain,
    ffn_shift,
    time_table,
):
    n = lax.axis_size("ctx")
    place = lax.axis_index("ctx")
    d = lax.axis_index("dp") % GROUP
    _, slots, width = hidden_in.shape
    hidden = inner_weight.shape[1]
    cols = width // n
    deep = hidden // n
    pairs = cols // PAIR
    span = (n - 1) * slots + TAIL
    holder = block_device[0]
    context = context_len[0]

    order = [j + (j >= holder).astype(jnp.int32) for j in range(n - 1)] + [holder]
    position = lambda g: jnp.where(g == holder, n - 1, g - (g > holder).astype(jnp.int32))
    counts = [context // (n - 1) + (j < context % (n - 1)).astype(jnp.int32) for j in range(n - 1)]
    counts = jnp.stack(counts + [jnp.int32(BLOCK)])
    slot = jnp.arange(slots, dtype=jnp.int32)
    live = (slot[None, :] < counts[:, None]).reshape(n * slots)[:span]
    bias = jnp.where(live, 0.0, -1e30).astype(WIDE)
    bias_row, bias_col = bias[None, :], jnp.broadcast_to(bias[:, None], (span, 128))
    owned = lax.dynamic_index_in_dim(counts, position(place), keepdims=False)
    here = jnp.where(holder == place, BLOCK, 0)
    ids = [place, d, d & 1, (d >> 1) & 1, (d >> 2) & 1, owned, here]
    ids += [position((place - k + n) % n) for k in range(n)]
    ids += [(g - place + n) % n for g in order]
    ids += [position((place + k) % n) for k in range(n)]
    ids = jnp.stack([jnp.asarray(v, jnp.int32) for v in ids])
    embed = lax.dynamic_slice_in_dim(time_table, timestep[0], 1, 0).astype(WIDE)
    block = ((holder == place) & (slot < BLOCK)).astype(WIDE)[:, None]
    start = hidden_in[0].astype(WIDE) + block * embed
    start_low = start.astype(LOW)

    def piece(weight):
        part = weight.shape[0] // GROUP
        return lax.dynamic_slice_in_dim(weight, d * part, part, 0).reshape(2, part // 2, -1)

    side_piece = jnp.concatenate(
        [piece(w) for w in (query_weight, key_weight, value_weight, inner_weight)], 2
    )
    tall_piece = jnp.concatenate([piece(output_weight), piece(outer_weight)], 1)
    side = jnp.stack([turn(side_piece, k) for k in range(1, n)])
    tall_piece = after(tall_piece, side)
    tall = jnp.stack([turn(tall_piece, k) for k in range(1, n)])
    sent = after(start_low, tall)
    parts = [start_low] + [turn(sent, k) for k in range(1, n)]
    side = plane_gather(side[:, 0], side[:, 1])
    tall = plane_gather(tall[:, 0], tall[:, 1])
    own_bias = lambda v: lax.dynamic_slice_in_dim(v, place * cols, cols, 0).astype(WIDE)
    qkv_bias = jnp.concatenate([own_bias(query_bias), jnp.zeros((cols,), WIDE), own_bias(value_bias)])
    _, qkv = pl.pallas_call(
        functools.partial(project, n),
        in_specs=[SMEM] + [VMEM] * n + [ANY] * (3 + 2 * GROUP) + [VMEM],
        out_specs=[VMEM, VMEM],
        out_shape=[shape(n * slots, width), shape(span, 3 * cols)],
        scratch_shapes=[
            pltpu.VMEM((n, cols, 3 * cols), LOW),
            pltpu.SemaphoreType.DMA((3 + 6 * GROUP,)),
        ],
        compiler_params=params(),
        cost_estimate=cost(6 * span * width * cols, 4 * span * width),
    )(ids, *parts, query_weight, key_weight, value_weight, *side, qkv_bias[None])

    mixed, lses = [], []
    for pair in range(pairs):
        *outs, lse = attention(ids, qkv, bias_row, pair, pairs, n, slots)
        lses.append(lse)
        mixed += [outs[0]] + [turn(outs[k], k) for k in range(1, n)]

    row = lambda v: v[None, :]
    weights = [
        pltpu.VMEM((n, cols, width), LOW),
        pltpu.VMEM((n, cols, hidden), LOW),
        pltpu.VMEM((n, deep, width), LOW),
    ]
    sems = [pltpu.SemaphoreType.DMA((1 + 2 * GROUP,))] * 3
    flops = 2 * slots * width * (width + 2 * hidden)
    attn, first, normed_low, active, slope, out, grad_second, second_low, sums = pl.pallas_call(
        functools.partial(forward, n, pairs),
        in_specs=[SMEM] + [VMEM] * (n * pairs + 2) + [ANY] * 3 + [VMEM] * 7 + [ANY] * (4 * GROUP),
        out_specs=[VMEM] * 9,
        out_shape=[
            shape(slots, width),
            shape(slots, width, dtype=WIDE),
            shape(slots, width),
            shape(slots, hidden),
            shape(slots, hidden, dtype=WIDE),
            shape(slots, width),
            shape(slots, width, dtype=WIDE),
            shape(slots, width),
            shape(8, width, dtype=WIDE),
        ],
        scratch_shapes=weights
        + [pltpu.VMEM((slots, width), WIDE), pltpu.VMEM((slots, width), WIDE)]
        + sems,
        compiler_params=params(),
        cost_estimate=cost(flops, flops / 300),
    )(
        ids,
        *mixed,
        start,
        cotangent[0],
        output_weight,
        inner_weight,
        outer_weight,
        row(output_bias),
        row(inner_bias),
        row(outer_bias),
        row(attn_gain),
        row(attn_shift),
        row(ffn_gain),
        row(ffn_shift),
        *side,
        *tall,
    )
    outer_spec = [([(active, second_low)], width)]
    outer_held = reduce_first(ids, outer_spec, n)

    inner_low, grad_first, first_low, *rest = pl.pallas_call(
        functools.partial(backward, n),
        in_specs=[SMEM] + [VMEM] * 6 + [ANY] * (3 + 4 * GROUP),
        out_specs=[VMEM] * (4 + n),
        out_shape=[
            shape(slots, hidden),
            shape(slots, width, dtype=WIDE),
            shape(slots, width),
        ]
        + [shape(slots, cols)] * n
        + [shape(n, 16, cols, dtype=WIDE)],
        scratch_shapes=weights
        + [
            pltpu.VMEM((slots, width), WIDE),
            pltpu.VMEM((1, hidden), WIDE),
            pltpu.VMEM((8, width), WIDE),
        ]
        + sems,
        compiler_params=params(),
        cost_estimate=cost(flops, flops / 300),
    )(
        ids,
        second_low,
        grad_second,
        slope,
        first,
        row(attn_gain),
        sums,
        output_weight,
        inner_weight,
        outer_weight,
        *side,
        *tall,
    )
    grad_parts, small = rest[:n], rest[n]
    grad_mixed = [grad_parts[0]] + [turn(grad_parts[n - k], k) for k in range(1, n)]
    inner_spec = [([(normed_low, inner_low)], hidden), ([(attn, first_low)], width)]
    inner_held = reduce_first(ids, inner_spec, n)
    outer_held = reduce_second(ids, outer_spec, n, outer_held)
    inner_held = reduce_second(ids, inner_spec, n, inner_held)
    outer_held = reduce_third(ids, n, outer_held)

    backs, received = [], []
    for pair in range(pairs):
        back = attention_back(ids, qkv, bias_col, grad_mixed, lses[pair], pair, pairs, n, slots)
        backs.append(back)
        received += [back[0]] + [turn(back[k], k) for k in range(1, n)]
        if pair == 0:
            outer_held = reduce_fourth(ids, n, outer_held)
            inner_held = reduce_third(ids, n, inner_held)
    qkv_spec = [([(parts[-k % n], back[k]) for k in range(n)], 3 * PAIR) for back in backs]
    qkv_held = reduce_first(ids, qkv_spec, n)
    qkv_held = reduce_second(ids, qkv_spec, n, qkv_held)
    inner_held = reduce_fourth(ids, n, inner_held)
    outer_pieces = reduce_fifth(ids, outer_held)
    qkv_held = reduce_third(ids, n, qkv_held)
    qkv_held = reduce_fourth(ids, n, qkv_held)
    inner_pieces = reduce_fifth(ids, inner_held)
    qkv_pieces = reduce_fifth(ids, qkv_held, heads=True)
    (outer_grad,) = reduce_last(ids, outer_pieces, [[(0, 0, width)]], [width])
    inner_grad, output_grad = reduce_last(
        ids, inner_pieces, [[(0, 0, hidden)], [(hidden, 0, width)]], [hidden, width]
    )
    plan = [
        [
            (g * 3 * cols + p * 3 * PAIR + j * PAIR, g * cols + p * PAIR, PAIR)
            for g in range(n)
            for p in range(pairs)
        ]
        for j in range(3)
    ]
    weight_grads = reduce_last(ids, qkv_pieces, plan, [width] * 3)

    grad_hidden, block_sum = pl.pallas_call(
        functools.partial(finish_hidden, n, pairs),
        in_specs=[SMEM] + [VMEM] * (n * pairs + 1) + [ANY] * (3 + 2 * GROUP),
        out_specs=[VMEM] * 2,
        out_shape=[shape(slots, width, dtype=WIDE), shape(1, width, dtype=WIDE)],
        scratch_shapes=[
            pltpu.VMEM((n, cols, 3 * width), LOW),
            pltpu.VMEM((slots, 3 * width), LOW),
            pltpu.SemaphoreType.DMA((3 + 2 * GROUP,)),
        ],
        compiler_params=params(),
        cost_estimate=cost(6 * slots * width * width, 8 * width * width),
    )(ids, *received, grad_first, query_weight, key_weight, value_weight, *side)

    def everywhere(value):
        mask = 1
        while mask < lax.axis_size("dp"):
            value = value + swap(value, mask)
            mask *= 2
        return value

    total = small[0]
    for k in range(1, n):
        total = total + turn(small[k], k)
    total = everywhere(total)
    per = deep // cols
    sums = [total[0], total[1 : 1 + per].reshape(deep)] + [total[1 + per + i] for i in range(5)]
    bias_sums = jnp.stack([sum(jnp.sum(v.astype(WIDE), 0) for v in back) for back in backs])
    bias_sums = everywhere(bias_sums)
    query_sum = bias_sums[:, :PAIR].reshape(cols)
    value_sum = bias_sums[:, 2 * PAIR :].reshape(cols)

    vector, level = block_sum, timestep.astype(WIDE)[:, None]
    vector = vector + sum(turn(block_sum, k) for k in range(1, n))
    mask = 1
    while mask < lax.axis_size("dp"):
        vector = jnp.concatenate([vector, swap(vector, mask)])
        level = jnp.concatenate([level, swap(level, mask)])
        mask *= 2
    share = time_table.shape[0] // n
    levels = (jnp.arange(share, dtype=jnp.int32) + place * share).astype(WIDE)
    onehot = (level == levels[None, :]).astype(WIDE)
    time_table_grad = lax.dot_general(
        onehot,
        vector,
        (((0,), (0,)), ((), ())),
        precision=lax.Precision.HIGHEST,
        preferred_element_type=WIDE,
    )
    return (
        out[None],
        grad_hidden[None],
        *weight_grads,
        output_grad,
        inner_grad,
        outer_grad,
        query_sum,
        value_sum,
        *sums,
        time_table_grad,
    )


def solution(mesh):
    row, shard, same = P("dp", "ctx", None), P("ctx", None), P()
    return jax.shard_map(
        per_device,
        mesh=mesh,
        in_specs=(row, row, P("dp"), P("dp"), P("dp")) + (shard,) * 6 + (same,) * 10,
        out_specs=(row, row) + (shard,) * 6 + (P("ctx"),) * 9 + (shard,),
        check_vma=False,
    )
```

```python
import functools
import math

import jax
import jax.numpy as jnp
from jax import lax
from jax.experimental import pallas as pl
from jax.experimental.pallas import tpu as pltpu
from jax.sharding import PartitionSpec as P

HEADS = 16
HD = 64
BLOCK = 25
EPSILON = 1e-05
GROUP = 8
TAIL = 128
PAIR = 2 * HD
STEP = 512
LOG2E = 1.4426950408889634
LOW = jnp.bfloat16
WIDE = jnp.float32
VMEM = pl.BlockSpec(memory_space=pltpu.VMEM)
SMEM = pl.BlockSpec(memory_space=pltpu.SMEM)
ANY = pl.BlockSpec(memory_space=pl.ANY)
PLACE, INDEX, CORE, X, Y, OWNED, HERE, LISTS = range(8)


def params(mib=56):
    return pltpu.CompilerParams(vmem_limit_bytes=mib << 20)


def cost():
    return pl.CostEstimate(flops=10**11, bytes_accessed=10**9, transcendentals=0)


def shape(*dims, dtype=LOW):
    return jax.ShapeDtypeStruct(dims, dtype)


def dot(left, right, dims=((1,), (0,))):
    return lax.dot_general(left, right, (dims, ((), ())), preferred_element_type=WIDE)


def left_dot(left, right):
    return dot(left, right, ((0,), (0,)))


def right_dot(left, right):
    return dot(left, right, ((1,), (1,)))


def part_of(start, size):
    return pl.ds(pl.multiple_of(start, size), size)


def swap(value, mask):
    size = lax.axis_size("dp")
    return lax.ppermute(value, "dp", [(i, i ^ mask) for i in range(size)])


def turn(value, k):
    size = lax.axis_size("ctx")
    return lax.ppermute(value, "ctx", [(i, (i + k) % size) for i in range(size)])


def exchange(value):
    return lax.all_to_all(value, "ctx", 0, 0)


def after(value, *others):
    return lax.optimization_barrier((value, *others))[0]


def shard_gather(value, *early):
    n = lax.axis_size("ctx")
    value = after(value, *early) if early else value
    if n != 4:
        got = [turn(value, k) for k in range(1, n)]
        return got, got[0]
    place = lax.axis_index("ctx")
    far = lax.ppermute(value, "ctx", [(0, 2), (1, 3), (2, 0), (3, 1)])
    up = lax.ppermute(value, "ctx", [(0, 1), (1, 2), (2, 3)])
    down = lax.ppermute(value, "ctx", [(1, 0), (2, 1), (3, 2)])
    on = lax.ppermute(far, "ctx", [(2, 3), (1, 0)])
    return [jnp.where(place == 0, on, up), far, jnp.where(place == n - 1, on, down)], far


class Order:
    def __init__(self, ids):
        self.ids = ids

    def call(self, body, *args, **kwargs):
        outs = pl.pallas_call(body, **kwargs)(self.ids, *args)
        self.wait(outs[0] if isinstance(outs, (list, tuple)) else outs)
        return outs

    def wait(self, *values):
        self.ids = after(self.ids, *values)


def gather_near(one, two):
    return jnp.stack([one, swap(one, 2)]), jnp.stack([two, swap(two, 4)])


def gather_far(one, two):
    return jnp.stack([one, swap(one, 4)]), jnp.stack([two, swap(two, 2)])


def gather_cores(one, two):
    return one, two, swap(one, 1), swap(two, 1)


def piece_of(arrays, mask, half):
    x, y = (mask >> 1) & 1, (mask >> 2) & 1
    return arrays[2 * (mask & 1) + half].at[(x, y) if half else (y, x)]


def loads(ids, own, pieces, sems, held, rows, row, col):
    n, _, cols = held.shape
    copies = []
    at = 0
    for ref, width in own:
        copies.append(
            pltpu.make_async_copy(ref, held.at[0, :, pl.ds(at, width)], sems.at[len(copies)])
        )
        at += width
    for i in range(2 * GROUP):
        where = ((ids[INDEX] ^ (i // 2)) * 2 + i % 2) * rows
        piece = piece_of(pieces, i // 2, i % 2)
        copies.append(
            pltpu.make_async_copy(
                piece.at[:, pl.ds(row, rows), pl.ds(col, cols)],
                held.at[pl.ds(1, n - 1), part_of(where, rows), :],
                sems.at[len(copies)],
            )
        )
    return copies


def begin(copies):
    for copy in copies:
        copy.start()


def finish(copies):
    for copy in copies:
        copy.wait()


def shard_of(ids, k, n):
    return lax.rem(ids[PLACE] + n - k, n)


def project(n, ids, *refs):
    row_ref, wq, wk, wv = refs[:4]
    refs = refs[4:]
    pieces, (bias, out, compact, held, sems) = refs[:4], refs[4:]
    width = row_ref.shape[1]
    slots = row_ref.shape[0] // n
    cols = width // n
    rows = pieces[0].shape[3]
    copies = []
    for j, own in enumerate((wq, wk, wv)):
        copies.append(
            pltpu.make_async_copy(
                own.at[:, part_of(ids[PLACE] * cols, cols)],
                held.at[0, :, pl.ds(j * cols, cols)],
                sems.at[len(copies)],
            )
        )
        for i in range(2 * GROUP):
            where = ((ids[INDEX] ^ (i // 2)) * 2 + i % 2) * rows
            piece = piece_of(pieces, i // 2, i % 2)
            copies.append(
                pltpu.make_async_copy(
                    piece.at[:, :, part_of(j * width + ids[PLACE] * cols, cols)],
                    held.at[pl.ds(1, n - 1), part_of(where, rows), pl.ds(j * cols, cols)],
                    sems.at[len(copies)],
                )
            )
    begin(copies)
    for g in range(n):
        compact[part_of(ids[LISTS + g] * slots, slots), :] = row_ref[g * slots : (g + 1) * slots, :]
    finish(copies)

    def block(i, _):
        row = part_of(i * 256, 256)
        total = bias[...]
        for k in range(n):
            column = part_of(shard_of(ids, k, n) * cols, cols)
            total = total + dot(compact[row, column], held[k])
        out[row, :] = total.astype(LOW)
        return 0

    lax.fori_loop(0, out.shape[0] // 256, block, 0)


def attend(n, ids, bias_ref, q_ref, k_ref, v_ref, *refs):
    out_ref, lse_ref = refs
    tile = pl.program_id(0)
    slots = q_ref.shape[0]
    first = lax.broadcasted_iota(jnp.int32, (1, PAIR), 1) < HD

    def work(rows):
        query = q_ref[:rows, :]
        keys, values = k_ref[...], v_ref[...]
        mixed = []
        for h in range(2):
            mine = first if h == 0 else jnp.logical_not(first)
            scores = right_dot(jnp.where(mine, query, 0), keys)
            scores = scores * (LOG2E / math.sqrt(HD)) + bias_ref[...]
            high = jnp.max(scores, -1, keepdims=True)
            expo = jnp.exp2(scores - high)
            total = jnp.sum(expo, -1, keepdims=True)
            probs = (expo * (1.0 / total)).astype(LOW)
            mixed.append(dot(probs, values))
            lse = jnp.broadcast_to(high + jnp.log2(total), (rows, 128))
            lse_ref[h : h + 1, :rows] = lse.T[:1, :]
        out_ref[0, :rows, :] = jnp.where(first, mixed[0], mixed[1]).astype(LOW)
        if rows < slots:
            out_ref[0, rows:, :] = jnp.zeros((slots - rows, PAIR), LOW)

    @pl.when(tile < n - 1)
    def _():
        work(slots)

    @pl.when(tile == n - 1)
    def _():
        work(TAIL)
        lse_ref[:, TAIL:] = jnp.zeros((8, slots - TAIL), WIDE)


def attention(order, qkv, bias, pair, pairs, n, slots):
    span = qkv.shape[0]
    whole = lambda col: pl.BlockSpec((span, PAIR), lambda t, ids: (0, col))
    return order.call(
        functools.partial(attend, n),
        *(bias, qkv, qkv, qkv),
        grid_spec=pltpu.PrefetchScalarGridSpec(
            num_scalar_prefetch=1,
            grid=(n,),
            in_specs=[
                pl.BlockSpec((1, span), lambda t, ids: (0, 0)),
                pl.BlockSpec((slots, PAIR), lambda t, ids: (t, pair)),
                whole(pairs + pair),
                whole(2 * pairs + pair),
            ],
            out_specs=[
                pl.BlockSpec((1, slots, PAIR), lambda t, ids: (ids[LISTS + n + t], 0, 0)),
                pl.BlockSpec((8, slots), lambda t, ids: (0, t)),
            ],
        ),
        out_shape=[shape(n, slots, PAIR), shape(8, n * slots, dtype=WIDE)],
        compiler_params=params(),
        cost_estimate=cost(),
    )


def attend_back(n, ids, bias_ref, q_ref, k_ref, v_ref, *refs):
    grad_ref, lse_ref, out_ref, do_ref, dk_ref, dv_ref = refs
    tile = pl.program_id(0)
    slots = q_ref.shape[0]
    span = k_ref.shape[0]
    first = lax.broadcasted_iota(jnp.int32, (1, PAIR), 1) < HD
    scale = 1.0 / math.sqrt(HD)

    @pl.when(tile == 0)
    def _():
        dk_ref[...] = jnp.zeros_like(dk_ref)
        dv_ref[...] = jnp.zeros_like(dv_ref)
        for g in range(n):
            do_ref[part_of(ids[LISTS + g] * slots, slots), :] = grad_ref[g]

    def work(rows):
        keys, values = k_ref[...], v_ref[...]
        here = pl.ds(pl.multiple_of(tile * slots, slots), rows)
        parts = []
        for h in range(2):
            mine = first if h == 0 else jnp.logical_not(first)
            query = jnp.where(mine, q_ref[:rows, :], 0)
            grad = jnp.where(mine, do_ref[here, :], 0)
            scores = right_dot(keys, query) * (LOG2E * scale)
            bias = jnp.concatenate([bias_ref[...]] * (rows // 128), 1)
            probs = jnp.exp2(scores + bias - lse_ref[h : h + 1, :rows])
            grad_probs = right_dot(values, grad)
            center = jnp.sum(grad_probs * probs, 0, keepdims=True)
            grad_scores = (probs * (grad_probs - center)).astype(LOW)
            dk_ref[:span, :] += dot(grad_scores, query)
            dv_ref[:span, :] += dot(probs.astype(LOW), grad)
            parts.append(left_dot(grad_scores, keys))
        group = ids[LISTS + n + tile]
        out_ref[group, :rows, :PAIR] = (jnp.where(first, parts[0], parts[1]) * scale).astype(LOW)
        if rows < slots:
            out_ref[group, rows:, :PAIR] = jnp.zeros((slots - rows, PAIR), LOW)

    @pl.when(tile < n - 1)
    def _():
        work(slots)

    @pl.when(tile == n - 1)
    def _():
        work(TAIL)
        for g in range(n):
            here = part_of(ids[LISTS + g] * slots, slots)
            out_ref[g, :, PAIR : 2 * PAIR] = (dk_ref[here, :] * scale).astype(LOW)
            out_ref[g, :, 2 * PAIR :] = dv_ref[here, :].astype(LOW)


def attention_back(order, qkv, bias, grad, lse, pair, pairs, n, slots):
    span = qkv.shape[0]
    whole = lambda col: pl.BlockSpec((span, PAIR), lambda t, ids: (0, col))
    return order.call(
        functools.partial(attend_back, n),
        *(bias, qkv, qkv, qkv, grad, lse),
        grid_spec=pltpu.PrefetchScalarGridSpec(
            num_scalar_prefetch=1,
            grid=(n,),
            in_specs=[
                pl.BlockSpec((span, 128), lambda t, ids: (0, 0)),
                pl.BlockSpec((slots, PAIR), lambda t, ids: (t, pair)),
                whole(pairs + pair),
                whole(2 * pairs + pair),
                pl.BlockSpec((n, slots, PAIR), lambda t, ids: (0, 0, pair)),
                pl.BlockSpec((8, slots), lambda t, ids: (0, t)),
            ],
            out_specs=pl.BlockSpec((n, slots, 3 * PAIR), lambda t, ids: (0, 0, 0)),
            scratch_shapes=[
                pltpu.VMEM((n * slots, PAIR), LOW),
                pltpu.VMEM((n * slots, PAIR), WIDE),
                pltpu.VMEM((n * slots, PAIR), WIDE),
            ],
        ),
        out_shape=shape(n, slots, 3 * PAIR),
        compiler_params=params(),
        cost_estimate=cost(),
    )


def normal(values):
    center = values - jnp.mean(values, -1, keepdims=True)
    scale = lax.rsqrt(jnp.mean(center * center, -1, keepdims=True) + EPSILON)
    return center * scale, scale


def normal_back(grad, unit, scale):
    inner = jnp.mean(grad * unit, -1, keepdims=True)
    return (grad - jnp.mean(grad, -1, keepdims=True) - unit * inner) * scale


def wide(ref):
    return ref[...].astype(WIDE)


def forward(n, pairs, ids, *refs):
    parts, refs = refs[:pairs], refs[pairs:]
    start, cotangent, wo_own, wi_own, wu_own = refs[:5]
    bo, bi, bu, gain1, shift1, gain2, shift2 = refs[5:12]
    refs = refs[12:]
    side, tall, refs = refs[:4], refs[4:8], refs[8:]
    attn, first, normed_low, active, slope, out, grad_second, second_low, sums = refs[:9]
    wo, wi, wu, normed, second, sem_o, sem_i, sem_u = refs[9:]
    slots, width = start.shape
    cols = width // n
    hidden = active.shape[1]
    deep = hidden // n
    row_o, row_u = cols // (2 * GROUP), deep // (2 * GROUP)
    get_o = loads(ids, [(wo_own, width)], tall, sem_o, wo, row_o, 0, 0)
    get_i = loads(ids, [(wi_own, hidden)], side, sem_i, wi, row_o, 0, 3 * width)
    get_u = loads(ids, [(wu_own, width)], tall, sem_u, wu, row_u, row_o, 0)
    begin(get_o)
    begin(get_i)
    begin(get_u)
    for g in range(n):
        for p in range(pairs):
            attn[:, pl.ds(g * cols + p * PAIR, PAIR)] = parts[p][g]
    finish(get_o)

    def mix(j, _):
        column = part_of(j * STEP, STEP)
        total = start[:, column] + wide(bo.at[:, column])
        for k in range(n):
            left = attn[:, part_of(shard_of(ids, k, n) * cols, cols)]
            total = total + dot(left, wo[k, :, column])
        first[:, column] = total
        return 0

    lax.fori_loop(0, width // STEP, mix, 0)

    def norm(i, _):
        row = part_of(i * 128, 128)
        unit, _ = normal(first[row, :])
        value = unit * wide(gain1) + wide(shift1)
        normed[row, :] = value
        normed_low[row, :] = value.astype(LOW)
        return 0

    lax.fori_loop(0, slots // 128, norm, 0)
    finish(get_i)

    def expand(j, _):
        column = part_of(j * STEP, STEP)
        x = jnp.broadcast_to(wide(bi.at[:, column]), (slots, STEP))
        for k in range(n):
            left = normed_low[:, part_of(shard_of(ids, k, n) * cols, cols)]
            x = x + dot(left, wi[k, :, column])
        factor = math.sqrt(2 / math.pi)
        square = x * x
        t = jnp.tanh(factor * x * (1.0 + 0.044715 * square))
        half = 0.5 * (1.0 + t)
        active[:, column] = (x * half).astype(LOW)
        slope[:, column] = half + (0.5 * factor) * x * (1.0 - t * t) * (1.0 + 0.134145 * square)
        return 0

    lax.fori_loop(0, hidden // STEP, expand, 0)
    finish(get_u)

    def contract(j, _):
        column = part_of(j * STEP, STEP)
        total = normed[:, column] + wide(bu.at[:, column])
        for k in range(n):
            left = active[:, part_of(shard_of(ids, k, n) * deep, deep)]
            total = total + dot(left, wu[k, :, column])
        second[:, column] = total
        return 0

    lax.fori_loop(0, width // STEP, contract, 0)
    sums[...] = jnp.zeros_like(sums)

    def last(i, _):
        row = part_of(i * 128, 128)
        live = lax.broadcasted_iota(jnp.int32, (128, 1), 0) + i * 128 < ids[OWNED]
        live = live.astype(WIDE)
        unit, scale = normal(second[row, :])
        out[row, :] = ((unit * wide(gain2) + wide(shift2)) * live).astype(LOW)
        grad = cotangent[row, :].astype(WIDE) * live
        result = normal_back(grad * wide(gain2), unit, scale)
        grad_second[row, :] = result
        second_low[row, :] = result.astype(LOW)
        for j, item in enumerate((grad * unit, grad, result)):
            sums[j : j + 1, :] += jnp.sum(item, 0, keepdims=True)
        return 0

    lax.fori_loop(0, slots // 128, last, 0)


def backward_inner(n, ids, *refs):
    second_low, slope, wu_own = refs[:3]
    tall, (inner_low, bias_sum, wu, sem_u) = refs[3:7], refs[7:]
    hidden = slope.shape[1]
    deep, cols = hidden // n, second_low.shape[1] // n
    row_o, row_u = cols // (2 * GROUP), deep // (2 * GROUP)
    get_u = loads(ids, [(wu_own, second_low.shape[1])], tall, sem_u, wu, row_u, row_o, 0)
    begin(get_u)
    finish(get_u)

    def expand(j, _):
        for k in range(n):
            column = part_of(shard_of(ids, k, n) * deep + j * STEP, STEP)
            grad = right_dot(second_low[...], wu[k, part_of(j * STEP, STEP), :])
            value = (grad * slope[:, column]).astype(LOW)
            inner_low[:, column] = value
            bias_sum[:, column] = jnp.sum(value.astype(WIDE), 0, keepdims=True)
        return 0

    lax.fori_loop(0, deep // STEP, expand, 0)


def backward(n, ids, *refs):
    inner_low, bias_sum, grad_second, first, gain1, sums, wo_own, wi_own = refs[:8]
    side, tall, refs = refs[8:12], refs[12:16], refs[16:]
    grad_first, first_low = refs[:2]
    grad_attn, small = refs[2:4]
    wo, wi, grad_normed, more, sem_o, sem_i = refs[4:]
    slots, width = first.shape
    cols = width // n
    hidden = inner_low.shape[1]
    deep = hidden // n
    row_o = cols // (2 * GROUP)
    get_o = loads(ids, [(wo_own, width)], tall, sem_o, wo, row_o, 0, 0)
    get_i = loads(ids, [(wi_own, hidden)], side, sem_i, wi, row_o, 0, 3 * width)
    begin(get_i)
    begin(get_o)
    finish(get_i)
    for k in range(n):
        column = part_of(shard_of(ids, k, n) * cols, cols)
        grad_normed[:, column] = right_dot(inner_low[...], wi[k]) + grad_second[:, column]
    more[...] = jnp.zeros_like(more)

    def norm(i, _):
        row = part_of(i * 128, 128)
        unit, scale = normal(first[row, :])
        grad = grad_normed[row, :]
        result = normal_back(grad * wide(gain1), unit, scale)
        grad_first[row, :] = result
        first_low[row, :] = result.astype(LOW)
        for j, item in enumerate((result, grad * unit, grad)):
            more[j : j + 1, :] += jnp.sum(item, 0, keepdims=True)
        return 0

    lax.fori_loop(0, slots // 128, norm, 0)
    finish(get_o)
    for k in range(n):
        grad_attn[shard_of(ids, k, n)] = right_dot(first_low[...], wo[k]).astype(LOW)
    small[...] = jnp.zeros_like(small)
    for z in range(n):
        here = pl.ds(z * cols, cols)
        rows = [more[0:1, here]]
        rows += [bias_sum[:, pl.ds(z * deep + j * cols, cols)] for j in range(deep // cols)]
        rows += [sums[2:3, here], more[1:2, here], more[2:3, here], sums[0:1, here], sums[1:2, here]]
        for j, item in enumerate(rows):
            small[z, j : j + 1, :] = item


def finish_hidden(n, pairs, ids, *refs):
    parts, refs = refs[:pairs], refs[pairs:]
    grad_first, wq, wk, wv = refs[:4]
    side, (out, total, held, acts, sems) = refs[4:8], refs[8:]
    slots, width = out.shape
    cols = width // n
    copies = loads(
        ids, [(wq, width), (wk, width), (wv, width)], side, sems, held, cols // (2 * GROUP), 0, 0
    )
    begin(copies)
    for g in range(n):
        for p in range(pairs):
            for j in range(3):
                column = j * width + g * cols + p * PAIR
                acts[:, column : column + PAIR] = parts[p][g, :, j * PAIR : (j + 1) * PAIR]
    finish(copies)
    for k in range(n):
        column = part_of(shard_of(ids, k, n) * cols, cols)
        out[:, column] = right_dot(acts[...], held[k]) + grad_first[:, column]
    block = lax.broadcasted_iota(jnp.int32, (32, 1), 0) < ids[HERE]
    total[...] = jnp.sum(jnp.where(block, out[:32, :], 0.0), 0, keepdims=True)


def outer_product(spec, keep, ids, *refs):
    lefts, rights = [], []
    for count, _ in spec:
        lefts.append(refs[:count])
        rights.append(refs[count : 2 * count])
        refs = refs[2 * count :]
    at = 0
    for (count, cols), left, right in zip(spec, lefts, rights):
        step = min(cols, 1024)
        for col in range(0, cols, step):
            total = left_dot(left[0][...], right[0][:, col : col + step])
            for i in range(1, count):
                total = total + left_dot(left[i][...], right[i][:, col : col + step])
            here = slice(at + col, at + col + step)
            if not keep:
                refs[0][0, :, here] = total.astype(LOW)
                continue
            got, outs = refs[0], refs[1:]
            total = (total + got[0, :, here].astype(WIDE)).astype(LOW)
            split_halves(ids, total, [out.at[0, :, here] for out in outs], (X, Y))
        at += cols


def split_halves(ids, total, outs, bits):
    rows = total.shape[0] // 4
    parts = [total[i * rows : (i + 1) * rows] for i in range(4)]
    for half, bit in enumerate(bits):
        high = ids[bit] == 1
        low_part, high_part = parts[2 * half], parts[2 * half + 1]
        outs[2 * half][...] = jnp.where(high, low_part, high_part)
        outs[2 * half + 1][...] = jnp.where(high, high_part, low_part)


def gradient(order, spec, n, got=None):
    rows = spec[0][0][0][0].shape[1] // (2 * n)
    keep = got is not None
    in_specs, args, total, flops = [], [], 0, 0
    for pairs, cols in spec:
        for left, _ in pairs:
            block = lambda z, ids: (0, 2 * z + (ids[CORE] if keep else 1 - ids[CORE]))
            in_specs.append(pl.BlockSpec((left.shape[0], rows), block))
            args.append(left)
        for _, right in pairs:
            in_specs.append(pl.BlockSpec(right.shape, lambda z, ids: (0, 0)))
            args.append(right)
            flops += 2 * n * rows * right.shape[0] * cols
        total += cols
    if keep:
        in_specs.append(pl.BlockSpec((1, rows, total), lambda z, ids: (z, 0, 0)))
        args.append(got)
    out_rows, count = (rows // 4, 4) if keep else (rows, 1)
    return order.call(
        functools.partial(outer_product, [(len(pairs), cols) for pairs, cols in spec], keep),
        *args,
        grid_spec=pltpu.PrefetchScalarGridSpec(
            num_scalar_prefetch=1,
            grid=(n,),
            in_specs=in_specs,
            out_specs=[pl.BlockSpec((1, out_rows, total), lambda z, ids: (z, 0, 0))] * count,
        ),
        out_shape=[shape(n, out_rows, total)] * count,
        compiler_params=params(),
        cost_estimate=cost(),
    )


def fold_two(ids, keep_one, got_one, keep_two, got_two, *outs):
    rows = keep_one.shape[1] // 2
    for z in range(keep_one.shape[0]):
        one = (keep_one[z].astype(WIDE) + got_one[z].astype(WIDE)).astype(LOW)
        two = (keep_two[z].astype(WIDE) + got_two[z].astype(WIDE)).astype(LOW)
        for total, bit, (send, keep) in ((one, Y, outs[:2]), (two, X, outs[2:])):
            high = ids[bit] == 1
            send[z] = jnp.where(high, total[:rows], total[rows:])
            keep[z] = jnp.where(high, total[rows:], total[:rows])


def fold_three(ids, keep_one, got_one, keep_two, got_two, out):
    for z in range(out.shape[0]):
        out[z, 0] = (keep_one[z].astype(WIDE) + got_one[z].astype(WIDE)).astype(LOW)
        out[z, 1] = (keep_two[z].astype(WIDE) + got_two[z].astype(WIDE)).astype(LOW)


def fold_four(split, ids, terms, *outs):
    n, cols = terms.shape[0], terms.shape[3]
    for h, out in enumerate(outs):
        if split < cols:
            total = terms[0, h, :, split:].astype(WIDE)
            for z in range(1, n):
                total = total + terms[z, h, :, split:].astype(WIDE)
            out[:, n * split :] = total.astype(LOW)
        for z in range(n if split else 0):
            out[:, z * split : (z + 1) * split] = terms[z, h, :, :split]


def small_call(order, body, args, outs):
    return order.call(
        body,
        *args,
        in_specs=[SMEM] + [VMEM] * len(args),
        out_specs=[VMEM] * len(outs),
        out_shape=outs,
        compiler_params=params(),
        cost_estimate=cost(),
    )


def reduce_first(order, spec, n):
    (send,) = gradient(order, spec, n)
    return swap(send, 1)


def reduce_second(order, spec, n, got):
    send_one, keep_one, send_two, keep_two = gradient(order, spec, n, got)
    return keep_one, swap(send_one, 2), keep_two, swap(send_two, 4)


def reduce_third(order, n, held):
    rows, cols = held[0].shape[1:]
    outs = [shape(n, rows // 2, cols)] * 4
    send_one, keep_one, send_two, keep_two = small_call(order, fold_two, held, outs)
    return keep_one, swap(send_one, 4), keep_two, swap(send_two, 2)


def reduce_fourth(order, n, held):
    rows, cols = held[0].shape[1:]
    (out,) = small_call(order, fold_three, held, [shape(n, 2, rows, cols)])
    return exchange(out)


def reduce_fifth(order, held, split=0):
    n, _, rows, cols = held.shape
    outs = [shape(rows, cols + (n - 1) * split)] * 2
    one, two = small_call(order, functools.partial(fold_four, split), [held], outs)
    mask = GROUP
    while mask < lax.axis_size("dp"):
        one, two = [(v.astype(WIDE) + swap(v, mask).astype(WIDE)).astype(LOW) for v in (one, two)]
        mask *= 2
    return one, two


def place_grad(plan, ids, *refs):
    pieces, outs = refs[:4], refs[4:]
    rows = pieces[0].shape[2]
    for i in range(2 * GROUP):
        piece = piece_of(pieces, i // 2, i % 2)
        home = ids[INDEX] ^ (i // 2)
        core, x, y = home & 1, (home >> 1) & 1, (home >> 2) & 1
        block = core * 8 + (x * 2 + y if i % 2 == 0 else 4 + y * 2 + x)
        row = part_of(block * rows, rows)
        for out, moves in zip(outs, plan):
            for source, target, size in moves:
                out[row, target : target + size] = piece[:, source : source + size].astype(WIDE)


def reduce_last(order, pieces, plan, widths):
    rows = pieces[0].shape[2] * 2 * GROUP
    return small_call(
        order,
        functools.partial(place_grad, plan),
        pieces,
        [shape(rows, width, dtype=WIDE) for width in widths],
    )


def per_device(
    hidden_in,
    cotangent,
    context_len,
    block_device,
    timestep,
    query_weight,
    key_weight,
    value_weight,
    output_weight,
    inner_weight,
    outer_weight,
    query_bias,
    value_bias,
    output_bias,
    inner_bias,
    outer_bias,
    attn_gain,
    attn_shift,
    ffn_gain,
    ffn_shift,
    time_table,
):
    n = lax.axis_size("ctx")
    place = lax.axis_index("ctx")
    d = lax.axis_index("dp") % GROUP
    _, slots, width = hidden_in.shape
    hidden = inner_weight.shape[1]
    cols = width // n
    deep = hidden // n
    pairs = cols // PAIR
    span = (n - 1) * slots + TAIL
    holder = block_device[0]
    context = context_len[0]

    groups = [j + (j >= holder).astype(jnp.int32) for j in range(n - 1)] + [holder]
    position = lambda g: jnp.where(g == holder, n - 1, g - (g > holder).astype(jnp.int32))
    counts = [context // (n - 1) + (j < context % (n - 1)).astype(jnp.int32) for j in range(n - 1)]
    counts = jnp.stack(counts + [jnp.int32(BLOCK)])
    slot = jnp.arange(slots, dtype=jnp.int32)
    live = (slot[None, :] < counts[:, None]).reshape(n * slots)[:span]
    bias = jnp.where(live, 0.0, -1e30).astype(WIDE)
    bias_row, bias_col = bias[None, :], jnp.broadcast_to(bias[:, None], (span, 128))
    owned = lax.dynamic_index_in_dim(counts, position(place), keepdims=False)
    here = jnp.where(holder == place, BLOCK, 0)
    ids = [place, d, d & 1, (d >> 1) & 1, (d >> 2) & 1, owned, here]
    ids += [position(jnp.int32(g)) for g in range(n)] + groups
    order = Order(jnp.stack([jnp.asarray(v, jnp.int32) for v in ids]))
    embed = lax.dynamic_slice_in_dim(time_table, timestep[0], 1, 0).astype(WIDE)
    block = ((holder == place) & (slot < BLOCK)).astype(WIDE)[:, None]
    start = hidden_in[0].astype(WIDE) + block * embed
    start_low = start.astype(LOW)

    def piece(weight):
        part = weight.shape[0] // GROUP
        return lax.dynamic_slice_in_dim(weight, d * part, part, 0).reshape(2, part // 2, -1)

    side_piece = jnp.concatenate(
        [piece(w) for w in (query_weight, key_weight, value_weight, inner_weight)], 2
    )
    tall_piece = jnp.concatenate([piece(output_weight), piece(outer_weight)], 1)
    side, early = shard_gather(side_piece)
    tall, late = shard_gather(tall_piece, early)
    row_low = lax.all_gather(after(start_low, late), "ctx", tiled=True)
    side, tall = jnp.stack(side), jnp.stack(tall)
    side = gather_cores(*gather_far(*gather_near(side[:, 0], side[:, 1])))
    tall = gather_near(tall[:, 0], tall[:, 1])
    order.wait(*tall)
    tall = gather_far(*tall)
    own_bias = lambda v: lax.dynamic_slice_in_dim(v, place * cols, cols, 0).astype(WIDE)
    qkv_bias = jnp.concatenate([own_bias(query_bias), jnp.zeros((cols,), WIDE), own_bias(value_bias)])
    qkv = order.call(
        functools.partial(project, n),
        *(row_low, query_weight, key_weight, value_weight, *side, qkv_bias[None]),
        in_specs=[SMEM] + [VMEM] + [ANY] * 7 + [VMEM],
        out_specs=VMEM,
        out_shape=shape(span, 3 * cols),
        scratch_shapes=[
            pltpu.VMEM((n * slots, width), LOW),
            pltpu.VMEM((n, cols, 3 * cols), LOW),
            pltpu.SemaphoreType.DMA((3 + 6 * GROUP,)),
        ],
        compiler_params=params(),
        cost_estimate=cost(),
    )

    mixed, lses = [], []
    for pair in range(pairs):
        if pair == 1:
            order.wait(*tall)
            tall = gather_cores(*tall)
        mix, lse = attention(order, qkv, bias_row, pair, pairs, n, slots)
        lses.append(lse)
        mixed.append(exchange(mix))

    row = lambda v: v[None, :]
    held_o = pltpu.VMEM((n, cols, width), LOW)
    held_i = pltpu.VMEM((n, cols, hidden), LOW)
    held_u = pltpu.VMEM((n, deep, width), LOW)
    wide_one = pltpu.VMEM((slots, width), WIDE)
    sem = pltpu.SemaphoreType.DMA((1 + 2 * GROUP,))
    flops = 2 * slots * width * (width + 2 * hidden)
    attn, first, normed_low, active, slope, out, grad_second, second_low, sums = order.call(
        functools.partial(forward, n, pairs),
        *(*mixed, start, cotangent[0], output_weight, inner_weight, outer_weight),
        *(row(output_bias), row(inner_bias), row(outer_bias)),
        *(row(attn_gain), row(attn_shift), row(ffn_gain), row(ffn_shift), *side, *tall),
        in_specs=[SMEM] + [VMEM] * (pairs + 2) + [ANY] * 3 + [VMEM] * 7 + [ANY] * 8,
        out_specs=[VMEM] * 9,
        out_shape=[
            shape(slots, width),
            shape(slots, width, dtype=WIDE),
            shape(slots, width),
            shape(slots, hidden),
            shape(slots, hidden, dtype=WIDE),
            shape(slots, width),
            shape(slots, width, dtype=WIDE),
            shape(slots, width),
            shape(8, width, dtype=WIDE),
        ],
        scratch_shapes=[held_o, held_i, held_u, wide_one, wide_one, sem, sem, sem],
        compiler_params=params(),
        cost_estimate=cost(),
    )
    outer_spec = [([(active, second_low)], width)]
    outer_held = reduce_first(order, outer_spec, n)
    inner_low, bias_sum = order.call(
        functools.partial(backward_inner, n),
        *(second_low, slope, outer_weight, *tall),
        in_specs=[SMEM] + [VMEM] * 2 + [ANY] * 5,
        out_specs=[VMEM] * 2,
        out_shape=[shape(slots, hidden), shape(1, hidden, dtype=WIDE)],
        scratch_shapes=[held_u, sem],
        compiler_params=params(),
        cost_estimate=cost(),
    )
    outer_held = reduce_second(order, outer_spec, n, outer_held)
    inner_spec = [([(normed_low, inner_low)], hidden)]
    inner_held = reduce_first(order, inner_spec, n)
    grad_first, first_low, grad_attn, small = order.call(
        functools.partial(backward, n),
        *(inner_low, bias_sum, grad_second, first, row(attn_gain), sums),
        *(output_weight, inner_weight, *side, *tall),
        in_specs=[SMEM] + [VMEM] * 6 + [ANY] * 10,
        out_specs=[VMEM] * 4,
        out_shape=[
            shape(slots, width, dtype=WIDE),
            shape(slots, width),
            shape(n, slots, cols),
            shape(n, 16, cols, dtype=WIDE),
        ],
        scratch_shapes=[held_o, held_i, wide_one, pltpu.VMEM((8, width), WIDE), sem, sem],
        compiler_params=params(),
        cost_estimate=cost(),
    )
    grad_mixed = exchange(grad_attn)
    outer_held = reduce_third(order, n, outer_held)
    inner_held = reduce_second(order, inner_spec, n, inner_held)
    order.wait(grad_mixed)
    outer_held = reduce_fourth(order, n, outer_held)

    backs, received = [], []

    def head_pair(pair):
        back = attention_back(order, qkv, bias_col, grad_mixed, lses[pair], pair, pairs, n, slots)
        backs.append(back)
        received.append(exchange(back))

    head_pair(0)
    order.wait(outer_held)
    inner_held = reduce_third(order, n, inner_held)
    for pair in range(1, pairs):
        head_pair(pair)
        order.wait(received[-2], *inner_held)
    outer_pieces = gather_near(*reduce_fifth(order, outer_held))
    rest_spec = [([(row_low, back.reshape(n * slots, -1))], 3 * PAIR) for back in backs]
    rest_spec += [([(attn, first_low)], width)]
    rest_held = reduce_first(order, rest_spec, n)
    order.wait(*outer_pieces)
    rest_held = reduce_second(order, rest_spec, n, rest_held)
    order.wait(*received)
    inner_held = reduce_fourth(order, n, inner_held)
    grad_hidden, block_sum = order.call(
        functools.partial(finish_hidden, n, pairs),
        *(*received, grad_first, query_weight, key_weight, value_weight, *side),
        in_specs=[SMEM] + [VMEM] * (pairs + 1) + [ANY] * 7,
        out_specs=[VMEM] * 2,
        out_shape=[shape(slots, width, dtype=WIDE), shape(1, width, dtype=WIDE)],
        scratch_shapes=[
            pltpu.VMEM((n, cols, 3 * width), LOW),
            pltpu.VMEM((slots, 3 * width), LOW),
            pltpu.SemaphoreType.DMA((3 + 2 * GROUP,)),
        ],
        compiler_params=params(),
        cost_estimate=cost(),
    )
    rest_held = reduce_third(order, n, rest_held)
    order.wait(*rest_held)
    outer_pieces = gather_far(*outer_pieces)
    order.wait(*outer_pieces)
    outer_pieces = gather_cores(*outer_pieces)
    order.wait(inner_held)

    packed = jnp.concatenate([small, block_sum.reshape(1, n, cols).repeat(n, 0)], 1)
    total = jnp.sum(exchange(after(packed, inner_held)), 0)
    order.wait(total)
    used = small.shape[1]
    bias_sums = jnp.stack([jnp.sum(back.astype(WIDE), (0, 1)) for back in backs])
    vector = jnp.concatenate([total[used:], jnp.full((1, cols), timestep[0], WIDE)])[None]
    total = jnp.concatenate([total[:used], bias_sums.reshape(-1, cols)])
    mask = 1
    while mask < lax.axis_size("dp"):
        flat = jnp.concatenate([total, vector.reshape(-1, cols)])
        flat = swap(flat, mask)
        total = total + flat[: total.shape[0]]
        vector = jnp.concatenate([vector, flat[total.shape[0] :].reshape(vector.shape)])
        mask *= 2
    per = deep // cols
    sums = [total[0], total[1 : 1 + per].reshape(deep)] + [total[1 + per + i] for i in range(5)]
    bias_sums = total[used:].reshape(pairs, 3 * PAIR)
    query_sum = bias_sums[:, :PAIR].reshape(cols)
    value_sum = bias_sums[:, 2 * PAIR :].reshape(cols)
    share = time_table.shape[0] // n
    levels = (jnp.arange(share, dtype=jnp.int32) + place * share).astype(WIDE)
    onehot = (vector[:, n, :1] == levels[None, :]).astype(WIDE)
    time_table_grad = lax.dot_general(
        onehot,
        vector[:, :n].reshape(-1, width),
        (((0,), (0,)), ((), ())),
        precision=lax.Precision.HIGHEST,
        preferred_element_type=WIDE,
    )

    inner_pieces = gather_near(*reduce_fifth(order, inner_held))
    rest_held = reduce_fourth(order, n, rest_held)
    order.wait(*inner_pieces)
    inner_pieces = gather_far(*inner_pieces)
    (outer_grad,) = reduce_last(order, outer_pieces, [[(0, 0, width)]], [width])
    rest_pieces = gather_near(*reduce_fifth(order, rest_held, 3 * cols))
    order.wait(*inner_pieces)
    inner_pieces = gather_cores(*inner_pieces)
    order.wait(*rest_pieces)
    rest_pieces = gather_far(*rest_pieces)
    (inner_grad,) = reduce_last(order, inner_pieces, [[(0, 0, hidden)]], [hidden])
    rest_pieces = gather_cores(*rest_pieces)
    plan = [
        [
            (g * 3 * cols + p * 3 * PAIR + j * PAIR, g * cols + p * PAIR, PAIR)
            for g in range(n)
            for p in range(pairs)
        ]
        for j in range(3)
    ]
    plan += [[(n * 3 * cols, 0, width)]]
    *weight_grads, output_grad = reduce_last(order, rest_pieces, plan, [width] * 4)
    return (
        out[None],
        grad_hidden[None],
        *weight_grads,
        output_grad,
        inner_grad,
        outer_grad,
        query_sum,
        value_sum,
        *sums,
        time_table_grad,
    )


def solution(mesh):
    row, shard, same = P("dp", "ctx", None), P("ctx", None), P()
    return jax.shard_map(
        per_device,
        mesh=mesh,
        in_specs=(row, row, P("dp"), P("dp"), P("dp")) + (shard,) * 6 + (same,) * 10,
        out_specs=(row, row) + (shard,) * 6 + (P("ctx"),) * 9 + (shard,),
        check_vma=False,
    )
```

```python
import functools
import math

import jax
import jax.numpy as jnp
from jax import lax
from jax.experimental import pallas as pl
from jax.experimental.pallas import tpu as pltpu
from jax.sharding import PartitionSpec as P

HEADS = 16
HD = 64
BLOCK = 25
EPSILON = 1e-05
GROUP = 8
TAIL = 128
PAIR = 2 * HD
STEP = 512
FACTOR = 16
LOG2E = 1.4426950408889634
LOW = jnp.bfloat16
WIDE = jnp.float32
VMEM = pl.BlockSpec(memory_space=pltpu.VMEM)
SMEM = pl.BlockSpec(memory_space=pltpu.SMEM)
ANY = pl.BlockSpec(memory_space=pl.ANY)
PLACE, INDEX, CORE, X, Y, OWNED, HERE, LISTS = range(8)


def params(mib=56):
    return pltpu.CompilerParams(vmem_limit_bytes=mib << 20)


def cost(us):
    us = us * FACTOR
    return pl.CostEstimate(flops=int(us * 1e9), bytes_accessed=int(us * 3e6), transcendentals=0)


def shape(*dims, dtype=LOW):
    return jax.ShapeDtypeStruct(dims, dtype)


def dot(left, right, dims=((1,), (0,))):
    return lax.dot_general(left, right, (dims, ((), ())), preferred_element_type=WIDE)


def left_dot(left, right):
    return dot(left, right, ((0,), (0,)))


def right_dot(left, right):
    return dot(left, right, ((1,), (1,)))


def part_of(start, size):
    return pl.ds(pl.multiple_of(start, size), size)


def swap(value, mask):
    size = lax.axis_size("dp")
    return lax.ppermute(value, "dp", [(i, i ^ mask) for i in range(size)])


def along(value, *pairs):
    return lax.ppermute(value, "ctx", pairs)


def exchange(value, axis="ctx"):
    return lax.all_to_all(value, axis, 0, 0)


def after(value, *others):
    return lax.optimization_barrier((value, *others))[0]


def two_off(value):
    return along(value, (0, 2), (1, 3), (2, 0), (3, 1))


def one_off(value):
    return along(value, (0, 1), (1, 2), (2, 3)), along(value, (1, 0), (2, 1), (3, 2))


def sent_on(far):
    return along(far, (2, 3), (1, 0))


def by_distance(far, up, down, on):
    place = lax.axis_index("ctx")
    return jnp.stack([jnp.where(place == 0, on, up), far, jnp.where(place == 3, on, down)])


def copy_numbers(ids, out):
    for i in range(ids.shape[0]):
        out[i] = ids[i]


class Order:
    def __init__(self, ids):
        self.ids = ids

    def call(self, body, *args, **kwargs):
        outs = pl.pallas_call(body, **kwargs)(self.ids, *args)
        self.wait(outs[0] if isinstance(outs, (list, tuple)) else outs)
        return outs

    def wait(self, *values):
        self.ids = after(self.ids, *values)

    def tick(self, *values):
        self.wait(*values)
        self.call(
            copy_numbers,
            in_specs=[SMEM],
            out_specs=SMEM,
            out_shape=jax.ShapeDtypeStruct(self.ids.shape, jnp.int32),
            cost_estimate=cost(0),
        )

    def release(self, *values):
        outs = lax.optimization_barrier((*values, self.ids))[:-1]
        return outs if len(outs) > 1 else outs[0]


def gather_near(one, two):
    return jnp.stack([one, swap(one, 2)]), jnp.stack([two, swap(two, 4)])


def gather_far(one, two):
    return jnp.stack([one, swap(one, 4)]), jnp.stack([two, swap(two, 2)])


def gather_cores(one, two):
    return one, two, swap(one, 1), swap(two, 1)


def piece_of(arrays, mask, half):
    x, y = (mask >> 1) & 1, (mask >> 2) & 1
    return arrays[2 * (mask & 1) + half].at[(x, y) if half else (y, x)]


def loads(ids, own, pieces, sems, held, rows, row, col):
    n, _, cols = held.shape
    copies = []
    at = 0
    for ref, width in own:
        copies.append(
            pltpu.make_async_copy(ref, held.at[0, :, pl.ds(at, width)], sems.at[len(copies)])
        )
        at += width
    for i in range(2 * GROUP):
        where = ((ids[INDEX] ^ (i // 2)) * 2 + i % 2) * rows
        piece = piece_of(pieces, i // 2, i % 2)
        copies.append(
            pltpu.make_async_copy(
                piece.at[:, pl.ds(row, rows), pl.ds(col, cols)],
                held.at[pl.ds(1, n - 1), part_of(where, rows), :],
                sems.at[len(copies)],
            )
        )
    return copies


def begin(copies):
    for copy in copies:
        copy.start()


def finish(copies):
    for copy in copies:
        copy.wait()


def shard_of(ids, k, n):
    return lax.rem(ids[PLACE] + n - k, n)


def project(n, ids, *refs):
    row_ref, wq, wk, wv = refs[:4]
    refs = refs[4:]
    pieces, (bias, out, compact, held, sems) = refs[:4], refs[4:]
    width = row_ref.shape[1]
    slots = row_ref.shape[0] // n
    cols = width // n
    rows = pieces[0].shape[3]
    copies = []
    for j, own in enumerate((wq, wk, wv)):
        copies.append(
            pltpu.make_async_copy(
                own.at[:, part_of(ids[PLACE] * cols, cols)],
                held.at[0, :, pl.ds(j * cols, cols)],
                sems.at[len(copies)],
            )
        )
        for i in range(2 * GROUP):
            where = ((ids[INDEX] ^ (i // 2)) * 2 + i % 2) * rows
            piece = piece_of(pieces, i // 2, i % 2)
            copies.append(
                pltpu.make_async_copy(
                    piece.at[:, :, part_of(j * width + ids[PLACE] * cols, cols)],
                    held.at[pl.ds(1, n - 1), part_of(where, rows), pl.ds(j * cols, cols)],
                    sems.at[len(copies)],
                )
            )
    begin(copies)
    for g in range(n):
        compact[part_of(ids[LISTS + g] * slots, slots), :] = row_ref[g * slots : (g + 1) * slots, :]
    finish(copies)

    def block(i, _):
        row = part_of(i * 256, 256)
        total = bias[...]
        for k in range(n):
            column = part_of(shard_of(ids, k, n) * cols, cols)
            total = total + dot(compact[row, column], held[k])
        out[row, :] = total.astype(LOW)
        return 0

    lax.fori_loop(0, out.shape[0] // 256, block, 0)


def attend(n, ids, bias_ref, q_ref, k_ref, v_ref, *refs):
    out_ref, lse_ref = refs
    tile = pl.program_id(0)
    slots = q_ref.shape[0]
    first = lax.broadcasted_iota(jnp.int32, (1, PAIR), 1) < HD

    def work(rows):
        query = q_ref[:rows, :]
        keys, values = k_ref[...], v_ref[...]
        mixed = []
        for h in range(2):
            mine = first if h == 0 else jnp.logical_not(first)
            scores = right_dot(jnp.where(mine, query, 0), keys)
            scores = scores * (LOG2E / math.sqrt(HD)) + bias_ref[...]
            high = jnp.max(scores, -1, keepdims=True)
            expo = jnp.exp2(scores - high)
            total = jnp.sum(expo, -1, keepdims=True)
            probs = (expo * (1.0 / total)).astype(LOW)
            mixed.append(dot(probs, values))
            lse = jnp.broadcast_to(high + jnp.log2(total), (rows, 128))
            lse_ref[h : h + 1, :rows] = lse.T[:1, :]
        out_ref[0, :rows, :] = jnp.where(first, mixed[0], mixed[1]).astype(LOW)
        if rows < slots:
            out_ref[0, rows:, :] = jnp.zeros((slots - rows, PAIR), LOW)

    @pl.when(tile < n - 1)
    def _():
        work(slots)

    @pl.when(tile == n - 1)
    def _():
        work(TAIL)
        lse_ref[:, TAIL:] = jnp.zeros((8, slots - TAIL), WIDE)


def attention(order, qkv, bias, pair, pairs, n, slots):
    span = qkv.shape[0]
    whole = lambda col: pl.BlockSpec((span, PAIR), lambda t, ids: (0, col))
    return order.call(
        functools.partial(attend, n),
        *(bias, qkv, qkv, qkv),
        grid_spec=pltpu.PrefetchScalarGridSpec(
            num_scalar_prefetch=1,
            grid=(n,),
            in_specs=[
                pl.BlockSpec((1, span), lambda t, ids: (0, 0)),
                pl.BlockSpec((slots, PAIR), lambda t, ids: (t, pair)),
                whole(pairs + pair),
                whole(2 * pairs + pair),
            ],
            out_specs=[
                pl.BlockSpec((1, slots, PAIR), lambda t, ids: (ids[LISTS + n + t], 0, 0)),
                pl.BlockSpec((8, slots), lambda t, ids: (0, t)),
            ],
        ),
        out_shape=[shape(n, slots, PAIR), shape(8, n * slots, dtype=WIDE)],
        compiler_params=params(),
        cost_estimate=cost(11),
    )


def attend_back(n, ids, bias_ref, q_ref, k_ref, v_ref, *refs):
    grad_ref, lse_ref, out_ref, do_ref, dk_ref, dv_ref = refs
    tile = pl.program_id(0)
    slots = q_ref.shape[0]
    span = k_ref.shape[0]
    first = lax.broadcasted_iota(jnp.int32, (1, PAIR), 1) < HD
    scale = 1.0 / math.sqrt(HD)

    @pl.when(tile == 0)
    def _():
        dk_ref[...] = jnp.zeros_like(dk_ref)
        dv_ref[...] = jnp.zeros_like(dv_ref)
        for g in range(n):
            do_ref[part_of(ids[LISTS + g] * slots, slots), :] = grad_ref[g]

    def work(rows):
        keys, values = k_ref[...], v_ref[...]
        here = pl.ds(pl.multiple_of(tile * slots, slots), rows)
        parts = []
        for h in range(2):
            mine = first if h == 0 else jnp.logical_not(first)
            query = jnp.where(mine, q_ref[:rows, :], 0)
            grad = jnp.where(mine, do_ref[here, :], 0)
            scores = right_dot(keys, query) * (LOG2E * scale)
            bias = jnp.concatenate([bias_ref[...]] * (rows // 128), 1)
            probs = jnp.exp2(scores + bias - lse_ref[h : h + 1, :rows])
            grad_probs = right_dot(values, grad)
            center = jnp.sum(grad_probs * probs, 0, keepdims=True)
            grad_scores = (probs * (grad_probs - center)).astype(LOW)
            dk_ref[:span, :] += dot(grad_scores, query)
            dv_ref[:span, :] += dot(probs.astype(LOW), grad)
            parts.append(left_dot(grad_scores, keys))
        group = ids[LISTS + n + tile]
        out_ref[group, :rows, :PAIR] = (jnp.where(first, parts[0], parts[1]) * scale).astype(LOW)
        if rows < slots:
            out_ref[group, rows:, :PAIR] = jnp.zeros((slots - rows, PAIR), LOW)

    @pl.when(tile < n - 1)
    def _():
        work(slots)

    @pl.when(tile == n - 1)
    def _():
        work(TAIL)
        for g in range(n):
            here = part_of(ids[LISTS + g] * slots, slots)
            out_ref[g, :, PAIR : 2 * PAIR] = (dk_ref[here, :] * scale).astype(LOW)
            out_ref[g, :, 2 * PAIR :] = dv_ref[here, :].astype(LOW)


def attention_back(order, qkv, bias, grad, lse, pair, pairs, n, slots):
    span = qkv.shape[0]
    whole = lambda col: pl.BlockSpec((span, PAIR), lambda t, ids: (0, col))
    return order.call(
        functools.partial(attend_back, n),
        *(bias, qkv, qkv, qkv, grad, lse),
        grid_spec=pltpu.PrefetchScalarGridSpec(
            num_scalar_prefetch=1,
            grid=(n,),
            in_specs=[
                pl.BlockSpec((span, 128), lambda t, ids: (0, 0)),
                pl.BlockSpec((slots, PAIR), lambda t, ids: (t, pair)),
                whole(pairs + pair),
                whole(2 * pairs + pair),
                pl.BlockSpec((n, slots, PAIR), lambda t, ids: (0, 0, pair)),
                pl.BlockSpec((8, slots), lambda t, ids: (0, t)),
            ],
            out_specs=pl.BlockSpec((n, slots, 3 * PAIR), lambda t, ids: (0, 0, 0)),
            scratch_shapes=[
                pltpu.VMEM((n * slots, PAIR), LOW),
                pltpu.VMEM((n * slots, PAIR), WIDE),
                pltpu.VMEM((n * slots, PAIR), WIDE),
            ],
        ),
        out_shape=shape(n, slots, 3 * PAIR),
        compiler_params=params(),
        cost_estimate=cost(16),
    )


def normal(values):
    center = values - jnp.mean(values, -1, keepdims=True)
    scale = lax.rsqrt(jnp.mean(center * center, -1, keepdims=True) + EPSILON)
    return center * scale, scale


def normal_back(grad, unit, scale):
    inner = jnp.mean(grad * unit, -1, keepdims=True)
    return (grad - jnp.mean(grad, -1, keepdims=True) - unit * inner) * scale


def forward(n, pairs, ids, *refs):
    parts, refs = refs[:pairs], refs[pairs:]
    start, cotangent, wo_own, wi_own, wu_own = refs[:5]
    vectors, bi = refs[5:7]
    bo, bu, gain1, shift1, gain2, shift2 = [vectors.at[i : i + 1] for i in range(6)]
    refs = refs[7:]
    side, tall, refs = refs[:4], refs[4:8], refs[8:]
    attn, first, normed_low, active, slope, out, grad_second, second_low, sums = refs[:9]
    wo, wi, wu, normed, second, ordered, sem_o, sem_i, sem_u = refs[9:]
    slots, width = start.shape
    cols = width // n
    hidden = active.shape[1]
    deep = hidden // n
    row_o, row_u = cols // (2 * GROUP), deep // (2 * GROUP)
    get_o = loads(ids, [(wo_own, width)], tall, sem_o, wo, row_o, 0, 0)
    get_i = loads(ids, [(wi_own, hidden)], side, sem_i, wi, row_o, 0, 3 * width)
    get_u = loads(ids, [(wu_own, width)], tall, sem_u, wu, row_u, row_o, 0)
    begin(get_o)
    begin(get_i)
    begin(get_u)
    for g in range(n):
        for p in range(pairs):
            attn[:, pl.ds(g * cols + p * PAIR, PAIR)] = parts[p][g]

    def put_in_order(ref):
        for k in range(n):
            ordered[:, k * cols : (k + 1) * cols] = ref[:, part_of(shard_of(ids, k, n) * cols, cols)]

    put_in_order(attn)
    finish(get_o)

    def mix(j, _):
        column = part_of(j * STEP, STEP)
        total = dot(ordered[...], wo[:, :, column].reshape(width, STEP))
        first[:, column] = total + start[:, column] + bo[:, column]
        return 0

    lax.fori_loop(0, width // STEP, mix, 0)

    def norm(i, _):
        row = part_of(i * 128, 128)
        unit, _ = normal(first[row, :])
        value = unit * gain1[...] + shift1[...]
        normed[row, :] = value
        normed_low[row, :] = value.astype(LOW)
        return 0

    lax.fori_loop(0, slots // 128, norm, 0)
    put_in_order(normed_low)
    finish(get_i)

    def expand(j, _):
        column = part_of(j * STEP, STEP)
        x = dot(ordered[...], wi[:, :, column].reshape(width, STEP)) + bi[:, column]
        factor = math.sqrt(2 / math.pi)
        square = x * x
        t = jnp.tanh(factor * x * (1.0 + 0.044715 * square))
        half = 0.5 * (1.0 + t)
        active[:, column] = (x * half).astype(LOW)
        steep = half + (0.5 * factor) * x * (1.0 - t * t) * (1.0 + 0.134145 * square)
        slope[:, column] = steep.astype(LOW)
        return 0

    lax.fori_loop(0, hidden // STEP, expand, 0)
    finish(get_u)

    def contract(j, _):
        column = part_of(j * STEP, STEP)
        total = normed[:, column] + bu[:, column]
        for k in range(n):
            left = active[:, part_of(shard_of(ids, k, n) * deep, deep)]
            total = total + dot(left, wu[k, :, column])
        second[:, column] = total
        return 0

    lax.fori_loop(0, width // STEP, contract, 0)
    sums[...] = jnp.zeros_like(sums)

    def last(i, _):
        row = part_of(i * 128, 128)
        live = lax.broadcasted_iota(jnp.int32, (128, 1), 0) + i * 128 < ids[OWNED]
        live = live.astype(WIDE)
        unit, scale = normal(second[row, :])
        out[row, :] = ((unit * gain2[...] + shift2[...]) * live).astype(LOW)
        grad = cotangent[row, :].astype(WIDE) * live
        result = normal_back(grad * gain2[...], unit, scale)
        grad_second[row, :] = result
        second_low[row, :] = result.astype(LOW)
        for j, item in enumerate((grad * unit, grad, result)):
            sums[j : j + 1, :] += jnp.sum(item, 0, keepdims=True)
        return 0

    lax.fori_loop(0, slots // 128, last, 0)


def backward_inner(n, ids, *refs):
    second_low, slope, wu_own = refs[:3]
    tall, (inner_low, bias_sum, wu, sem_u) = refs[3:7], refs[7:]
    hidden = slope.shape[1]
    deep, cols = hidden // n, second_low.shape[1] // n
    row_o, row_u = cols // (2 * GROUP), deep // (2 * GROUP)
    get_u = loads(ids, [(wu_own, second_low.shape[1])], tall, sem_u, wu, row_u, row_o, 0)
    begin(get_u)
    finish(get_u)

    def expand(j, _):
        for k in range(n):
            column = part_of(shard_of(ids, k, n) * deep + j * STEP, STEP)
            grad = right_dot(second_low[...], wu[k, part_of(j * STEP, STEP), :])
            value = (grad * slope[:, column].astype(WIDE)).astype(LOW)
            inner_low[:, column] = value
            bias_sum[:, column] = jnp.sum(value.astype(WIDE), 0, keepdims=True)
        return 0

    lax.fori_loop(0, deep // STEP, expand, 0)


def backward(n, ids, *refs):
    inner_low, bias_sum, grad_second, first, vectors, sums, wo_own, wi_own = refs[:8]
    side, tall, refs = refs[8:12], refs[12:16], refs[16:]
    grad_first, first_low = refs[:2]
    grad_attn, small = refs[2:4]
    wo, wi, grad_normed, more, sem_o, sem_i = refs[4:]
    slots, width = first.shape
    cols = width // n
    hidden = inner_low.shape[1]
    deep = hidden // n
    row_o = cols // (2 * GROUP)
    get_o = loads(ids, [(wo_own, width)], tall, sem_o, wo, row_o, 0, 0)
    get_i = loads(ids, [(wi_own, hidden)], side, sem_i, wi, row_o, 0, 3 * width)
    begin(get_i)
    begin(get_o)
    finish(get_i)
    for k in range(n):
        column = part_of(shard_of(ids, k, n) * cols, cols)
        grad_normed[:, column] = right_dot(inner_low[...], wi[k]) + grad_second[:, column]
    more[...] = jnp.zeros_like(more)

    def norm(i, _):
        row = part_of(i * 128, 128)
        unit, scale = normal(first[row, :])
        grad = grad_normed[row, :]
        result = normal_back(grad * vectors[2:3], unit, scale)
        grad_first[row, :] = result
        first_low[row, :] = result.astype(LOW)
        for j, item in enumerate((result, grad * unit, grad)):
            more[j : j + 1, :] += jnp.sum(item, 0, keepdims=True)
        return 0

    lax.fori_loop(0, slots // 128, norm, 0)
    finish(get_o)
    for k in range(n):
        grad_attn[shard_of(ids, k, n)] = right_dot(first_low[...], wo[k]).astype(LOW)
    small[...] = jnp.zeros_like(small)
    for z in range(n):
        here = pl.ds(z * cols, cols)
        rows = [more[0:1, here]]
        rows += [bias_sum[:, pl.ds(z * deep + j * cols, cols)] for j in range(deep // cols)]
        rows += [sums[2:3, here], more[1:2, here], more[2:3, here], sums[0:1, here], sums[1:2, here]]
        for j, item in enumerate(rows):
            small[z, j : j + 1, :] = item


def finish_hidden(n, pairs, ids, *refs):
    parts, refs = refs[:pairs], refs[pairs:]
    grad_first, wq, wk, wv = refs[:4]
    side, (out, total, held, acts, sems) = refs[4:8], refs[8:]
    slots, width = out.shape
    cols = width // n
    copies = loads(
        ids, [(wq, width), (wk, width), (wv, width)], side, sems, held, cols // (2 * GROUP), 0, 0
    )
    begin(copies)
    for g in range(n):
        for p in range(pairs):
            for j in range(3):
                column = j * width + g * cols + p * PAIR
                acts[:, column : column + PAIR] = parts[p][g, :, j * PAIR : (j + 1) * PAIR]
    finish(copies)
    for k in range(n):
        column = part_of(shard_of(ids, k, n) * cols, cols)
        out[:, column] = right_dot(acts[...], held[k]) + grad_first[:, column]
    block = lax.broadcasted_iota(jnp.int32, (32, 1), 0) < ids[HERE]
    total[...] = jnp.sum(jnp.where(block, out[:32, :], 0.0), 0, keepdims=True)


def outer_product(spec, keep, ids, *refs):
    lefts, rights = [], []
    for count, _ in spec:
        lefts.append(refs[:count])
        rights.append(refs[count : 2 * count])
        refs = refs[2 * count :]
    at = 0
    for (count, cols), left, right in zip(spec, lefts, rights):
        step = min(cols, 1024)
        for col in range(0, cols, step):
            total = left_dot(left[0][...], right[0][:, col : col + step])
            for i in range(1, count):
                total = total + left_dot(left[i][...], right[i][:, col : col + step])
            here = slice(at + col, at + col + step)
            if not keep:
                refs[0][0, :, here] = total.astype(LOW)
                continue
            got, outs = refs[0], refs[1:]
            total = (total + got[0, :, here].astype(WIDE)).astype(LOW)
            split_halves(ids, total, [out.at[0, :, here] for out in outs], (X, Y))
        at += cols


def split_halves(ids, total, outs, bits):
    rows = total.shape[0] // 4
    parts = [total[i * rows : (i + 1) * rows] for i in range(4)]
    for half, bit in enumerate(bits):
        high = ids[bit] == 1
        low_part, high_part = parts[2 * half], parts[2 * half + 1]
        outs[2 * half][...] = jnp.where(high, low_part, high_part)
        outs[2 * half + 1][...] = jnp.where(high, high_part, low_part)


def gradient(order, spec, n, got=None):
    rows = spec[0][0][0][0].shape[1] // (2 * n)
    keep = got is not None
    in_specs, args, total, flops = [], [], 0, 0
    for pairs, cols in spec:
        for left, _ in pairs:
            block = lambda z, ids: (0, 2 * z + (ids[CORE] if keep else 1 - ids[CORE]))
            in_specs.append(pl.BlockSpec((left.shape[0], rows), block))
            args.append(left)
        for _, right in pairs:
            in_specs.append(pl.BlockSpec(right.shape, lambda z, ids: (0, 0)))
            args.append(right)
            flops += 2 * n * rows * right.shape[0] * cols
        total += cols
    if keep:
        in_specs.append(pl.BlockSpec((1, rows, total), lambda z, ids: (z, 0, 0)))
        args.append(got)
    out_rows, count = (rows // 4, 4) if keep else (rows, 1)
    return order.call(
        functools.partial(outer_product, [(len(pairs), cols) for pairs, cols in spec], keep),
        *args,
        grid_spec=pltpu.PrefetchScalarGridSpec(
            num_scalar_prefetch=1,
            grid=(n,),
            in_specs=in_specs,
            out_specs=[pl.BlockSpec((1, out_rows, total), lambda z, ids: (z, 0, 0))] * count,
        ),
        out_shape=[shape(n, out_rows, total)] * count,
        compiler_params=params(),
        cost_estimate=cost(0),
    )


def fold_two(ids, keep_one, got_one, keep_two, got_two, *outs):
    rows = keep_one.shape[1] // 2
    for z in range(keep_one.shape[0]):
        one = (keep_one[z].astype(WIDE) + got_one[z].astype(WIDE)).astype(LOW)
        two = (keep_two[z].astype(WIDE) + got_two[z].astype(WIDE)).astype(LOW)
        for total, bit, (send, keep) in ((one, Y, outs[:2]), (two, X, outs[2:])):
            high = ids[bit] == 1
            send[z] = jnp.where(high, total[:rows], total[rows:])
            keep[z] = jnp.where(high, total[rows:], total[:rows])


def fold_three(ids, keep_one, got_one, keep_two, got_two, out):
    for z in range(out.shape[0]):
        out[z, 0] = (keep_one[z].astype(WIDE) + got_one[z].astype(WIDE)).astype(LOW)
        out[z, 1] = (keep_two[z].astype(WIDE) + got_two[z].astype(WIDE)).astype(LOW)


def fold_four(splits, ids, *refs):
    parts, outs = refs[: len(splits)], refs[len(splits) :]
    for i, (split, terms) in enumerate(zip(splits, parts)):
        n, cols = terms.shape[0], terms.shape[3]
        for h, out in enumerate(outs):
            if split < cols:
                total = terms[0, h, :, split:].astype(WIDE)
                for z in range(1, n):
                    total = total + terms[z, h, :, split:].astype(WIDE)
                out[i, :, n * split :] = total.astype(LOW)
            for z in range(n if split else 0):
                out[i, :, z * split : (z + 1) * split] = terms[z, h, :, :split]


def small_call(order, body, args, outs):
    return order.call(
        body,
        *args,
        in_specs=[SMEM] + [VMEM] * len(args),
        out_specs=[VMEM] * len(outs),
        out_shape=outs,
        compiler_params=params(),
        cost_estimate=cost(0),
    )


def reduce_first(order, spec, n):
    (send,) = gradient(order, spec, n)
    return swap(send, 1)


def reduce_second(order, spec, n, got):
    send_one, keep_one, send_two, keep_two = gradient(order, spec, n, got)
    return keep_one, swap(send_one, 2), keep_two, swap(send_two, 4)


def reduce_third(order, n, held):
    rows, cols = held[0].shape[1:]
    outs = [shape(n, rows // 2, cols)] * 4
    send_one, keep_one, send_two, keep_two = small_call(order, fold_two, held, outs)
    return keep_one, swap(send_one, 4), keep_two, swap(send_two, 2)


def reduce_fourth(order, n, held, send=True):
    rows, cols = held[0].shape[1:]
    (out,) = small_call(order, fold_three, held, [shape(n, 2, rows, cols)])
    return exchange(out) if send else out


def reduce_fifth(order, held, splits):
    n, _, rows, cols = held[0].shape
    outs = [shape(len(held), rows, cols + (n - 1) * splits[0])] * 2
    one, two = small_call(order, functools.partial(fold_four, splits), held, outs)
    mask = GROUP
    while mask < lax.axis_size("dp"):
        one, two = [(v.astype(WIDE) + swap(v, mask).astype(WIDE)).astype(LOW) for v in (one, two)]
        mask *= 2
    return one, two


def place_grad(plan, ids, *refs):
    pieces, outs = refs[:4], refs[4:]
    rows = pieces[0].shape[3]
    for i in range(2 * GROUP):
        piece = piece_of(pieces, i // 2, i % 2)
        home = ids[INDEX] ^ (i // 2)
        core, x, y = home & 1, (home >> 1) & 1, (home >> 2) & 1
        block = core * 8 + (x * 2 + y if i % 2 == 0 else 4 + y * 2 + x)
        row = part_of(block * rows, rows)
        for out, moves in zip(outs, plan):
            for layer, source, target, size in moves:
                value = piece[layer, :, source : source + size]
                out[row, target : target + size] = value.astype(WIDE)


def reduce_last(order, pieces, plan, widths):
    rows = pieces[0].shape[3] * 2 * GROUP
    return small_call(
        order,
        functools.partial(place_grad, plan),
        pieces,
        [shape(rows, width, dtype=WIDE) for width in widths],
    )


def per_device(
    hidden_in,
    cotangent,
    context_len,
    block_device,
    timestep,
    query_weight,
    key_weight,
    value_weight,
    output_weight,
    inner_weight,
    outer_weight,
    query_bias,
    value_bias,
    output_bias,
    inner_bias,
    outer_bias,
    attn_gain,
    attn_shift,
    ffn_gain,
    ffn_shift,
    time_table,
):
    n = lax.axis_size("ctx")
    place = lax.axis_index("ctx")
    d = lax.axis_index("dp") % GROUP
    _, slots, width = hidden_in.shape
    hidden = inner_weight.shape[1]
    cols = width // n
    deep = hidden // n
    pairs = cols // PAIR
    span = (n - 1) * slots + TAIL
    holder = block_device[0]
    context = context_len[0]

    groups = [j + (j >= holder).astype(jnp.int32) for j in range(n - 1)] + [holder]
    position = lambda g: jnp.where(g == holder, n - 1, g - (g > holder).astype(jnp.int32))
    counts = [context // (n - 1) + (j < context % (n - 1)).astype(jnp.int32) for j in range(n - 1)]
    counts = jnp.stack(counts + [jnp.int32(BLOCK)])
    slot = jnp.arange(slots, dtype=jnp.int32)
    live = (slot[None, :] < counts[:, None]).reshape(n * slots)[:span]
    bias = jnp.where(live, 0.0, -1e30).astype(WIDE)
    bias_row, bias_col = bias[None, :], jnp.broadcast_to(bias[:, None], (span, 128))
    owned = lax.dynamic_index_in_dim(counts, position(place), keepdims=False)
    here = jnp.where(holder == place, BLOCK, 0)
    ids = [place, d, d & 1, (d >> 1) & 1, (d >> 2) & 1, owned, here]
    ids += [position(jnp.int32(g)) for g in range(n)] + groups
    order = Order(jnp.stack([jnp.asarray(v, jnp.int32) for v in ids]))
    embed = lax.dynamic_slice_in_dim(time_table, timestep[0], 1, 0).astype(WIDE)
    block = ((holder == place) & (slot < BLOCK)).astype(WIDE)[:, None]
    start = hidden_in[0].astype(WIDE) + block * embed
    start_low = start.astype(LOW)

    def piece(weight):
        part = weight.shape[0] // GROUP
        return lax.dynamic_slice_in_dim(weight, d * part, part, 0).reshape(2, part // 2, -1)

    side_piece = jnp.concatenate(
        [piece(w) for w in (query_weight, key_weight, value_weight, inner_weight)], 2
    )
    tall_piece = jnp.concatenate([piece(output_weight), piece(outer_weight)], 1)
    one, two = one_off(side_piece)
    far = two_off(side_piece)
    order.tick(far)
    on = sent_on(order.release(far))
    tall_far = two_off(order.release(tall_piece))
    order.tick(one, two, on)
    side = by_distance(far, one, two, on)
    side = gather_near(side[:, 0], side[:, 1])
    one, two = one_off(order.release(tall_piece))
    order.tick(tall_far, *side)
    on = sent_on(order.release(tall_far))
    side = gather_far(*side)
    order.tick(one, two, on)
    row_low = exchange(jnp.broadcast_to(order.release(start_low), (n, slots, width)))
    row_low = row_low.reshape(n * slots, width)
    tall = by_distance(tall_far, one, two, on)
    tall = gather_near(tall[:, 0], tall[:, 1])
    order.tick(*side)
    side = gather_cores(*side)
    order.tick(*tall)
    tall = gather_far(*tall)
    vectors = (output_bias, outer_bias, attn_gain, attn_shift, ffn_gain, ffn_shift)
    vectors = jnp.stack([v.astype(WIDE) for v in vectors])
    inner_row = inner_bias.astype(WIDE)[None]
    own_bias = lambda v: lax.dynamic_slice_in_dim(v, place * cols, cols, 0).astype(WIDE)
    qkv_bias = jnp.concatenate([own_bias(query_bias), jnp.zeros((cols,), WIDE), own_bias(value_bias)])
    qkv_bias = qkv_bias[None]
    vectors, inner_row, qkv_bias, bias_row, bias_col, start = lax.optimization_barrier(
        (vectors, inner_row, qkv_bias, bias_row, bias_col, start)
    )
    order.wait(vectors, inner_row, qkv_bias, bias_row, bias_col, start)
    qkv = order.call(
        functools.partial(project, n),
        *(row_low, query_weight, key_weight, value_weight, *side, qkv_bias),
        in_specs=[SMEM] + [VMEM] + [ANY] * 7 + [VMEM],
        out_specs=VMEM,
        out_shape=shape(span, 3 * cols),
        scratch_shapes=[
            pltpu.VMEM((n * slots, width), LOW),
            pltpu.VMEM((n, cols, 3 * cols), LOW),
            pltpu.SemaphoreType.DMA((3 + 6 * GROUP,)),
        ],
        compiler_params=params(),
        cost_estimate=cost(8),
    )

    mixed, lses = [], []
    for pair in range(pairs):
        if pair == 1:
            order.wait(*tall)
            tall = gather_cores(*tall)
        mix, lse = attention(order, qkv, bias_row, pair, pairs, n, slots)
        lses.append(lse)
        if mixed:
            order.tick(mixed[-1])
            mix = order.release(mix)
        mixed.append(exchange(mix))

    held_o = pltpu.VMEM((n, cols, width), LOW)
    held_i = pltpu.VMEM((n, cols, hidden), LOW)
    held_u = pltpu.VMEM((n, deep, width), LOW)
    wide_one = pltpu.VMEM((slots, width), WIDE)
    sem = pltpu.SemaphoreType.DMA((1 + 2 * GROUP,))
    flops = 2 * slots * width * (width + 2 * hidden)
    attn, first, normed_low, active, slope, out, grad_second, second_low, sums = order.call(
        functools.partial(forward, n, pairs),
        *(*mixed, start, cotangent[0], output_weight, inner_weight, outer_weight),
        *(vectors, inner_row, *side, *tall),
        in_specs=[SMEM] + [VMEM] * (pairs + 2) + [ANY] * 3 + [VMEM] * 2 + [ANY] * 8,
        out_specs=[VMEM] * 9,
        out_shape=[
            shape(slots, width),
            shape(slots, width, dtype=WIDE),
            shape(slots, width),
            shape(slots, hidden),
            shape(slots, hidden),
            shape(slots, width),
            shape(slots, width, dtype=WIDE),
            shape(slots, width),
            shape(8, width, dtype=WIDE),
        ],
        scratch_shapes=[
            *(held_o, held_i, held_u, wide_one, wide_one),
            pltpu.VMEM((slots, width), LOW),
            *(sem, sem, sem),
        ],
        compiler_params=params(),
        cost_estimate=cost(24),
    )
    outer_spec = [([(active, second_low)], width)]
    outer_held = reduce_first(order, outer_spec, n)
    inner_low, bias_sum = order.call(
        functools.partial(backward_inner, n),
        *(second_low, slope, outer_weight, *tall),
        in_specs=[SMEM] + [VMEM] * 2 + [ANY] * 5,
        out_specs=[VMEM] * 2,
        out_shape=[shape(slots, hidden), shape(1, hidden, dtype=WIDE)],
        scratch_shapes=[held_u, sem],
        compiler_params=params(),
        cost_estimate=cost(12),
    )
    outer_held = reduce_second(order, outer_spec, n, outer_held)
    inner_spec = [([(normed_low, inner_low)], hidden)]
    inner_held = reduce_first(order, inner_spec, n)
    grad_first, first_low, grad_attn, small = order.call(
        functools.partial(backward, n),
        *(inner_low, bias_sum, grad_second, first, vectors, sums),
        *(output_weight, inner_weight, *side, *tall),
        in_specs=[SMEM] + [VMEM] * 6 + [ANY] * 10,
        out_specs=[VMEM] * 4,
        out_shape=[
            shape(slots, width, dtype=WIDE),
            shape(slots, width),
            shape(n, slots, cols),
            shape(n, 16, cols, dtype=WIDE),
        ],
        scratch_shapes=[held_o, held_i, wide_one, pltpu.VMEM((8, width), WIDE), sem, sem],
        compiler_params=params(),
        cost_estimate=cost(13),
    )
    grad_mixed = exchange(grad_attn)
    outer_held = reduce_third(order, n, outer_held)
    inner_held = reduce_second(order, inner_spec, n, inner_held)
    order.wait(grad_mixed)
    outer_held = reduce_fourth(order, n, outer_held)

    backs, received = [], []
    for pair in range(pairs):
        if pair:
            received.append(exchange(backs[-1]))
            order.wait(outer_held)
            outer_pieces = gather_near(*reduce_fifth(order, [outer_held], [0]))
            inner_held = reduce_third(order, n, inner_held)
        backs.append(
            attention_back(order, qkv, bias_col, grad_mixed, lses[pair], pair, pairs, n, slots)
        )
    order.wait(*received, *inner_held, *outer_pieces)
    received.append(exchange(backs[-1]))
    outer_pieces = gather_far(*order.release(*outer_pieces))
    rest_spec = [([(row_low, back.reshape(n * slots, -1))], 3 * PAIR) for back in backs]
    rest_spec += [([(attn, first_low)], width)]
    rest_held = reduce_first(order, rest_spec, n)
    inner_held = reduce_fourth(order, n, inner_held, False)
    order.wait(*outer_pieces)
    outer_pieces = gather_cores(*order.release(*outer_pieces))
    rest_held = reduce_second(order, rest_spec, n, rest_held)
    order.tick(received[-1])
    inner_held = exchange(order.release(inner_held))
    (outer_grad,) = reduce_last(order, outer_pieces, [[(0, 0, 0, width)]], [width])
    rest_held = reduce_third(order, n, rest_held)
    grad_hidden, block_sum = order.call(
        functools.partial(finish_hidden, n, pairs),
        *(*received, grad_first, query_weight, key_weight, value_weight, *side),
        in_specs=[SMEM] + [VMEM] * (pairs + 1) + [ANY] * 7,
        out_specs=[VMEM] * 2,
        out_shape=[shape(slots, width, dtype=WIDE), shape(1, width, dtype=WIDE)],
        scratch_shapes=[
            pltpu.VMEM((n, cols, 3 * width), LOW),
            pltpu.VMEM((slots, 3 * width), LOW),
            pltpu.SemaphoreType.DMA((3 + 2 * GROUP,)),
        ],
        compiler_params=params(),
        cost_estimate=cost(9),
    )
    order.wait(*rest_held)
    rest_held = reduce_fourth(order, n, rest_held, False)
    order.tick(inner_held)
    rest_held = exchange(order.release(rest_held))
    inner_pieces = gather_near(*reduce_fifth(order, [inner_held], [0]))
    order.tick(rest_held, *inner_pieces)
    inner_pieces = gather_far(*order.release(*inner_pieces))
    pieces = gather_near(*reduce_fifth(order, [rest_held], [3 * cols]))

    packed = jnp.concatenate([small, block_sum.reshape(1, n, cols).repeat(n, 0)], 1)
    total = jnp.sum(exchange(order.release(packed)), 0)
    used = small.shape[1]
    bias_sums = jnp.stack([jnp.sum(back.astype(WIDE), (0, 1)) for back in backs])
    level = jnp.full((1, cols), timestep[0], WIDE)
    total = jnp.concatenate([total, level, bias_sums.reshape(-1, cols)])
    order.tick(*inner_pieces, total)
    inner_pieces = gather_cores(*order.release(*inner_pieces))
    rows = lax.axis_size("dp")
    total = exchange(jnp.broadcast_to(order.release(total), (rows, *total.shape)), "dp")
    vector = total[:, used : used + n + 1]
    total = jnp.sum(total, 0)
    total = jnp.concatenate([total[:used], total[used + n + 1 :]])
    per = deep // cols
    sums = [total[0], total[1 : 1 + per].reshape(deep)] + [total[1 + per + i] for i in range(5)]
    bias_sums = total[used:].reshape(pairs, 3 * PAIR)
    query_sum = bias_sums[:, :PAIR].reshape(cols)
    value_sum = bias_sums[:, 2 * PAIR :].reshape(cols)
    share = time_table.shape[0] // n
    levels = (jnp.arange(share, dtype=jnp.int32) + place * share).astype(WIDE)
    onehot = (vector[:, n, :1] == levels[None, :]).astype(WIDE)
    time_table_grad = lax.dot_general(
        onehot,
        vector[:, :n].reshape(-1, width),
        (((0,), (0,)), ((), ())),
        precision=lax.Precision.HIGHEST,
        preferred_element_type=WIDE,
    )

    order.wait(*pieces)
    pieces = gather_far(*order.release(*pieces))
    (inner_grad,) = reduce_last(order, inner_pieces, [[(0, 0, 0, hidden)]], [hidden])
    order.wait(*pieces)
    pieces = gather_cores(*order.release(*pieces))
    plan = [
        [
            (0, g * 3 * cols + p * 3 * PAIR + j * PAIR, g * cols + p * PAIR, PAIR)
            for g in range(n)
            for p in range(pairs)
        ]
        for j in range(3)
    ]
    plan += [[(0, n * 3 * cols, 0, width)]]
    *weight_grads, output_grad = reduce_last(order, pieces, plan, [width] * 4)
    return (
        out[None],
        grad_hidden[None],
        *weight_grads,
        output_grad,
        inner_grad,
        outer_grad,
        query_sum,
        value_sum,
        *sums,
        time_table_grad,
    )


def solution(mesh):
    row, shard, same = P("dp", "ctx", None), P("ctx", None), P()
    return jax.shard_map(
        per_device,
        mesh=mesh,
        in_specs=(row, row, P("dp"), P("dp"), P("dp")) + (shard,) * 6 + (same,) * 10,
        out_specs=(row, row) + (shard,) * 6 + (P("ctx"),) * 9 + (shard,),
        check_vma=False,
    )
```

```python
import functools
import math

import jax
import jax.numpy as jnp
from jax import lax
from jax.experimental import pallas as pl
from jax.experimental.pallas import tpu as pltpu
from jax.sharding import PartitionSpec as P

HEADS = 16
HD = 64
BLOCK = 25
EPSILON = 1e-05
GROUP = 8
TAIL = 128
FEW = 32
PAIR = 2 * HD
STEP = 512
FACTOR = 16
LOG2E = 1.4426950408889634
LOW = jnp.bfloat16
WIDE = jnp.float32
VMEM = pl.BlockSpec(memory_space=pltpu.VMEM)
SMEM = pl.BlockSpec(memory_space=pltpu.SMEM)
ANY = pl.BlockSpec(memory_space=pl.ANY)
PLACE, INDEX, CORE, X, Y, OWNED, HERE, LISTS = range(8)


def params(mib=56):
    return pltpu.CompilerParams(vmem_limit_bytes=mib << 20)


def cost(us):
    us = us * FACTOR
    return pl.CostEstimate(flops=int(us * 1e9), bytes_accessed=int(us * 3e6), transcendentals=0)


def shape(*dims, dtype=LOW):
    return jax.ShapeDtypeStruct(dims, dtype)


def dot(left, right, dims=((1,), (0,))):
    return lax.dot_general(left, right, (dims, ((), ())), preferred_element_type=WIDE)


def left_dot(left, right):
    return dot(left, right, ((0,), (0,)))


def right_dot(left, right):
    return dot(left, right, ((1,), (1,)))


def part_of(start, size):
    return pl.ds(pl.multiple_of(start, size), size)


def swap(value, mask):
    size = lax.axis_size("dp")
    return lax.ppermute(value, "dp", [(i, i ^ mask) for i in range(size)])


def along(value, *pairs):
    return lax.ppermute(value, "ctx", pairs)


def exchange(value, axis="ctx"):
    return lax.all_to_all(value, axis, 0, 0)


def after(value, *others):
    return lax.optimization_barrier((value, *others))[0]


def two_off(value):
    return along(value, (0, 2), (1, 3), (2, 0), (3, 1))


def one_off(value):
    return along(value, (0, 1), (1, 2), (2, 3)), along(value, (1, 0), (2, 1), (3, 2))


def sent_on(far):
    return along(far, (2, 3), (1, 0))


def by_distance(far, up, down, on):
    place = lax.axis_index("ctx")
    return jnp.stack([jnp.where(place == 0, on, up), far, jnp.where(place == 3, on, down)])


def copy_numbers(ids, out):
    for i in range(ids.shape[0]):
        out[i] = ids[i]


class Order:
    def __init__(self, ids):
        self.ids = ids

    def call(self, body, *args, **kwargs):
        outs = pl.pallas_call(body, **kwargs)(self.ids, *args)
        self.wait(outs[0] if isinstance(outs, (list, tuple)) else outs)
        return outs

    def wait(self, *values):
        self.ids = after(self.ids, *values)

    def tick(self, *values):
        self.wait(*values)
        self.call(
            copy_numbers,
            in_specs=[SMEM],
            out_specs=SMEM,
            out_shape=jax.ShapeDtypeStruct(self.ids.shape, jnp.int32),
            cost_estimate=cost(0),
        )

    def release(self, *values):
        outs = lax.optimization_barrier((*values, self.ids))[:-1]
        return outs if len(outs) > 1 else outs[0]


def gather_near(one, two):
    return jnp.stack([one, swap(one, 2)]), jnp.stack([two, swap(two, 4)])


def gather_far(one, two):
    return jnp.stack([one, swap(one, 4)]), jnp.stack([two, swap(two, 2)])


def gather_cores(one, two):
    return one, two, swap(one, 1), swap(two, 1)


def piece_of(arrays, mask, half):
    x, y = (mask >> 1) & 1, (mask >> 2) & 1
    return arrays[2 * (mask & 1) + half].at[(x, y) if half else (y, x)]


def loads(ids, own, pieces, sems, held, rows, row, col):
    n, _, cols = held.shape
    copies = []
    at = 0
    for ref, width in own:
        copies.append(
            pltpu.make_async_copy(ref, held.at[0, :, pl.ds(at, width)], sems.at[len(copies)])
        )
        at += width
    for i in range(2 * GROUP):
        where = ((ids[INDEX] ^ (i // 2)) * 2 + i % 2) * rows
        piece = piece_of(pieces, i // 2, i % 2)
        copies.append(
            pltpu.make_async_copy(
                piece.at[:, pl.ds(row, rows), pl.ds(col, cols)],
                held.at[pl.ds(1, n - 1), part_of(where, rows), :],
                sems.at[len(copies)],
            )
        )
    return copies


def begin(copies):
    for copy in copies:
        copy.start()


def finish(copies):
    for copy in copies:
        copy.wait()


def shard_of(ids, k, n):
    return lax.rem(ids[PLACE] + n - k, n)


def project(n, ids, *refs):
    row_ref, wq, wk, wv = refs[:4]
    refs = refs[4:]
    pieces, (bias, out, compact, held, sems) = refs[:4], refs[4:]
    width = row_ref.shape[1]
    slots = row_ref.shape[0] // n
    cols = width // n
    rows = pieces[0].shape[3]
    copies = []
    for j, own in enumerate((wq, wk, wv)):
        copies.append(
            pltpu.make_async_copy(
                own.at[:, part_of(ids[PLACE] * cols, cols)],
                held.at[0, :, pl.ds(j * cols, cols)],
                sems.at[len(copies)],
            )
        )
        for i in range(2 * GROUP):
            where = ((ids[INDEX] ^ (i // 2)) * 2 + i % 2) * rows
            piece = piece_of(pieces, i // 2, i % 2)
            copies.append(
                pltpu.make_async_copy(
                    piece.at[:, :, part_of(j * width + ids[PLACE] * cols, cols)],
                    held.at[pl.ds(1, n - 1), part_of(where, rows), pl.ds(j * cols, cols)],
                    sems.at[len(copies)],
                )
            )
    begin(copies)
    for g in range(n):
        compact[part_of(ids[LISTS + g] * slots, slots), :] = row_ref[g * slots : (g + 1) * slots, :]
    finish(copies)

    def block(i, _):
        row = part_of(i * 256, 256)
        total = bias[...]
        for k in range(n):
            column = part_of(shard_of(ids, k, n) * cols, cols)
            total = total + dot(compact[row, column], held[k])
        out[row, :] = total.astype(LOW)
        return 0

    lax.fori_loop(0, out.shape[0] // 256, block, 0)


def attend(n, ids, bias_ref, q_ref, k_ref, v_ref, *refs):
    out_ref, lse_ref = refs
    tile = pl.program_id(0)
    slots = q_ref.shape[0]
    first = lax.broadcasted_iota(jnp.int32, (1, PAIR), 1) < HD

    def work(rows):
        query = q_ref[:rows, :]
        keys, values = k_ref[...], v_ref[...]
        mixed = []
        for h in range(2):
            mine = first if h == 0 else jnp.logical_not(first)
            scores = right_dot(jnp.where(mine, query, 0), keys)
            scores = scores * (LOG2E / math.sqrt(HD)) + bias_ref[...]
            high = jnp.max(scores, -1, keepdims=True)
            expo = jnp.exp2(scores - high)
            total = jnp.sum(expo, -1, keepdims=True)
            probs = (expo * (1.0 / total)).astype(LOW)
            mixed.append(dot(probs, values))
            lse = jnp.broadcast_to(high + jnp.log2(total), (rows, 128))
            lse_ref[h : h + 1, :rows] = lse.T[:1, :]
        out_ref[0, :rows, :] = jnp.where(first, mixed[0], mixed[1]).astype(LOW)
        if rows < slots:
            out_ref[0, rows:, :] = jnp.zeros((slots - rows, PAIR), LOW)

    @pl.when(tile < n - 1)
    def _():
        work(slots)

    @pl.when(tile == n - 1)
    def _():
        work(TAIL)
        lse_ref[:, TAIL:] = jnp.zeros((8, slots - TAIL), WIDE)


def attention(order, qkv, bias, pair, pairs, n, slots):
    span = qkv.shape[0]
    whole = lambda col: pl.BlockSpec((span, PAIR), lambda t, ids: (0, col))
    return order.call(
        functools.partial(attend, n),
        *(bias, qkv, qkv, qkv),
        grid_spec=pltpu.PrefetchScalarGridSpec(
            num_scalar_prefetch=1,
            grid=(n,),
            in_specs=[
                pl.BlockSpec((1, span), lambda t, ids: (0, 0)),
                pl.BlockSpec((slots, PAIR), lambda t, ids: (t, pair)),
                whole(pairs + pair),
                whole(2 * pairs + pair),
            ],
            out_specs=[
                pl.BlockSpec((1, slots, PAIR), lambda t, ids: (ids[LISTS + n + t], 0, 0)),
                pl.BlockSpec((8, slots), lambda t, ids: (0, t)),
            ],
        ),
        out_shape=[shape(n, slots, PAIR), shape(8, n * slots, dtype=WIDE)],
        compiler_params=params(),
        cost_estimate=cost(11),
    )


def attend_back(n, ids, bias_ref, q_ref, k_ref, v_ref, *refs):
    grad_ref, lse_ref, out_ref, do_ref, dk_ref, dv_ref = refs
    tile = pl.program_id(0)
    slots = q_ref.shape[0]
    span = k_ref.shape[0] - TAIL + FEW
    first = lax.broadcasted_iota(jnp.int32, (1, PAIR), 1) < HD
    scale = 1.0 / math.sqrt(HD)

    @pl.when(tile == 0)
    def _():
        dk_ref[...] = jnp.zeros_like(dk_ref)
        dv_ref[...] = jnp.zeros_like(dv_ref)
        for g in range(n):
            do_ref[part_of(ids[LISTS + g] * slots, slots), :] = grad_ref[g]

    def work(rows):
        keys, values = k_ref[:span, :], v_ref[:span, :]
        here = pl.ds(pl.multiple_of(tile * slots, slots), rows)
        parts = []
        for h in range(2):
            mine = first if h == 0 else jnp.logical_not(first)
            query = jnp.where(mine, q_ref[:rows, :], 0)
            grad = jnp.where(mine, do_ref[here, :], 0)
            scores = right_dot(keys, query) * (LOG2E * scale)
            bias = jnp.concatenate([bias_ref[:span, :]] * (rows // 128), 1)
            probs = jnp.exp2(scores + bias - lse_ref[h : h + 1, :rows])
            grad_probs = right_dot(values, grad)
            center = jnp.sum(grad_probs * probs, 0, keepdims=True)
            grad_scores = (probs * (grad_probs - center)).astype(LOW)
            dk_ref[:span, :] += dot(grad_scores, query)
            dv_ref[:span, :] += dot(probs.astype(LOW), grad)
            parts.append(left_dot(grad_scores, keys))
        group = ids[LISTS + n + tile]
        out_ref[group, :rows, :PAIR] = (jnp.where(first, parts[0], parts[1]) * scale).astype(LOW)
        if rows < slots:
            out_ref[group, rows:, :PAIR] = jnp.zeros((slots - rows, PAIR), LOW)

    @pl.when(tile < n - 1)
    def _():
        work(slots)

    @pl.when(tile == n - 1)
    def _():
        work(TAIL)
        for g in range(n):
            here = part_of(ids[LISTS + g] * slots, slots)
            out_ref[g, :, PAIR : 2 * PAIR] = (dk_ref[here, :] * scale).astype(LOW)
            out_ref[g, :, 2 * PAIR :] = dv_ref[here, :].astype(LOW)


def attention_back(order, qkv, bias, grad, lse, pair, pairs, n, slots):
    span = qkv.shape[0]
    whole = lambda col: pl.BlockSpec((span, PAIR), lambda t, ids: (0, col))
    return order.call(
        functools.partial(attend_back, n),
        *(bias, qkv, qkv, qkv, grad, lse),
        grid_spec=pltpu.PrefetchScalarGridSpec(
            num_scalar_prefetch=1,
            grid=(n,),
            in_specs=[
                pl.BlockSpec((span, 128), lambda t, ids: (0, 0)),
                pl.BlockSpec((slots, PAIR), lambda t, ids: (t, pair)),
                whole(pairs + pair),
                whole(2 * pairs + pair),
                pl.BlockSpec((n, slots, PAIR), lambda t, ids: (0, 0, pair)),
                pl.BlockSpec((8, slots), lambda t, ids: (0, t)),
            ],
            out_specs=pl.BlockSpec((n, slots, 3 * PAIR), lambda t, ids: (0, 0, 0)),
            scratch_shapes=[
                pltpu.VMEM((n * slots, PAIR), LOW),
                pltpu.VMEM((n * slots, PAIR), WIDE),
                pltpu.VMEM((n * slots, PAIR), WIDE),
            ],
        ),
        out_shape=shape(n, slots, 3 * PAIR),
        compiler_params=params(),
        cost_estimate=cost(16),
    )


def normal(values):
    center = values - jnp.mean(values, -1, keepdims=True)
    scale = lax.rsqrt(jnp.mean(center * center, -1, keepdims=True) + EPSILON)
    return center * scale, scale


def normal_back(grad, unit, scale):
    inner = jnp.mean(grad * unit, -1, keepdims=True)
    return (grad - jnp.mean(grad, -1, keepdims=True) - unit * inner) * scale


def forward(n, pairs, ids, *refs):
    parts, refs = refs[:pairs], refs[pairs:]
    start, cotangent, wo_own, wi_own, wu_own = refs[:5]
    vectors, bi = refs[5:7]
    bo, bu, gain1, shift1, gain2, shift2 = [vectors.at[i : i + 1] for i in range(6)]
    refs = refs[7:]
    side, tall, refs = refs[:4], refs[4:8], refs[8:]
    attn, first, normed_low, active, slope, out, grad_second, second_low, sums = refs[:9]
    wo, wi, wu, normed, second, ordered, sem_o, sem_i, sem_u = refs[9:]
    slots, width = start.shape
    cols = width // n
    hidden = active.shape[1]
    deep = hidden // n
    row_o, row_u = cols // (2 * GROUP), deep // (2 * GROUP)
    get_o = loads(ids, [(wo_own, width)], tall, sem_o, wo, row_o, 0, 0)
    get_i = loads(ids, [(wi_own, hidden)], side, sem_i, wi, row_o, 0, 3 * width)
    get_u = loads(ids, [(wu_own, width)], tall, sem_u, wu, row_u, row_o, 0)
    begin(get_o)
    begin(get_i)
    begin(get_u)
    for g in range(n):
        for p in range(pairs):
            attn[:, pl.ds(g * cols + p * PAIR, PAIR)] = parts[p][g]

    def put_in_order(ref):
        for k in range(n):
            ordered[:, k * cols : (k + 1) * cols] = ref[:, part_of(shard_of(ids, k, n) * cols, cols)]

    put_in_order(attn)
    finish(get_o)

    def mix(j, _):
        column = part_of(j * STEP, STEP)
        total = dot(ordered[...], wo[:, :, column].reshape(width, STEP))
        first[:, column] = total + start[:, column] + bo[:, column]
        return 0

    lax.fori_loop(0, width // STEP, mix, 0)

    def norm(i, _):
        row = part_of(i * 128, 128)
        unit, _ = normal(first[row, :])
        value = unit * gain1[...] + shift1[...]
        normed[row, :] = value
        normed_low[row, :] = value.astype(LOW)
        return 0

    lax.fori_loop(0, slots // 128, norm, 0)
    put_in_order(normed_low)
    finish(get_i)

    def expand(j, _):
        column = part_of(j * STEP, STEP)
        x = dot(ordered[...], wi[:, :, column].reshape(width, STEP)) + bi[:, column]
        factor = math.sqrt(2 / math.pi)
        square = x * x
        t = jnp.tanh(factor * x * (1.0 + 0.044715 * square))
        half = 0.5 * (1.0 + t)
        active[:, column] = (x * half).astype(LOW)
        steep = half + (0.5 * factor) * x * (1.0 - t * t) * (1.0 + 0.134145 * square)
        slope[:, column] = steep.astype(LOW)
        return 0

    lax.fori_loop(0, hidden // STEP, expand, 0)
    finish(get_u)

    def contract(j, _):
        column = part_of(j * STEP, STEP)
        total = normed[:, column] + bu[:, column]
        for k in range(n):
            left = active[:, part_of(shard_of(ids, k, n) * deep, deep)]
            total = total + dot(left, wu[k, :, column])
        second[:, column] = total
        return 0

    lax.fori_loop(0, width // STEP, contract, 0)
    sums[...] = jnp.zeros_like(sums)

    def last(i, _):
        row = part_of(i * 128, 128)
        live = lax.broadcasted_iota(jnp.int32, (128, 1), 0) + i * 128 < ids[OWNED]
        live = live.astype(WIDE)
        unit, scale = normal(second[row, :])
        out[row, :] = ((unit * gain2[...] + shift2[...]) * live).astype(LOW)
        grad = cotangent[row, :].astype(WIDE) * live
        result = normal_back(grad * gain2[...], unit, scale)
        grad_second[row, :] = result
        second_low[row, :] = result.astype(LOW)
        for j, item in enumerate((grad * unit, grad, result)):
            sums[j : j + 1, :] += jnp.sum(item, 0, keepdims=True)
        return 0

    lax.fori_loop(0, slots // 128, last, 0)


def backward_inner(n, ids, *refs):
    second_low, slope, wu_own = refs[:3]
    tall, (inner_low, bias_sum, wu, sem_u) = refs[3:7], refs[7:]
    hidden = slope.shape[1]
    deep, cols = hidden // n, second_low.shape[1] // n
    row_o, row_u = cols // (2 * GROUP), deep // (2 * GROUP)
    get_u = loads(ids, [(wu_own, second_low.shape[1])], tall, sem_u, wu, row_u, row_o, 0)
    begin(get_u)
    finish(get_u)

    def expand(j, _):
        for k in range(n):
            column = part_of(shard_of(ids, k, n) * deep + j * STEP, STEP)
            grad = right_dot(second_low[...], wu[k, part_of(j * STEP, STEP), :])
            value = (grad * slope[:, column].astype(WIDE)).astype(LOW)
            inner_low[:, column] = value
            bias_sum[:, column] = jnp.sum(value.astype(WIDE), 0, keepdims=True)
        return 0

    lax.fori_loop(0, deep // STEP, expand, 0)


def backward(n, ids, *refs):
    inner_low, bias_sum, grad_second, first, vectors, sums, wo_own, wi_own = refs[:8]
    side, tall, refs = refs[8:12], refs[12:16], refs[16:]
    grad_first, first_low = refs[:2]
    grad_attn, small = refs[2:4]
    wo, wi, grad_normed, more, sem_o, sem_i = refs[4:]
    slots, width = first.shape
    cols = width // n
    hidden = inner_low.shape[1]
    deep = hidden // n
    row_o = cols // (2 * GROUP)
    get_o = loads(ids, [(wo_own, width)], tall, sem_o, wo, row_o, 0, 0)
    get_i = loads(ids, [(wi_own, hidden)], side, sem_i, wi, row_o, 0, 3 * width)
    begin(get_i)
    begin(get_o)
    finish(get_i)
    for k in range(n):
        column = part_of(shard_of(ids, k, n) * cols, cols)
        grad_normed[:, column] = right_dot(inner_low[...], wi[k]) + grad_second[:, column]
    more[...] = jnp.zeros_like(more)

    def norm(i, _):
        row = part_of(i * 128, 128)
        unit, scale = normal(first[row, :])
        grad = grad_normed[row, :]
        result = normal_back(grad * vectors[2:3], unit, scale)
        grad_first[row, :] = result
        first_low[row, :] = result.astype(LOW)
        for j, item in enumerate((result, grad * unit, grad)):
            more[j : j + 1, :] += jnp.sum(item, 0, keepdims=True)
        return 0

    lax.fori_loop(0, slots // 128, norm, 0)
    finish(get_o)
    for k in range(n):
        grad_attn[shard_of(ids, k, n)] = right_dot(first_low[...], wo[k]).astype(LOW)
    small[...] = jnp.zeros_like(small)
    for z in range(n):
        here = pl.ds(z * cols, cols)
        rows = [more[0:1, here]]
        rows += [bias_sum[:, pl.ds(z * deep + j * cols, cols)] for j in range(deep // cols)]
        rows += [sums[2:3, here], more[1:2, here], more[2:3, here], sums[0:1, here], sums[1:2, here]]
        for j, item in enumerate(rows):
            small[z, j : j + 1, :] = item


def finish_hidden(n, pairs, ids, *refs):
    parts, refs = refs[:pairs], refs[pairs:]
    grad_first, wq, wk, wv = refs[:4]
    side, (out, total, held, acts, sems) = refs[4:8], refs[8:]
    slots, width = out.shape
    cols = width // n
    copies = loads(
        ids, [(wq, width), (wk, width), (wv, width)], side, sems, held, cols // (2 * GROUP), 0, 0
    )
    begin(copies)
    for g in range(n):
        for p in range(pairs):
            for j in range(3):
                column = j * width + g * cols + p * PAIR
                acts[:, column : column + PAIR] = parts[p][g, :, j * PAIR : (j + 1) * PAIR]
    finish(copies)
    for k in range(n):
        column = part_of(shard_of(ids, k, n) * cols, cols)
        out[:, column] = right_dot(acts[...], held[k]) + grad_first[:, column]
    block = lax.broadcasted_iota(jnp.int32, (32, 1), 0) < ids[HERE]
    total[...] = jnp.sum(jnp.where(block, out[:32, :], 0.0), 0, keepdims=True)


def outer_product(spec, keep, ids, *refs):
    lefts, rights = [], []
    for count, _ in spec:
        lefts.append(refs[:count])
        rights.append(refs[count : 2 * count])
        refs = refs[2 * count :]
    at = 0
    for (count, cols), left, right in zip(spec, lefts, rights):
        step = min(cols, 1024)
        for col in range(0, cols, step):
            total = left_dot(left[0][...], right[0][:, col : col + step])
            for i in range(1, count):
                total = total + left_dot(left[i][...], right[i][:, col : col + step])
            here = slice(at + col, at + col + step)
            if not keep:
                refs[0][0, :, here] = total.astype(LOW)
                continue
            got, outs = refs[0], refs[1:]
            total = (total + got[0, :, here].astype(WIDE)).astype(LOW)
            split_halves(ids, total, [out.at[0, :, here] for out in outs], (X, Y))
        at += cols


def split_halves(ids, total, outs, bits):
    rows = total.shape[0] // 4
    parts = [total[i * rows : (i + 1) * rows] for i in range(4)]
    for half, bit in enumerate(bits):
        high = ids[bit] == 1
        low_part, high_part = parts[2 * half], parts[2 * half + 1]
        outs[2 * half][...] = jnp.where(high, low_part, high_part)
        outs[2 * half + 1][...] = jnp.where(high, high_part, low_part)


def gradient(order, spec, n, got=None):
    rows = spec[0][0][0][0].shape[1] // (2 * n)
    keep = got is not None
    in_specs, args, total, flops = [], [], 0, 0
    for pairs, cols in spec:
        for left, _ in pairs:
            block = lambda z, ids: (0, 2 * z + (ids[CORE] if keep else 1 - ids[CORE]))
            in_specs.append(pl.BlockSpec((left.shape[0], rows), block))
            args.append(left)
        for _, right in pairs:
            in_specs.append(pl.BlockSpec(right.shape, lambda z, ids: (0, 0)))
            args.append(right)
            flops += 2 * n * rows * right.shape[0] * cols
        total += cols
    if keep:
        in_specs.append(pl.BlockSpec((1, rows, total), lambda z, ids: (z, 0, 0)))
        args.append(got)
    out_rows, count = (rows // 4, 4) if keep else (rows, 1)
    return order.call(
        functools.partial(outer_product, [(len(pairs), cols) for pairs, cols in spec], keep),
        *args,
        grid_spec=pltpu.PrefetchScalarGridSpec(
            num_scalar_prefetch=1,
            grid=(n,),
            in_specs=in_specs,
            out_specs=[pl.BlockSpec((1, out_rows, total), lambda z, ids: (z, 0, 0))] * count,
        ),
        out_shape=[shape(n, out_rows, total)] * count,
        compiler_params=params(),
        cost_estimate=cost(0),
    )


def fold_two(ids, keep_one, got_one, keep_two, got_two, *outs):
    rows = keep_one.shape[1] // 2
    for z in range(keep_one.shape[0]):
        one = (keep_one[z].astype(WIDE) + got_one[z].astype(WIDE)).astype(LOW)
        two = (keep_two[z].astype(WIDE) + got_two[z].astype(WIDE)).astype(LOW)
        for total, bit, (send, keep) in ((one, Y, outs[:2]), (two, X, outs[2:])):
            high = ids[bit] == 1
            send[z] = jnp.where(high, total[:rows], total[rows:])
            keep[z] = jnp.where(high, total[rows:], total[:rows])


def fold_three(ids, keep_one, got_one, keep_two, got_two, out):
    for z in range(out.shape[0]):
        out[z, 0] = (keep_one[z].astype(WIDE) + got_one[z].astype(WIDE)).astype(LOW)
        out[z, 1] = (keep_two[z].astype(WIDE) + got_two[z].astype(WIDE)).astype(LOW)


def fold_four(splits, ids, *refs):
    parts, outs = refs[: len(splits)], refs[len(splits) :]
    for i, (split, terms) in enumerate(zip(splits, parts)):
        n, cols = terms.shape[0], terms.shape[3]
        for h, out in enumerate(outs):
            if split < cols:
                total = terms[0, h, :, split:].astype(WIDE)
                for z in range(1, n):
                    total = total + terms[z, h, :, split:].astype(WIDE)
                out[i, :, n * split :] = total.astype(LOW)
            for z in range(n if split else 0):
                out[i, :, z * split : (z + 1) * split] = terms[z, h, :, :split]


def small_call(order, body, args, outs):
    return order.call(
        body,
        *args,
        in_specs=[SMEM] + [VMEM] * len(args),
        out_specs=[VMEM] * len(outs),
        out_shape=outs,
        compiler_params=params(),
        cost_estimate=cost(0),
    )


def reduce_first(order, spec, n):
    (send,) = gradient(order, spec, n)
    return swap(send, 1)


def reduce_second(order, spec, n, got):
    send_one, keep_one, send_two, keep_two = gradient(order, spec, n, got)
    return keep_one, swap(send_one, 2), keep_two, swap(send_two, 4)


def reduce_third(order, n, held):
    rows, cols = held[0].shape[1:]
    outs = [shape(n, rows // 2, cols)] * 4
    send_one, keep_one, send_two, keep_two = small_call(order, fold_two, held, outs)
    return keep_one, swap(send_one, 4), keep_two, swap(send_two, 2)


def reduce_fourth(order, n, held, send=True):
    rows, cols = held[0].shape[1:]
    (out,) = small_call(order, fold_three, held, [shape(n, 2, rows, cols)])
    return exchange(out) if send else out


def reduce_fifth(order, held, splits):
    n, _, rows, cols = held[0].shape
    outs = [shape(len(held), rows, cols + (n - 1) * splits[0])] * 2
    one, two = small_call(order, functools.partial(fold_four, splits), held, outs)
    mask = GROUP
    while mask < lax.axis_size("dp"):
        one, two = [(v.astype(WIDE) + swap(v, mask).astype(WIDE)).astype(LOW) for v in (one, two)]
        mask *= 2
    return one, two


def place_grad(plan, ids, *refs):
    pieces, outs = refs[:4], refs[4:]
    rows = pieces[0].shape[3]
    for i in range(2 * GROUP):
        piece = piece_of(pieces, i // 2, i % 2)
        home = ids[INDEX] ^ (i // 2)
        core, x, y = home & 1, (home >> 1) & 1, (home >> 2) & 1
        block = core * 8 + (x * 2 + y if i % 2 == 0 else 4 + y * 2 + x)
        row = part_of(block * rows, rows)
        for out, moves in zip(outs, plan):
            for layer, source, target, size in moves:
                value = piece[layer, :, source : source + size]
                out[row, target : target + size] = value.astype(WIDE)


def reduce_last(order, pieces, plan, widths):
    rows = pieces[0].shape[3] * 2 * GROUP
    return small_call(
        order,
        functools.partial(place_grad, plan),
        pieces,
        [shape(rows, width, dtype=WIDE) for width in widths],
    )


def per_device(
    hidden_in,
    cotangent,
    context_len,
    block_device,
    timestep,
    query_weight,
    key_weight,
    value_weight,
    output_weight,
    inner_weight,
    outer_weight,
    query_bias,
    value_bias,
    output_bias,
    inner_bias,
    outer_bias,
    attn_gain,
    attn_shift,
    ffn_gain,
    ffn_shift,
    time_table,
):
    n = lax.axis_size("ctx")
    place = lax.axis_index("ctx")
    d = lax.axis_index("dp") % GROUP
    _, slots, width = hidden_in.shape
    hidden = inner_weight.shape[1]
    cols = width // n
    deep = hidden // n
    pairs = cols // PAIR
    span = (n - 1) * slots + TAIL
    holder = block_device[0]
    context = context_len[0]

    groups = [j + (j >= holder).astype(jnp.int32) for j in range(n - 1)] + [holder]
    position = lambda g: jnp.where(g == holder, n - 1, g - (g > holder).astype(jnp.int32))
    counts = [context // (n - 1) + (j < context % (n - 1)).astype(jnp.int32) for j in range(n - 1)]
    counts = jnp.stack(counts + [jnp.int32(BLOCK)])
    slot = jnp.arange(slots, dtype=jnp.int32)
    live = (slot[None, :] < counts[:, None]).reshape(n * slots)[:span]
    bias = jnp.where(live, 0.0, -1e30).astype(WIDE)
    bias_row, bias_col = bias[None, :], jnp.broadcast_to(bias[:, None], (span, 128))
    owned = lax.dynamic_index_in_dim(counts, position(place), keepdims=False)
    here = jnp.where(holder == place, BLOCK, 0)
    ids = [place, d, d & 1, (d >> 1) & 1, (d >> 2) & 1, owned, here]
    ids += [position(jnp.int32(g)) for g in range(n)] + groups
    order = Order(jnp.stack([jnp.asarray(v, jnp.int32) for v in ids]))
    embed = lax.dynamic_slice_in_dim(time_table, timestep[0], 1, 0).astype(WIDE)
    block = ((holder == place) & (slot < BLOCK)).astype(WIDE)[:, None]
    start = hidden_in[0].astype(WIDE) + block * embed
    start_low = start.astype(LOW)

    def piece(weight):
        part = weight.shape[0] // GROUP
        return lax.dynamic_slice_in_dim(weight, d * part, part, 0).reshape(2, part // 2, -1)

    side_piece = jnp.concatenate(
        [piece(w) for w in (query_weight, key_weight, value_weight, inner_weight)], 2
    )
    tall_piece = jnp.concatenate([piece(output_weight), piece(outer_weight)], 1)
    one, two = one_off(side_piece)
    far = two_off(side_piece)
    order.tick(far)
    on = sent_on(order.release(far))
    tall_far = two_off(order.release(tall_piece))
    order.tick(one, two, on)
    side = by_distance(far, one, two, on)
    side = gather_near(side[:, 0], side[:, 1])
    one, two = one_off(order.release(tall_piece))
    order.tick(tall_far, *side)
    on = sent_on(order.release(tall_far))
    side = gather_far(*side)
    order.tick(one, two, on)
    row_low = exchange(jnp.broadcast_to(order.release(start_low), (n, slots, width)))
    row_low = row_low.reshape(n * slots, width)
    tall = by_distance(tall_far, one, two, on)
    tall = gather_near(tall[:, 0], tall[:, 1])
    order.tick(*side)
    side = gather_cores(*side)
    order.tick(*tall)
    tall = gather_far(*tall)
    vectors = (output_bias, outer_bias, attn_gain, attn_shift, ffn_gain, ffn_shift)
    vectors = jnp.stack([v.astype(WIDE) for v in vectors])
    inner_row = inner_bias.astype(WIDE)[None]
    own_bias = lambda v: lax.dynamic_slice_in_dim(v, place * cols, cols, 0).astype(WIDE)
    qkv_bias = jnp.concatenate([own_bias(query_bias), jnp.zeros((cols,), WIDE), own_bias(value_bias)])
    qkv_bias = qkv_bias[None]
    vectors, inner_row, qkv_bias, bias_row, bias_col, start = lax.optimization_barrier(
        (vectors, inner_row, qkv_bias, bias_row, bias_col, start)
    )
    order.wait(vectors, inner_row, qkv_bias, bias_row, bias_col, start)
    qkv = order.call(
        functools.partial(project, n),
        *(row_low, query_weight, key_weight, value_weight, *side, qkv_bias),
        in_specs=[SMEM] + [VMEM] + [ANY] * 7 + [VMEM],
        out_specs=VMEM,
        out_shape=shape(span, 3 * cols),
        scratch_shapes=[
            pltpu.VMEM((n * slots, width), LOW),
            pltpu.VMEM((n, cols, 3 * cols), LOW),
            pltpu.SemaphoreType.DMA((3 + 6 * GROUP,)),
        ],
        compiler_params=params(),
        cost_estimate=cost(8),
    )

    mixed, lses = [], []
    for pair in range(pairs):
        if pair == 1:
            order.wait(*tall)
            tall = gather_cores(*tall)
        mix, lse = attention(order, qkv, bias_row, pair, pairs, n, slots)
        lses.append(lse)
        if mixed:
            order.tick(mixed[-1])
            mix = order.release(mix)
        mixed.append(exchange(mix))

    held_o = pltpu.VMEM((n, cols, width), LOW)
    held_i = pltpu.VMEM((n, cols, hidden), LOW)
    held_u = pltpu.VMEM((n, deep, width), LOW)
    wide_one = pltpu.VMEM((slots, width), WIDE)
    sem = pltpu.SemaphoreType.DMA((1 + 2 * GROUP,))
    flops = 2 * slots * width * (width + 2 * hidden)
    attn, first, normed_low, active, slope, out, grad_second, second_low, sums = order.call(
        functools.partial(forward, n, pairs),
        *(*mixed, start, cotangent[0], output_weight, inner_weight, outer_weight),
        *(vectors, inner_row, *side, *tall),
        in_specs=[SMEM] + [VMEM] * (pairs + 2) + [ANY] * 3 + [VMEM] * 2 + [ANY] * 8,
        out_specs=[VMEM] * 9,
        out_shape=[
            shape(slots, width),
            shape(slots, width, dtype=WIDE),
            shape(slots, width),
            shape(slots, hidden),
            shape(slots, hidden),
            shape(slots, width),
            shape(slots, width, dtype=WIDE),
            shape(slots, width),
            shape(8, width, dtype=WIDE),
        ],
        scratch_shapes=[
            *(held_o, held_i, held_u, wide_one, wide_one),
            pltpu.VMEM((slots, width), LOW),
            *(sem, sem, sem),
        ],
        compiler_params=params(),
        cost_estimate=cost(24),
    )
    outer_spec = [([(active, second_low)], width)]
    outer_held = reduce_first(order, outer_spec, n)
    inner_low, bias_sum = order.call(
        functools.partial(backward_inner, n),
        *(second_low, slope, outer_weight, *tall),
        in_specs=[SMEM] + [VMEM] * 2 + [ANY] * 5,
        out_specs=[VMEM] * 2,
        out_shape=[shape(slots, hidden), shape(1, hidden, dtype=WIDE)],
        scratch_shapes=[held_u, sem],
        compiler_params=params(),
        cost_estimate=cost(12),
    )
    outer_held = reduce_second(order, outer_spec, n, outer_held)
    inner_spec = [([(normed_low, inner_low)], hidden)]
    inner_held = reduce_first(order, inner_spec, n)
    grad_first, first_low, grad_attn, small = order.call(
        functools.partial(backward, n),
        *(inner_low, bias_sum, grad_second, first, vectors, sums),
        *(output_weight, inner_weight, *side, *tall),
        in_specs=[SMEM] + [VMEM] * 6 + [ANY] * 10,
        out_specs=[VMEM] * 4,
        out_shape=[
            shape(slots, width, dtype=WIDE),
            shape(slots, width),
            shape(n, slots, cols),
            shape(n, 16, cols, dtype=WIDE),
        ],
        scratch_shapes=[held_o, held_i, wide_one, pltpu.VMEM((8, width), WIDE), sem, sem],
        compiler_params=params(),
        cost_estimate=cost(13),
    )
    grad_mixed = exchange(grad_attn)
    outer_held = reduce_third(order, n, outer_held)
    inner_held = reduce_second(order, inner_spec, n, inner_held)
    order.wait(grad_mixed)
    outer_held = reduce_fourth(order, n, outer_held)

    backs, received = [], []
    for pair in range(pairs):
        if pair:
            received.append(exchange(backs[-1]))
            order.wait(outer_held)
            outer_pieces = gather_near(*reduce_fifth(order, [outer_held], [0]))
            inner_held = reduce_third(order, n, inner_held)
        backs.append(
            attention_back(order, qkv, bias_col, grad_mixed, lses[pair], pair, pairs, n, slots)
        )
    order.wait(*received, *inner_held, *outer_pieces)
    received.append(exchange(backs[-1]))
    outer_pieces = gather_far(*order.release(*outer_pieces))
    rest_spec = [([(row_low, back.reshape(n * slots, -1))], 3 * PAIR) for back in backs]
    rest_spec += [([(attn, first_low)], width)]
    rest_held = reduce_first(order, rest_spec, n)
    inner_held = reduce_fourth(order, n, inner_held, False)
    order.wait(*outer_pieces)
    outer_pieces = gather_cores(*order.release(*outer_pieces))
    rest_held = reduce_second(order, rest_spec, n, rest_held)
    order.tick(received[-1])
    inner_held = exchange(order.release(inner_held))
    (outer_grad,) = reduce_last(order, outer_pieces, [[(0, 0, 0, width)]], [width])
    rest_held = reduce_third(order, n, rest_held)
    grad_hidden, block_sum = order.call(
        functools.partial(finish_hidden, n, pairs),
        *(*received, grad_first, query_weight, key_weight, value_weight, *side),
        in_specs=[SMEM] + [VMEM] * (pairs + 1) + [ANY] * 7,
        out_specs=[VMEM] * 2,
        out_shape=[shape(slots, width, dtype=WIDE), shape(1, width, dtype=WIDE)],
        scratch_shapes=[
            pltpu.VMEM((n, cols, 3 * width), LOW),
            pltpu.VMEM((slots, 3 * width), LOW),
            pltpu.SemaphoreType.DMA((3 + 2 * GROUP,)),
        ],
        compiler_params=params(),
        cost_estimate=cost(9),
    )
    order.wait(*rest_held)
    rest_held = reduce_fourth(order, n, rest_held, False)
    order.tick(inner_held)

    packed = jnp.concatenate([small, block_sum.reshape(1, n, cols).repeat(n, 0)], 1)
    total = jnp.sum(exchange(order.release(packed)), 0)
    inner_pieces = gather_near(*reduce_fifth(order, [inner_held], [0]))
    order.tick(total)
    rest_held = exchange(order.release(rest_held))
    used = small.shape[1]
    bias_sums = jnp.stack([jnp.sum(back.astype(WIDE), (0, 1)) for back in backs])
    vector = jnp.concatenate([total[used:], jnp.full((1, cols), timestep[0], WIDE)])[None]
    total = jnp.concatenate([total[:used], bias_sums.reshape(-1, cols)])
    mask = 1
    while mask < lax.axis_size("dp"):
        flat = swap(jnp.concatenate([total, vector.reshape(-1, cols)]), mask)
        total = total + flat[: total.shape[0]]
        vector = jnp.concatenate([vector, flat[total.shape[0] :].reshape(vector.shape)])
        mask *= 2
    order.tick(rest_held, total, vector, *inner_pieces)
    inner_pieces = gather_far(*order.release(*inner_pieces))
    pieces = gather_near(*reduce_fifth(order, [rest_held], [3 * cols]))
    order.tick(*inner_pieces)
    inner_pieces = gather_cores(*order.release(*inner_pieces))
    per = deep // cols
    sums = [total[0], total[1 : 1 + per].reshape(deep)] + [total[1 + per + i] for i in range(5)]
    bias_sums = total[used:].reshape(pairs, 3 * PAIR)
    query_sum = bias_sums[:, :PAIR].reshape(cols)
    value_sum = bias_sums[:, 2 * PAIR :].reshape(cols)
    share = time_table.shape[0] // n
    levels = (jnp.arange(share, dtype=jnp.int32) + place * share).astype(WIDE)
    onehot = (vector[:, n, :1] == levels[None, :]).astype(WIDE)
    time_table_grad = lax.dot_general(
        onehot,
        vector[:, :n].reshape(-1, width),
        (((0,), (0,)), ((), ())),
        precision=lax.Precision.HIGHEST,
        preferred_element_type=WIDE,
    )

    order.wait(*pieces)
    pieces = gather_far(*order.release(*pieces))
    (inner_grad,) = reduce_last(order, inner_pieces, [[(0, 0, 0, hidden)]], [hidden])
    order.wait(*pieces)
    pieces = gather_cores(*order.release(*pieces))
    plan = [
        [
            (0, g * 3 * cols + p * 3 * PAIR + j * PAIR, g * cols + p * PAIR, PAIR)
            for g in range(n)
            for p in range(pairs)
        ]
        for j in range(3)
    ]
    plan += [[(0, n * 3 * cols, 0, width)]]
    *weight_grads, output_grad = reduce_last(order, pieces, plan, [width] * 4)
    return (
        out[None],
        grad_hidden[None],
        *weight_grads,
        output_grad,
        inner_grad,
        outer_grad,
        query_sum,
        value_sum,
        *sums,
        time_table_grad,
    )


def solution(mesh):
    row, shard, same = P("dp", "ctx", None), P("ctx", None), P()
    return jax.shard_map(
        per_device,
        mesh=mesh,
        in_specs=(row, row, P("dp"), P("dp"), P("dp")) + (shard,) * 6 + (same,) * 10,
        out_specs=(row, row) + (shard,) * 6 + (P("ctx"),) * 9 + (shard,),
        check_vma=False,
    )
```

```python
import functools
import math

import jax
import jax.numpy as jnp
from jax import lax
from jax.experimental import pallas as pl
from jax.experimental.pallas import tpu as pltpu
from jax.sharding import PartitionSpec as P

HEADS = 16
HD = 64
BLOCK = 25
EPSILON = 1e-05
GROUP = 8
TAIL = 128
FEW = 32
PAIR = 2 * HD
STEP = 512
FACTOR = 16
LOG2E = 1.4426950408889634
LOW = jnp.bfloat16
WIDE = jnp.float32
VMEM = pl.BlockSpec(memory_space=pltpu.VMEM)
SMEM = pl.BlockSpec(memory_space=pltpu.SMEM)
ANY = pl.BlockSpec(memory_space=pl.ANY)
PLACE, INDEX, CORE, X, Y, OWNED, HERE, LISTS = range(8)


def params(mib=56):
    return pltpu.CompilerParams(vmem_limit_bytes=mib << 20)


def cost(us):
    us = us * FACTOR
    return pl.CostEstimate(flops=int(us * 1e9), bytes_accessed=int(us * 3e6), transcendentals=0)


def shape(*dims, dtype=LOW):
    return jax.ShapeDtypeStruct(dims, dtype)


def dot(left, right, dims=((1,), (0,))):
    return lax.dot_general(left, right, (dims, ((), ())), preferred_element_type=WIDE)


def left_dot(left, right):
    return dot(left, right, ((0,), (0,)))


def right_dot(left, right):
    return dot(left, right, ((1,), (1,)))


def part_of(start, size):
    return pl.ds(pl.multiple_of(start, size), size)


def swap(value, mask):
    size = lax.axis_size("dp")
    return lax.ppermute(value, "dp", [(i, i ^ mask) for i in range(size)])


def along(value, *pairs):
    return lax.ppermute(value, "ctx", pairs)


def exchange(value, axis="ctx"):
    return lax.all_to_all(value, axis, 0, 0)


def after(value, *others):
    return lax.optimization_barrier((value, *others))[0]


def two_off(value):
    return along(value, (0, 2), (1, 3), (2, 0), (3, 1))


def one_off(value):
    return along(value, (0, 1), (1, 2), (2, 3)), along(value, (1, 0), (2, 1), (3, 2))


def sent_on(far):
    return along(far, (2, 3), (1, 0))


def by_distance(far, up, down, on):
    place = lax.axis_index("ctx")
    return jnp.stack([jnp.where(place == 0, on, up), far, jnp.where(place == 3, on, down)])


def copy_numbers(ids, out):
    for i in range(ids.shape[0]):
        out[i] = ids[i]


class Order:
    def __init__(self, ids):
        self.ids = ids

    def call(self, body, *args, **kwargs):
        outs = pl.pallas_call(body, **kwargs)(self.ids, *args)
        self.wait(outs[0] if isinstance(outs, (list, tuple)) else outs)
        return outs

    def wait(self, *values):
        self.ids = after(self.ids, *values)

    def tick(self, *values):
        self.wait(*values)
        self.call(
            copy_numbers,
            in_specs=[SMEM],
            out_specs=SMEM,
            out_shape=jax.ShapeDtypeStruct(self.ids.shape, jnp.int32),
            cost_estimate=cost(0),
        )

    def release(self, *values):
        outs = lax.optimization_barrier((*values, self.ids))[:-1]
        return outs if len(outs) > 1 else outs[0]


def gather_near(one, two):
    return jnp.stack([one, swap(one, 2)]), jnp.stack([two, swap(two, 4)])


def gather_far(one, two):
    return jnp.stack([one, swap(one, 4)]), jnp.stack([two, swap(two, 2)])


def gather_cores(one, two):
    return one, two, swap(one, 1), swap(two, 1)


def piece_of(arrays, mask, half):
    x, y = (mask >> 1) & 1, (mask >> 2) & 1
    return arrays[2 * (mask & 1) + half].at[(x, y) if half else (y, x)]


def loads(ids, own, pieces, sems, held, rows, row, col):
    n, _, cols = held.shape
    copies = []
    at = 0
    for ref, width in own:
        copies.append(
            pltpu.make_async_copy(ref, held.at[0, :, pl.ds(at, width)], sems.at[len(copies)])
        )
        at += width
    for i in range(2 * GROUP):
        where = ((ids[INDEX] ^ (i // 2)) * 2 + i % 2) * rows
        piece = piece_of(pieces, i // 2, i % 2)
        copies.append(
            pltpu.make_async_copy(
                piece.at[:, pl.ds(row, rows), pl.ds(col, cols)],
                held.at[pl.ds(1, n - 1), part_of(where, rows), :],
                sems.at[len(copies)],
            )
        )
    return copies


def begin(copies):
    for copy in copies:
        copy.start()


def finish(copies):
    for copy in copies:
        copy.wait()


def shard_of(ids, k, n):
    return lax.rem(ids[PLACE] + n - k, n)


def project(n, ids, *refs):
    row_ref, wq, wk, wv = refs[:4]
    refs = refs[4:]
    pieces, (bias, out, compact, held, sems) = refs[:4], refs[4:]
    width = row_ref.shape[1]
    slots = row_ref.shape[0] // n
    cols = width // n
    rows = pieces[0].shape[3]
    copies = []
    for j, own in enumerate((wq, wk, wv)):
        copies.append(
            pltpu.make_async_copy(
                own.at[:, part_of(ids[PLACE] * cols, cols)],
                held.at[0, :, pl.ds(j * cols, cols)],
                sems.at[len(copies)],
            )
        )
        for i in range(2 * GROUP):
            where = ((ids[INDEX] ^ (i // 2)) * 2 + i % 2) * rows
            piece = piece_of(pieces, i // 2, i % 2)
            copies.append(
                pltpu.make_async_copy(
                    piece.at[:, :, part_of(j * width + ids[PLACE] * cols, cols)],
                    held.at[pl.ds(1, n - 1), part_of(where, rows), pl.ds(j * cols, cols)],
                    sems.at[len(copies)],
                )
            )
    begin(copies)
    for g in range(n):
        compact[part_of(ids[LISTS + g] * slots, slots), :] = row_ref[g * slots : (g + 1) * slots, :]
    finish(copies)

    def block(i, _):
        row = part_of(i * 256, 256)
        total = bias[...]
        for k in range(n):
            column = part_of(shard_of(ids, k, n) * cols, cols)
            total = total + dot(compact[row, column], held[k])
        out[row, :] = total.astype(LOW)
        return 0

    lax.fori_loop(0, out.shape[0] // 256, block, 0)


def attend(n, ids, bias_ref, q_ref, k_ref, v_ref, *refs):
    out_ref, lse_ref = refs
    tile = pl.program_id(0)
    slots = q_ref.shape[0]
    first = lax.broadcasted_iota(jnp.int32, (1, PAIR), 1) < HD

    def work(rows):
        query = q_ref[:rows, :]
        keys, values = k_ref[...], v_ref[...]
        mixed = []
        for h in range(2):
            mine = first if h == 0 else jnp.logical_not(first)
            scores = right_dot(jnp.where(mine, query, 0), keys)
            scores = scores * (LOG2E / math.sqrt(HD)) + bias_ref[...]
            high = jnp.max(scores, -1, keepdims=True)
            expo = jnp.exp2(scores - high)
            total = jnp.sum(expo, -1, keepdims=True)
            probs = (expo * (1.0 / total)).astype(LOW)
            mixed.append(dot(probs, values))
            lse = jnp.broadcast_to(high + jnp.log2(total), (rows, 128))
            lse_ref[h : h + 1, :rows] = lse.T[:1, :]
        out_ref[0, :rows, :] = jnp.where(first, mixed[0], mixed[1]).astype(LOW)
        if rows < slots:
            out_ref[0, rows:, :] = jnp.zeros((slots - rows, PAIR), LOW)

    @pl.when(tile < n - 1)
    def _():
        work(slots)

    @pl.when(tile == n - 1)
    def _():
        work(TAIL)
        lse_ref[:, TAIL:] = jnp.zeros((8, slots - TAIL), WIDE)


def attention(order, qkv, bias, pair, pairs, n, slots):
    span = qkv.shape[0]
    whole = lambda col: pl.BlockSpec((span, PAIR), lambda t, ids: (0, col))
    return order.call(
        functools.partial(attend, n),
        *(bias, qkv, qkv, qkv),
        grid_spec=pltpu.PrefetchScalarGridSpec(
            num_scalar_prefetch=1,
            grid=(n,),
            in_specs=[
                pl.BlockSpec((1, span), lambda t, ids: (0, 0)),
                pl.BlockSpec((slots, PAIR), lambda t, ids: (t, pair)),
                whole(pairs + pair),
                whole(2 * pairs + pair),
            ],
            out_specs=[
                pl.BlockSpec((1, slots, PAIR), lambda t, ids: (ids[LISTS + n + t], 0, 0)),
                pl.BlockSpec((8, slots), lambda t, ids: (0, t)),
            ],
        ),
        out_shape=[shape(n, slots, PAIR), shape(8, n * slots, dtype=WIDE)],
        compiler_params=params(),
        cost_estimate=cost(11),
    )


def attend_back(n, ids, bias_ref, q_ref, k_ref, v_ref, *refs):
    grad_ref, lse_ref, out_ref, do_ref, dk_ref, dv_ref = refs
    tile = pl.program_id(0)
    slots = q_ref.shape[0]
    span = k_ref.shape[0] - TAIL + FEW
    first = lax.broadcasted_iota(jnp.int32, (1, PAIR), 1) < HD
    scale = 1.0 / math.sqrt(HD)

    @pl.when(tile == 0)
    def _():
        dk_ref[...] = jnp.zeros_like(dk_ref)
        dv_ref[...] = jnp.zeros_like(dv_ref)
        for g in range(n):
            do_ref[part_of(ids[LISTS + g] * slots, slots), :] = grad_ref[g]

    def work(rows):
        keys, values = k_ref[:span, :], v_ref[:span, :]
        here = pl.ds(pl.multiple_of(tile * slots, slots), rows)
        parts = []
        for h in range(2):
            mine = first if h == 0 else jnp.logical_not(first)
            query = jnp.where(mine, q_ref[:rows, :], 0)
            grad = jnp.where(mine, do_ref[here, :], 0)
            scores = right_dot(keys, query) * (LOG2E * scale)
            bias = jnp.concatenate([bias_ref[:span, :]] * (rows // 128), 1)
            probs = jnp.exp2(scores + bias - lse_ref[h : h + 1, :rows])
            grad_probs = right_dot(values, grad)
            center = jnp.sum(grad_probs * probs, 0, keepdims=True)
            grad_scores = (probs * (grad_probs - center)).astype(LOW)
            dk_ref[:span, :] += dot(grad_scores, query)
            dv_ref[:span, :] += dot(probs.astype(LOW), grad)
            parts.append(left_dot(grad_scores, keys))
        group = ids[LISTS + n + tile]
        out_ref[group, :rows, :PAIR] = (jnp.where(first, parts[0], parts[1]) * scale).astype(LOW)
        if rows < slots:
            out_ref[group, rows:, :PAIR] = jnp.zeros((slots - rows, PAIR), LOW)

    @pl.when(tile < n - 1)
    def _():
        work(slots)

    @pl.when(tile == n - 1)
    def _():
        work(TAIL)
        for g in range(n):
            here = part_of(ids[LISTS + g] * slots, slots)
            out_ref[g, :, PAIR : 2 * PAIR] = (dk_ref[here, :] * scale).astype(LOW)
            out_ref[g, :, 2 * PAIR :] = dv_ref[here, :].astype(LOW)


def attention_back(order, qkv, bias, grad, lse, pair, pairs, n, slots):
    span = qkv.shape[0]
    whole = lambda col: pl.BlockSpec((span, PAIR), lambda t, ids: (0, col))
    return order.call(
        functools.partial(attend_back, n),
        *(bias, qkv, qkv, qkv, grad, lse),
        grid_spec=pltpu.PrefetchScalarGridSpec(
            num_scalar_prefetch=1,
            grid=(n,),
            in_specs=[
                pl.BlockSpec((span, 128), lambda t, ids: (0, 0)),
                pl.BlockSpec((slots, PAIR), lambda t, ids: (t, pair)),
                whole(pairs + pair),
                whole(2 * pairs + pair),
                pl.BlockSpec((n, slots, PAIR), lambda t, ids: (0, 0, pair)),
                pl.BlockSpec((8, slots), lambda t, ids: (0, t)),
            ],
            out_specs=pl.BlockSpec((n, slots, 3 * PAIR), lambda t, ids: (0, 0, 0)),
            scratch_shapes=[
                pltpu.VMEM((n * slots, PAIR), LOW),
                pltpu.VMEM((n * slots, PAIR), WIDE),
                pltpu.VMEM((n * slots, PAIR), WIDE),
            ],
        ),
        out_shape=shape(n, slots, 3 * PAIR),
        compiler_params=params(),
        cost_estimate=cost(16),
    )


def normal(values):
    center = values - jnp.mean(values, -1, keepdims=True)
    scale = lax.rsqrt(jnp.mean(center * center, -1, keepdims=True) + EPSILON)
    return center * scale, scale


def normal_back(grad, unit, scale):
    inner = jnp.mean(grad * unit, -1, keepdims=True)
    return (grad - jnp.mean(grad, -1, keepdims=True) - unit * inner) * scale


def forward(n, pairs, ids, *refs):
    parts, refs = refs[:pairs], refs[pairs:]
    start, cotangent, wo_own, wi_own, wu_own = refs[:5]
    vectors, bi = refs[5:7]
    bo, bu, gain1, shift1, gain2, shift2 = [vectors.at[i : i + 1] for i in range(6)]
    refs = refs[7:]
    side, tall, refs = refs[:4], refs[4:8], refs[8:]
    attn, first, normed_low, active, slope, out, grad_second, second_low, sums = refs[:9]
    wo, wi, wu, normed, second, ordered, sem_o, sem_i, sem_u = refs[9:]
    slots, width = start.shape
    cols = width // n
    hidden = active.shape[1]
    deep = hidden // n
    row_o, row_u = cols // (2 * GROUP), deep // (2 * GROUP)
    get_o = loads(ids, [(wo_own, width)], tall, sem_o, wo, row_o, 0, 0)
    get_i = loads(ids, [(wi_own, hidden)], side, sem_i, wi, row_o, 0, 3 * width)
    get_u = loads(ids, [(wu_own, width)], tall, sem_u, wu, row_u, row_o, 0)
    begin(get_o)
    begin(get_i)
    begin(get_u)
    for g in range(n):
        for p in range(pairs):
            attn[:, pl.ds(g * cols + p * PAIR, PAIR)] = parts[p][g]

    def put_in_order(ref):
        for k in range(n):
            ordered[:, k * cols : (k + 1) * cols] = ref[:, part_of(shard_of(ids, k, n) * cols, cols)]

    put_in_order(attn)
    finish(get_o)

    def mix(j, _):
        column = part_of(j * STEP, STEP)
        total = dot(ordered[...], wo[:, :, column].reshape(width, STEP))
        first[:, column] = total + start[:, column] + bo[:, column]
        return 0

    lax.fori_loop(0, width // STEP, mix, 0)

    def norm(i, _):
        row = part_of(i * 128, 128)
        unit, _ = normal(first[row, :])
        value = unit * gain1[...] + shift1[...]
        normed[row, :] = value
        normed_low[row, :] = value.astype(LOW)
        return 0

    lax.fori_loop(0, slots // 128, norm, 0)
    put_in_order(normed_low)
    finish(get_i)

    def expand(j, _):
        column = part_of(j * STEP, STEP)
        x = dot(ordered[...], wi[:, :, column].reshape(width, STEP)) + bi[:, column]
        factor = math.sqrt(2 / math.pi)
        square = x * x
        t = jnp.tanh(factor * x * (1.0 + 0.044715 * square))
        half = 0.5 * (1.0 + t)
        active[:, column] = (x * half).astype(LOW)
        steep = half + (0.5 * factor) * x * (1.0 - t * t) * (1.0 + 0.134145 * square)
        slope[:, column] = steep.astype(LOW)
        return 0

    lax.fori_loop(0, hidden // STEP, expand, 0)
    finish(get_u)

    def contract(j, _):
        column = part_of(j * STEP, STEP)
        total = normed[:, column] + bu[:, column]
        for k in range(n):
            left = active[:, part_of(shard_of(ids, k, n) * deep, deep)]
            total = total + dot(left, wu[k, :, column])
        second[:, column] = total
        return 0

    lax.fori_loop(0, width // STEP, contract, 0)
    sums[...] = jnp.zeros_like(sums)

    def last(i, _):
        row = part_of(i * 128, 128)
        live = lax.broadcasted_iota(jnp.int32, (128, 1), 0) + i * 128 < ids[OWNED]
        live = live.astype(WIDE)
        unit, scale = normal(second[row, :])
        out[row, :] = ((unit * gain2[...] + shift2[...]) * live).astype(LOW)
        grad = cotangent[row, :].astype(WIDE) * live
        result = normal_back(grad * gain2[...], unit, scale)
        grad_second[row, :] = result
        second_low[row, :] = result.astype(LOW)
        for j, item in enumerate((grad * unit, grad, result)):
            sums[j : j + 1, :] += jnp.sum(item, 0, keepdims=True)
        return 0

    lax.fori_loop(0, slots // 128, last, 0)


def backward_inner(n, ids, *refs):
    second_low, slope, wu_own = refs[:3]
    tall, (inner_low, bias_sum, wu, sem_u) = refs[3:7], refs[7:]
    hidden = slope.shape[1]
    deep, cols = hidden // n, second_low.shape[1] // n
    row_o, row_u = cols // (2 * GROUP), deep // (2 * GROUP)
    get_u = loads(ids, [(wu_own, second_low.shape[1])], tall, sem_u, wu, row_u, row_o, 0)
    begin(get_u)
    finish(get_u)

    def expand(j, _):
        for k in range(n):
            column = part_of(shard_of(ids, k, n) * deep + j * STEP, STEP)
            grad = right_dot(second_low[...], wu[k, part_of(j * STEP, STEP), :])
            value = (grad * slope[:, column].astype(WIDE)).astype(LOW)
            inner_low[:, column] = value
            bias_sum[:, column] = jnp.sum(value.astype(WIDE), 0, keepdims=True)
        return 0

    lax.fori_loop(0, deep // STEP, expand, 0)


def backward(n, ids, *refs):
    inner_low, bias_sum, grad_second, first, vectors, sums, wo_own, wi_own = refs[:8]
    side, tall, refs = refs[8:12], refs[12:16], refs[16:]
    grad_first, first_low = refs[:2]
    grad_attn, small = refs[2:4]
    wo, wi, grad_normed, more, sem_o, sem_i = refs[4:]
    slots, width = first.shape
    cols = width // n
    hidden = inner_low.shape[1]
    deep = hidden // n
    row_o = cols // (2 * GROUP)
    get_o = loads(ids, [(wo_own, width)], tall, sem_o, wo, row_o, 0, 0)
    get_i = loads(ids, [(wi_own, hidden)], side, sem_i, wi, row_o, 0, 3 * width)
    begin(get_i)
    begin(get_o)
    finish(get_i)
    for k in range(n):
        column = part_of(shard_of(ids, k, n) * cols, cols)
        grad_normed[:, column] = right_dot(inner_low[...], wi[k]) + grad_second[:, column]
    more[...] = jnp.zeros_like(more)

    def norm(i, _):
        row = part_of(i * 128, 128)
        unit, scale = normal(first[row, :])
        grad = grad_normed[row, :]
        result = normal_back(grad * vectors[2:3], unit, scale)
        grad_first[row, :] = result
        first_low[row, :] = result.astype(LOW)
        for j, item in enumerate((result, grad * unit, grad)):
            more[j : j + 1, :] += jnp.sum(item, 0, keepdims=True)
        return 0

    lax.fori_loop(0, slots // 128, norm, 0)
    finish(get_o)
    for k in range(n):
        grad_attn[shard_of(ids, k, n)] = right_dot(first_low[...], wo[k]).astype(LOW)
    small[...] = jnp.zeros_like(small)
    for z in range(n):
        here = pl.ds(z * cols, cols)
        rows = [more[0:1, here]]
        rows += [bias_sum[:, pl.ds(z * deep + j * cols, cols)] for j in range(deep // cols)]
        rows += [sums[2:3, here], more[1:2, here], more[2:3, here], sums[0:1, here], sums[1:2, here]]
        for j, item in enumerate(rows):
            small[z, j : j + 1, :] = item


def finish_hidden(n, pairs, ids, *refs):
    parts, refs = refs[:pairs], refs[pairs:]
    grad_first, wq, wk, wv = refs[:4]
    side, (out, total, held, acts, sems) = refs[4:8], refs[8:]
    slots, width = out.shape
    cols = width // n
    copies = loads(
        ids, [(wq, width), (wk, width), (wv, width)], side, sems, held, cols // (2 * GROUP), 0, 0
    )
    begin(copies)
    for g in range(n):
        for p in range(pairs):
            for j in range(3):
                column = j * width + g * cols + p * PAIR
                acts[:, column : column + PAIR] = parts[p][g, :, j * PAIR : (j + 1) * PAIR]
    finish(copies)
    for k in range(n):
        column = part_of(shard_of(ids, k, n) * cols, cols)
        out[:, column] = right_dot(acts[...], held[k]) + grad_first[:, column]
    block = lax.broadcasted_iota(jnp.int32, (32, 1), 0) < ids[HERE]
    total[...] = jnp.sum(jnp.where(block, out[:32, :], 0.0), 0, keepdims=True)


def outer_product(spec, keep, ids, *refs):
    lefts, rights = [], []
    for count, _ in spec:
        lefts.append(refs[:count])
        rights.append(refs[count : 2 * count])
        refs = refs[2 * count :]
    at = 0
    for (count, cols), left, right in zip(spec, lefts, rights):
        step = min(cols, 1024)
        for col in range(0, cols, step):
            total = left_dot(left[0][...], right[0][:, col : col + step])
            for i in range(1, count):
                total = total + left_dot(left[i][...], right[i][:, col : col + step])
            here = slice(at + col, at + col + step)
            if not keep:
                refs[0][0, :, here] = total.astype(LOW)
                continue
            got, outs = refs[0], refs[1:]
            total = (total + got[0, :, here].astype(WIDE)).astype(LOW)
            split_halves(ids, total, [out.at[0, :, here] for out in outs], (X, Y))
        at += cols


def split_halves(ids, total, outs, bits):
    rows = total.shape[0] // 4
    parts = [total[i * rows : (i + 1) * rows] for i in range(4)]
    for half, bit in enumerate(bits):
        high = ids[bit] == 1
        low_part, high_part = parts[2 * half], parts[2 * half + 1]
        outs[2 * half][...] = jnp.where(high, low_part, high_part)
        outs[2 * half + 1][...] = jnp.where(high, high_part, low_part)


def gradient(order, spec, n, got=None):
    rows = spec[0][0][0][0].shape[1] // (2 * n)
    keep = got is not None
    in_specs, args, total, flops = [], [], 0, 0
    for pairs, cols in spec:
        for left, _ in pairs:
            block = lambda z, ids: (0, 2 * z + (ids[CORE] if keep else 1 - ids[CORE]))
            in_specs.append(pl.BlockSpec((left.shape[0], rows), block))
            args.append(left)
        for _, right in pairs:
            in_specs.append(pl.BlockSpec(right.shape, lambda z, ids: (0, 0)))
            args.append(right)
            flops += 2 * n * rows * right.shape[0] * cols
        total += cols
    if keep:
        in_specs.append(pl.BlockSpec((1, rows, total), lambda z, ids: (z, 0, 0)))
        args.append(got)
    out_rows, count = (rows // 4, 4) if keep else (rows, 1)
    return order.call(
        functools.partial(outer_product, [(len(pairs), cols) for pairs, cols in spec], keep),
        *args,
        grid_spec=pltpu.PrefetchScalarGridSpec(
            num_scalar_prefetch=1,
            grid=(n,),
            in_specs=in_specs,
            out_specs=[pl.BlockSpec((1, out_rows, total), lambda z, ids: (z, 0, 0))] * count,
        ),
        out_shape=[shape(n, out_rows, total)] * count,
        compiler_params=params(),
        cost_estimate=cost(0),
    )


def fold_two(ids, keep_one, got_one, keep_two, got_two, *outs):
    rows = keep_one.shape[1] // 2
    for z in range(keep_one.shape[0]):
        one = (keep_one[z].astype(WIDE) + got_one[z].astype(WIDE)).astype(LOW)
        two = (keep_two[z].astype(WIDE) + got_two[z].astype(WIDE)).astype(LOW)
        for total, bit, (send, keep) in ((one, Y, outs[:2]), (two, X, outs[2:])):
            high = ids[bit] == 1
            send[z] = jnp.where(high, total[:rows], total[rows:])
            keep[z] = jnp.where(high, total[rows:], total[:rows])


def fold_three(ids, keep_one, got_one, keep_two, got_two, out):
    for z in range(out.shape[0]):
        out[z, 0] = (keep_one[z].astype(WIDE) + got_one[z].astype(WIDE)).astype(LOW)
        out[z, 1] = (keep_two[z].astype(WIDE) + got_two[z].astype(WIDE)).astype(LOW)


def fold_four(splits, ids, *refs):
    parts, outs = refs[: len(splits)], refs[len(splits) :]
    for i, (split, terms) in enumerate(zip(splits, parts)):
        n, cols = terms.shape[0], terms.shape[3]
        for h, out in enumerate(outs):
            if split < cols:
                total = terms[0, h, :, split:].astype(WIDE)
                for z in range(1, n):
                    total = total + terms[z, h, :, split:].astype(WIDE)
                out[i, :, n * split :] = total.astype(LOW)
            for z in range(n if split else 0):
                out[i, :, z * split : (z + 1) * split] = terms[z, h, :, :split]


def small_call(order, body, args, outs):
    return order.call(
        body,
        *args,
        in_specs=[SMEM] + [VMEM] * len(args),
        out_specs=[VMEM] * len(outs),
        out_shape=outs,
        compiler_params=params(),
        cost_estimate=cost(0),
    )


def reduce_first(order, spec, n):
    (send,) = gradient(order, spec, n)
    return swap(send, 1)


def reduce_second(order, spec, n, got):
    send_one, keep_one, send_two, keep_two = gradient(order, spec, n, got)
    return keep_one, swap(send_one, 2), keep_two, swap(send_two, 4)


def reduce_third(order, n, held):
    rows, cols = held[0].shape[1:]
    outs = [shape(n, rows // 2, cols)] * 4
    send_one, keep_one, send_two, keep_two = small_call(order, fold_two, held, outs)
    return keep_one, swap(send_one, 4), keep_two, swap(send_two, 2)


def reduce_fourth(order, n, held, send=True):
    rows, cols = held[0].shape[1:]
    (out,) = small_call(order, fold_three, held, [shape(n, 2, rows, cols)])
    return exchange(out) if send else out


def reduce_fifth(order, held, splits):
    n, _, rows, cols = held[0].shape
    outs = [shape(len(held), rows, cols + (n - 1) * splits[0])] * 2
    one, two = small_call(order, functools.partial(fold_four, splits), held, outs)
    mask = GROUP
    while mask < lax.axis_size("dp"):
        one, two = [(v.astype(WIDE) + swap(v, mask).astype(WIDE)).astype(LOW) for v in (one, two)]
        mask *= 2
    return one, two


def place_grad(plan, ids, *refs):
    pieces, outs = refs[:4], refs[4:]
    rows = pieces[0].shape[3]
    for i in range(2 * GROUP):
        piece = piece_of(pieces, i // 2, i % 2)
        home = ids[INDEX] ^ (i // 2)
        core, x, y = home & 1, (home >> 1) & 1, (home >> 2) & 1
        block = core * 8 + (x * 2 + y if i % 2 == 0 else 4 + y * 2 + x)
        row = part_of(block * rows, rows)
        for out, moves in zip(outs, plan):
            for layer, source, target, size in moves:
                value = piece[layer, :, source : source + size]
                out[row, target : target + size] = value.astype(WIDE)


def reduce_last(order, pieces, plan, widths):
    rows = pieces[0].shape[3] * 2 * GROUP
    return small_call(
        order,
        functools.partial(place_grad, plan),
        pieces,
        [shape(rows, width, dtype=WIDE) for width in widths],
    )


def per_device(
    hidden_in,
    cotangent,
    context_len,
    block_device,
    timestep,
    query_weight,
    key_weight,
    value_weight,
    output_weight,
    inner_weight,
    outer_weight,
    query_bias,
    value_bias,
    output_bias,
    inner_bias,
    outer_bias,
    attn_gain,
    attn_shift,
    ffn_gain,
    ffn_shift,
    time_table,
):
    n = lax.axis_size("ctx")
    place = lax.axis_index("ctx")
    d = lax.axis_index("dp") % GROUP
    _, slots, width = hidden_in.shape
    hidden = inner_weight.shape[1]
    cols = width // n
    deep = hidden // n
    pairs = cols // PAIR
    span = (n - 1) * slots + TAIL
    holder = block_device[0]
    context = context_len[0]

    groups = [j + (j >= holder).astype(jnp.int32) for j in range(n - 1)] + [holder]
    position = lambda g: jnp.where(g == holder, n - 1, g - (g > holder).astype(jnp.int32))
    counts = [context // (n - 1) + (j < context % (n - 1)).astype(jnp.int32) for j in range(n - 1)]
    counts = jnp.stack(counts + [jnp.int32(BLOCK)])
    slot = jnp.arange(slots, dtype=jnp.int32)
    live = (slot[None, :] < counts[:, None]).reshape(n * slots)[:span]
    bias = jnp.where(live, 0.0, -1e30).astype(WIDE)
    bias_row, bias_col = bias[None, :], jnp.broadcast_to(bias[:, None], (span, 128))
    owned = lax.dynamic_index_in_dim(counts, position(place), keepdims=False)
    here = jnp.where(holder == place, BLOCK, 0)
    ids = [place, d, d & 1, (d >> 1) & 1, (d >> 2) & 1, owned, here]
    ids += [position(jnp.int32(g)) for g in range(n)] + groups
    order = Order(jnp.stack([jnp.asarray(v, jnp.int32) for v in ids]))
    embed = lax.dynamic_slice_in_dim(time_table, timestep[0], 1, 0).astype(WIDE)
    block = ((holder == place) & (slot < BLOCK)).astype(WIDE)[:, None]
    start = hidden_in[0].astype(WIDE) + block * embed
    start_low = start.astype(LOW)

    def piece(weight):
        part = weight.shape[0] // GROUP
        return lax.dynamic_slice_in_dim(weight, d * part, part, 0).reshape(2, part // 2, -1)

    side_piece = jnp.concatenate(
        [piece(w) for w in (query_weight, key_weight, value_weight, inner_weight)], 2
    )
    tall_piece = jnp.concatenate([piece(output_weight), piece(outer_weight)], 1)
    one, two = one_off(side_piece)
    far = two_off(side_piece)
    copies = jnp.broadcast_to(start_low, (n, slots, width))
    order.tick(far, copies)
    on = sent_on(order.release(far))
    tall_far = two_off(order.release(tall_piece))
    order.tick(one, two, on)
    side = by_distance(far, one, two, on)
    side = gather_near(side[:, 0], side[:, 1])
    one, two = one_off(order.release(tall_piece))
    order.tick(tall_far, *side)
    on = sent_on(order.release(tall_far))
    side = gather_far(*side)
    order.tick(one, two, on)
    row_low = exchange(order.release(copies))
    row_low = row_low.reshape(n * slots, width)
    tall = by_distance(tall_far, one, two, on)
    tall = gather_near(tall[:, 0], tall[:, 1])
    order.tick(*side)
    side = gather_cores(*side)
    order.tick(*tall)
    tall = gather_far(*tall)
    vectors = (output_bias, outer_bias, attn_gain, attn_shift, ffn_gain, ffn_shift)
    vectors = jnp.stack([v.astype(WIDE) for v in vectors])
    inner_row = inner_bias.astype(WIDE)[None]
    own_bias = lambda v: lax.dynamic_slice_in_dim(v, place * cols, cols, 0).astype(WIDE)
    qkv_bias = jnp.concatenate([own_bias(query_bias), jnp.zeros((cols,), WIDE), own_bias(value_bias)])
    qkv_bias = qkv_bias[None]
    vectors, inner_row, qkv_bias, bias_row, bias_col, start = lax.optimization_barrier(
        (vectors, inner_row, qkv_bias, bias_row, bias_col, start)
    )
    order.wait(vectors, inner_row, qkv_bias, bias_row, bias_col, start)
    qkv = order.call(
        functools.partial(project, n),
        *(row_low, query_weight, key_weight, value_weight, *side, qkv_bias),
        in_specs=[SMEM] + [VMEM] + [ANY] * 7 + [VMEM],
        out_specs=VMEM,
        out_shape=shape(span, 3 * cols),
        scratch_shapes=[
            pltpu.VMEM((n * slots, width), LOW),
            pltpu.VMEM((n, cols, 3 * cols), LOW),
            pltpu.SemaphoreType.DMA((3 + 6 * GROUP,)),
        ],
        compiler_params=params(),
        cost_estimate=cost(8),
    )

    mixed, lses = [], []
    for pair in range(pairs):
        if pair == 1:
            order.wait(*tall)
            tall = gather_cores(*tall)
        mix, lse = attention(order, qkv, bias_row, pair, pairs, n, slots)
        lses.append(lse)
        if mixed:
            order.tick(mixed[-1])
            mix = order.release(mix)
        mixed.append(exchange(mix))

    held_o = pltpu.VMEM((n, cols, width), LOW)
    held_i = pltpu.VMEM((n, cols, hidden), LOW)
    held_u = pltpu.VMEM((n, deep, width), LOW)
    wide_one = pltpu.VMEM((slots, width), WIDE)
    sem = pltpu.SemaphoreType.DMA((1 + 2 * GROUP,))
    flops = 2 * slots * width * (width + 2 * hidden)
    attn, first, normed_low, active, slope, out, grad_second, second_low, sums = order.call(
        functools.partial(forward, n, pairs),
        *(*mixed, start, cotangent[0], output_weight, inner_weight, outer_weight),
        *(vectors, inner_row, *side, *tall),
        in_specs=[SMEM] + [VMEM] * (pairs + 2) + [ANY] * 3 + [VMEM] * 2 + [ANY] * 8,
        out_specs=[VMEM] * 9,
        out_shape=[
            shape(slots, width),
            shape(slots, width, dtype=WIDE),
            shape(slots, width),
            shape(slots, hidden),
            shape(slots, hidden),
            shape(slots, width),
            shape(slots, width, dtype=WIDE),
            shape(slots, width),
            shape(8, width, dtype=WIDE),
        ],
        scratch_shapes=[
            *(held_o, held_i, held_u, wide_one, wide_one),
            pltpu.VMEM((slots, width), LOW),
            *(sem, sem, sem),
        ],
        compiler_params=params(),
        cost_estimate=cost(24),
    )
    outer_spec = [([(active, second_low)], width)]
    outer_held = reduce_first(order, outer_spec, n)
    inner_low, bias_sum = order.call(
        functools.partial(backward_inner, n),
        *(second_low, slope, outer_weight, *tall),
        in_specs=[SMEM] + [VMEM] * 2 + [ANY] * 5,
        out_specs=[VMEM] * 2,
        out_shape=[shape(slots, hidden), shape(1, hidden, dtype=WIDE)],
        scratch_shapes=[held_u, sem],
        compiler_params=params(),
        cost_estimate=cost(12),
    )
    outer_held = reduce_second(order, outer_spec, n, outer_held)
    inner_spec = [([(normed_low, inner_low)], hidden)]
    inner_held = reduce_first(order, inner_spec, n)
    grad_first, first_low, grad_attn, small = order.call(
        functools.partial(backward, n),
        *(inner_low, bias_sum, grad_second, first, vectors, sums),
        *(output_weight, inner_weight, *side, *tall),
        in_specs=[SMEM] + [VMEM] * 6 + [ANY] * 10,
        out_specs=[VMEM] * 4,
        out_shape=[
            shape(slots, width, dtype=WIDE),
            shape(slots, width),
            shape(n, slots, cols),
            shape(n, 16, cols, dtype=WIDE),
        ],
        scratch_shapes=[held_o, held_i, wide_one, pltpu.VMEM((8, width), WIDE), sem, sem],
        compiler_params=params(),
        cost_estimate=cost(13),
    )
    grad_mixed = exchange(grad_attn)
    outer_held = reduce_third(order, n, outer_held)
    inner_held = reduce_second(order, inner_spec, n, inner_held)
    order.wait(grad_mixed)
    outer_held = reduce_fourth(order, n, outer_held)

    backs, received = [], []
    for pair in range(pairs):
        if pair:
            received.append(exchange(backs[-1]))
            order.wait(outer_held)
            outer_pieces = gather_near(*reduce_fifth(order, [outer_held], [0]))
            inner_held = reduce_third(order, n, inner_held)
        backs.append(
            attention_back(order, qkv, bias_col, grad_mixed, lses[pair], pair, pairs, n, slots)
        )
    order.wait(*received, *inner_held, *outer_pieces)
    received.append(exchange(backs[-1]))
    outer_pieces = gather_far(*order.release(*outer_pieces))
    rest_spec = [([(row_low, back.reshape(n * slots, -1))], 3 * PAIR) for back in backs]
    rest_spec += [([(attn, first_low)], width)]
    rest_held = reduce_first(order, rest_spec, n)
    inner_held = reduce_fourth(order, n, inner_held, False)
    order.wait(*outer_pieces)
    outer_pieces = gather_cores(*order.release(*outer_pieces))
    rest_held = reduce_second(order, rest_spec, n, rest_held)
    order.tick(received[-1])
    inner_held = exchange(order.release(inner_held))
    (outer_grad,) = reduce_last(order, outer_pieces, [[(0, 0, 0, width)]], [width])
    rest_held = reduce_third(order, n, rest_held)
    grad_hidden, block_sum = order.call(
        functools.partial(finish_hidden, n, pairs),
        *(*received, grad_first, query_weight, key_weight, value_weight, *side),
        in_specs=[SMEM] + [VMEM] * (pairs + 1) + [ANY] * 7,
        out_specs=[VMEM] * 2,
        out_shape=[shape(slots, width, dtype=WIDE), shape(1, width, dtype=WIDE)],
        scratch_shapes=[
            pltpu.VMEM((n, cols, 3 * width), LOW),
            pltpu.VMEM((slots, 3 * width), LOW),
            pltpu.SemaphoreType.DMA((3 + 2 * GROUP,)),
        ],
        compiler_params=params(),
        cost_estimate=cost(9),
    )
    order.wait(*rest_held)
    rest_held = reduce_fourth(order, n, rest_held, False)
    order.tick(inner_held)

    packed = jnp.concatenate([small, block_sum.reshape(1, n, cols).repeat(n, 0)], 1)
    total = jnp.sum(exchange(order.release(packed)), 0)
    inner_pieces = gather_near(*reduce_fifth(order, [inner_held], [0]))
    order.tick(total)
    rest_held = exchange(order.release(rest_held))
    used = small.shape[1]
    bias_sums = jnp.stack([jnp.sum(back.astype(WIDE), (0, 1)) for back in backs])
    vector = jnp.concatenate([total[used:], jnp.full((1, cols), timestep[0], WIDE)])[None]
    total = jnp.concatenate([total[:used], bias_sums.reshape(-1, cols)])
    mask = 1
    while mask < lax.axis_size("dp"):
        flat = swap(jnp.concatenate([total, vector.reshape(-1, cols)]), mask)
        total = total + flat[: total.shape[0]]
        vector = jnp.concatenate([vector, flat[total.shape[0] :].reshape(vector.shape)])
        mask *= 2
    order.tick(rest_held, total, vector, *inner_pieces)
    inner_pieces = gather_far(*order.release(*inner_pieces))
    pieces = gather_near(*reduce_fifth(order, [rest_held], [3 * cols]))
    order.tick(*inner_pieces)
    inner_pieces = gather_cores(*order.release(*inner_pieces))
    per = deep // cols
    sums = [total[0], total[1 : 1 + per].reshape(deep)] + [total[1 + per + i] for i in range(5)]
    bias_sums = total[used:].reshape(pairs, 3 * PAIR)
    query_sum = bias_sums[:, :PAIR].reshape(cols)
    value_sum = bias_sums[:, 2 * PAIR :].reshape(cols)
    share = time_table.shape[0] // n
    levels = (jnp.arange(share, dtype=jnp.int32) + place * share).astype(WIDE)
    onehot = (vector[:, n, :1] == levels[None, :]).astype(WIDE)
    time_table_grad = lax.dot_general(
        onehot,
        vector[:, :n].reshape(-1, width),
        (((0,), (0,)), ((), ())),
        precision=lax.Precision.HIGHEST,
        preferred_element_type=WIDE,
    )

    order.wait(*pieces)
    pieces = gather_far(*order.release(*pieces))
    (inner_grad,) = reduce_last(order, inner_pieces, [[(0, 0, 0, hidden)]], [hidden])
    order.wait(*pieces)
    pieces = gather_cores(*order.release(*pieces))
    plan = [
        [
            (0, g * 3 * cols + p * 3 * PAIR + j * PAIR, g * cols + p * PAIR, PAIR)
            for g in range(n)
            for p in range(pairs)
        ]
        for j in range(3)
    ]
    plan += [[(0, n * 3 * cols, 0, width)]]
    *weight_grads, output_grad = reduce_last(order, pieces, plan, [width] * 4)
    return (
        out[None],
        grad_hidden[None],
        *weight_grads,
        output_grad,
        inner_grad,
        outer_grad,
        query_sum,
        value_sum,
        *sums,
        time_table_grad,
    )


def solution(mesh):
    row, shard, same = P("dp", "ctx", None), P("ctx", None), P()
    return jax.shard_map(
        per_device,
        mesh=mesh,
        in_specs=(row, row, P("dp"), P("dp"), P("dp")) + (shard,) * 6 + (same,) * 10,
        out_specs=(row, row) + (shard,) * 6 + (P("ctx"),) * 9 + (shard,),
        check_vma=False,
    )
```
